32 devices in a mesh: pipe: 4 (over y, core), ctx: 4 (over z), tp: 2 (over x).
Axes of the slice: x: 2, y: 2, z: 4, core: 2. Of those that a mesh axis runs over, the one named last changes fastest.
Arguments:
- queries: bfloat16 [4, 512, 4096], P('pipe', 'ctx', 'tp'), may hold values from -15 to 15
- keys: bfloat16 [4, 512, 1024], P('pipe', 'ctx', 'tp'), may hold values from -5 to 5
- values: bfloat16 [4, 512, 1024], P('pipe', 'ctx', 'tp'), may hold values from -5 to 5
- span_ids: int32 [4, 8], P('pipe', 'ctx'), may hold values from 0 to 7, each once within a row
- cotangent: bfloat16 [4, 512, 4096], P('pipe', 'ctx'), may hold values from -6 to 6
Outputs:
- attention: bfloat16 [4, 512, 4096], P('pipe', 'ctx', 'tp')
- grad_out: bfloat16 [4, 4096, 4096], P('pipe', 'ctx', 'tp')
The draws below stay inside these ranges and needn't reach their ends.
Inputs may be any that keep to these rules, and one draw needn't show every extreme that they name: `span_ids`: each row is a permutation of 0 to 7.
All inputs are finite; a program needn't handle non-finite values.
Results may differ from the reference program's by a relative error of at most 0.015.
Values may be sent and summed in bfloat16 or wider, within the bound.
No kernel may reach another device: no remote copies, remote signals or barrier semaphores. Data moves between devices by JAX's collectives and lax.ppermute only.
A program may use at most 64 MiB of HBM per device.

```python
import math
import jax
import jax.numpy as jnp
from jax import lax

HQ = 32
HK = 8
HD = 128
DW = 4096
TOK_DEV = 128
SPAN = 64
SPANS = 8
SEQ = 512
N_PIPE = 4
N_CTX = 4


def drawn_pair(key):
    query_shape = (N_PIPE, SEQ, HQ * HD)
    key_shape = (N_PIPE, SEQ, HK * HD)
    query_draw = jnp.clip(jax.random.normal(jax.random.fold_in(key, 11), query_shape, jnp.float32), -4.0, 4.0)
    key_draw = jnp.clip(jax.random.normal(jax.random.fold_in(key, 12), key_shape, jnp.float32), -3.0, 3.0)
    return (query_draw, key_draw)


def draw_queries(key, part):
    return drawn_pair(key)[0].astype(jnp.bfloat16)


def draw_keys(key, part):
    return drawn_pair(key)[1].astype(jnp.bfloat16)


def with_spikes(drawn, own_key, source, target, parts, factor):
    def block_of(axis_at):
        return (jnp.arange(drawn.shape[axis_at]) // (drawn.shape[axis_at] // parts)).reshape((-1,) + (1,) * (drawn.ndim - 1 - axis_at))

    one_side = jax.random.permutation(own_key, parts)[block_of(target)]
    far = (block_of(target) + parts // 2) % parts
    return jnp.where((block_of(source) == one_side) | (block_of(source) == far), factor * drawn, drawn)


def level_of(own_key, shape, cuts, smallest, top_value):
    gain, own = 1.0, jax.random.fold_in(own_key, 6)
    for dim, shards_of in cuts:
        steps = jnp.exp(jax.random.uniform(jax.random.fold_in(own, dim), (shards_of,), jnp.float32, smallest / len(cuts), top_value / len(cuts)))
        gain = gain * jnp.repeat(steps, shape[dim] // shards_of).reshape([-1 if axis == dim else 1 for axis in range(len(shape))])
    return gain


def gaussian(own_key, shape, width, bound, cuts=(), kind=jnp.bfloat16):
    level = level_of(own_key, shape, cuts, -0.22, 0.18) if cuts else 1.0
    values = jax.random.normal(own_key, shape, jnp.float32) * width * level
    return jnp.minimum(jnp.maximum(values, -bound), bound).astype(kind)


def heavy_noise(stream_key, extent, deviation, bound, split, heavy, kind=jnp.bfloat16):
    entries = deviation * jax.random.normal(stream_key, extent, jnp.float32)
    if split:
        entries = entries * level_of(stream_key, extent, split, -0.22, 0.18)
    return jnp.clip(with_spikes(entries, jax.random.fold_in(stream_key, 3), *heavy), -bound, bound).astype(kind)


def setup_inputs(seed: int = 0) -> dict:
    key_list = jax.random.split(jax.random.key(seed), 6)
    return {
        "queries": draw_queries(jax.random.fold_in(key_list[5], 71), 0),
        "keys": draw_keys(jax.random.fold_in(key_list[5], 71), 0),
        "values": gaussian(key_list[2], (N_PIPE, SEQ, HK * HD), 1.0, 5.0, ((0, 4), (1, 4), (2, 2))),
        "span_ids": jax.vmap(lambda own: jax.random.permutation(own, SPANS))(jax.random.split(key_list[3], N_PIPE)).reshape((N_PIPE, SPANS)).astype(jnp.int32),
        "cotangent": heavy_noise(key_list[4], (N_PIPE, SEQ, DW), 1.0, 6.0, ((0, 4), (1, 4)), (1, 2, 4, 2.0)),
    }


def reference(queries, keys, values, span_ids, cotangent):
    rows = jnp.arange(SEQ, dtype=jnp.int32)
    group = HQ // HK
    scale = 1.0 / math.sqrt(HD)

    def one_batch(inputs):
        query_all, key_all, value_all, span_row, cot_all = inputs
        positions = span_row[rows // SPAN].astype(jnp.int32) * SPAN + rows % SPAN
        visible = positions[None, :] <= positions[:, None]
        query_heads = query_all.reshape(SEQ, HQ, HD).transpose(1, 0, 2)
        key_heads = key_all.reshape(SEQ, HK, HD).transpose(1, 0, 2)
        value_heads = value_all.reshape(SEQ, HK, HD).transpose(1, 0, 2)

        def one_head(head):
            query_one = query_heads[head]
            key_one = key_heads[head // group]
            value_one = value_heads[head // group]
            scores = jnp.dot(query_one, key_one.T, preferred_element_type=jnp.float32) * scale
            masked = jnp.where(visible, scores, -1e+30)
            top = lax.optimization_barrier(jnp.max(masked, axis=-1, keepdims=True))
            weights = jnp.where(visible, jnp.exp(scores - top), 0.0)
            total = lax.optimization_barrier(jnp.sum(weights, axis=-1))
            mixed = jnp.dot(weights.astype(jnp.bfloat16), value_one, preferred_element_type=jnp.float32)
            return mixed / total[:, None]
        outputs = lax.map(one_head, jnp.arange(HQ))
        attention = outputs.transpose(1, 0, 2).reshape(SEQ, HQ * HD).astype(jnp.bfloat16)
        blocks = attention.reshape(N_CTX, TOK_DEV, HQ * HD)
        cot_blocks = cot_all.reshape(N_CTX, TOK_DEV, DW)

        def add_block(summed, pair):
            att_block, cot_block = pair
            term = jnp.dot(cot_block.T, att_block, preferred_element_type=jnp.float32)
            term = lax.optimization_barrier(term.astype(jnp.bfloat16)).astype(jnp.float32)
            return (summed + term, None)
        summed = lax.scan(add_block, jnp.zeros((DW, HQ * HD), jnp.float32), (blocks, cot_blocks))[0]
        return (attention, summed)
    attention, summed = lax.map(one_batch, (queries, keys, values, span_ids, cotangent))
    grad_out = (summed + jnp.roll(summed, N_PIPE // 2, axis=0)).astype(jnp.bfloat16)
    return (attention, grad_out)
```

```python
import functools
import math

import jax
import jax.numpy as jnp
from jax import lax
from jax.experimental import pallas as pl
from jax.experimental.pallas import tpu as pltpu
from jax.sharding import PartitionSpec as P

HQ = 32
HK = 8
HD = 128
TAG = 16
VMEM = pl.BlockSpec(memory_space=pltpu.VMEM)
SMEM = pl.BlockSpec(memory_space=pltpu.SMEM)


def swap(x, axis, mask):
    return lax.ppermute(x, axis, [(i, i ^ mask) for i in range(lax.axis_size(axis))])


def params(mib):
    return pltpu.CompilerParams(vmem_limit_bytes=mib * 2**20)


def pack_kernel(n, span_ref, key_ref, value_ref, cot_ref, packed_ref, *cot_refs):
    tokens, width = key_ref.shape[1:]
    spans = span_ref.shape[1]
    packed_ref[:tokens, :width] = key_ref[0]
    packed_ref[:tokens, width:] = value_ref[0]
    lane = lax.broadcasted_iota(jnp.int32, (TAG, 2 * width), 1)
    ids = jnp.zeros((TAG, 2 * width), jnp.float32)
    for j in range(spans):
        ids = jnp.where(lane // (tokens // spans) == j, span_ref[0, j].astype(jnp.float32), ids)
    packed_ref[tokens:, :] = ids.astype(jnp.bfloat16)
    me = lax.axis_index("ctx")
    side = lax.axis_index("tp") & 1
    half = cot_ref.shape[2] // n // 2
    for s in range(n):
        at = pl.multiple_of((jnp.bitwise_xor(me, s) * 2 + side) * half, 128)
        cot_refs[s][...] = cot_ref[0, :, pl.ds(at, half)]


def attention_kernel(group, scale, span_ref, query_ref, *refs):
    kv_refs, out_ref = refs[:-1], refs[-1]
    tokens = query_ref.shape[1]
    width = kv_refs[0].shape[1] // 2
    spans = span_ref.shape[1]
    span = tokens // spans
    lane = lax.broadcasted_iota(jnp.int32, (1, tokens), 1)
    inner = (lane % span).astype(jnp.float32)
    key_pos = jnp.concatenate(
        [ref[tokens : tokens + 1, :tokens].astype(jnp.float32) * span + inner for ref in kv_refs],
        axis=1,
    )
    row = lax.broadcasted_iota(jnp.int32, (tokens, 1), 0)
    base = jnp.zeros((tokens, 1), jnp.int32)
    for j in range(spans):
        base = jnp.where(row // span == j, span_ref[0, j] * span, base)
    query_pos = (base + row % span).astype(jnp.float32)
    hidden = jnp.where(key_pos <= query_pos, 0.0, -1e30)
    hidden = jnp.concatenate([hidden] * group, axis=0)
    for j in range(width // HD):
        columns = slice(j * HD, (j + 1) * HD)
        key_block = jnp.concatenate([ref[:tokens, columns] for ref in kv_refs], axis=0)
        value_block = jnp.concatenate(
            [ref[:tokens, width + j * HD : width + (j + 1) * HD] for ref in kv_refs], axis=0
        )
        queries = jnp.concatenate(
            [query_ref[0, :, (j * group + g) * HD : (j * group + g + 1) * HD] for g in range(group)],
            axis=0,
        )
        scores = lax.dot_general(
            queries, key_block, (((1,), (1,)), ((), ())), preferred_element_type=jnp.float32
        )
        scores = jnp.where(hidden < 0.0, hidden, scores)
        top = jnp.max(scores, axis=1, keepdims=True)
        weights = jnp.exp2((scores - top) * (scale * math.log2(math.e)))
        total = jnp.sum(weights, axis=1, keepdims=True)
        mixed = jnp.dot(
            weights.astype(jnp.bfloat16), value_block, preferred_element_type=jnp.float32
        )
        mixed = (mixed / total).astype(jnp.bfloat16)
        for g in range(group):
            out_ref[0, :, (j * group + g) * HD : (j * group + g + 1) * HD] = mixed[
                g * tokens : (g + 1) * tokens
            ]


def turn_kernel(*refs):
    tokens = refs[0].shape[0]
    for s, ref in enumerate(refs[:-1]):
        refs[-1][:, s * tokens : (s + 1) * tokens] = ref[...].T


def grad_kernel(n, *refs):
    att_refs, (own_ref, own_far_ref, near_ref, far_ref), out_ref = refs[: 2 * n], refs[2 * n : -1], refs[-1]
    rows = jnp.concatenate([ref[0] for ref in att_refs], axis=0)
    depth = rows.shape[0] // 2
    half = own_ref.shape[0]
    side = lax.axis_index("tp") & 1
    for at, (left, right) in (
        (side, (own_ref, own_far_ref)),
        (1 - side, (near_ref, far_ref)),
    ):
        both = jnp.concatenate([left[...], right[...]], axis=1)
        out_ref[0, pl.ds(pl.multiple_of(at * half, half), half), :] = jnp.dot(
            both, rows, preferred_element_type=jnp.float32
        ).astype(jnp.bfloat16)


def local(queries, keys, values, span_ids, cotangent):
    n = lax.axis_size("ctx")
    far = lax.axis_size("pipe") // 2
    tokens, width = keys.shape[1:]
    heads = queries.shape[2]
    features = cotangent.shape[2] // n
    half = features // 2
    packed, *cots = pl.pallas_call(
        functools.partial(pack_kernel, n),
        out_shape=[jax.ShapeDtypeStruct((tokens + TAG, 2 * width), jnp.bfloat16)]
        + [jax.ShapeDtypeStruct((tokens, half), jnp.bfloat16)] * n,
        in_specs=[SMEM, VMEM, VMEM, VMEM],
        out_specs=[VMEM] * (n + 1),
        compiler_params=params(16),
        name="pack",
    )(span_ids, keys, values, cotangent)
    kv = [packed] + [swap(packed, "ctx", s) for s in range(1, n)]
    cots = cots[:1] + [swap(cots[s], "ctx", s) for s in range(1, n)]
    attention = pl.pallas_call(
        functools.partial(attention_kernel, HQ // HK, 1.0 / math.sqrt(HD)),
        out_shape=jax.ShapeDtypeStruct(queries.shape, jnp.bfloat16),
        in_specs=[SMEM] + [VMEM] * (n + 1),
        out_specs=VMEM,
        compiler_params=params(40),
        name="attend",
    )(span_ids, queries, *kv)
    near = [attention] + [swap(attention, "ctx", s) for s in range(1, n)]
    turned = pl.pallas_call(
        turn_kernel,
        out_shape=jax.ShapeDtypeStruct((half, n * tokens), jnp.bfloat16),
        in_specs=[VMEM] * n,
        out_specs=VMEM,
        compiler_params=params(16),
        name="turn",
    )(*cots)
    turned_far = swap(turned, "pipe", far)
    other = swap(turned, "tp", 1)
    other_far = swap(turned_far, "tp", 1)
    mirrored = [swap(piece, "pipe", far) for piece in near]
    tile = min(256, heads)
    piece_spec = pl.BlockSpec((1, tokens, tile), lambda j: (0, 0, j))
    grad_out = pl.pallas_call(
        functools.partial(grad_kernel, n),
        grid=(heads // tile,),
        out_shape=jax.ShapeDtypeStruct((1, features, heads), jnp.bfloat16),
        in_specs=[piece_spec] * (2 * n)
        + [pl.BlockSpec((half, n * tokens), lambda j: (0, 0))] * 4,
        out_specs=pl.BlockSpec((1, features, tile), lambda j: (0, 0, j)),
        compiler_params=params(40),
        cost_estimate=pl.CostEstimate(
            flops=4 * features * heads * n * tokens, bytes_accessed=12 * 2**20, transcendentals=0
        ),
        name="gradient",
    )(*near, *mirrored, turned, turned_far, other, other_far)
    return (attention, grad_out)


def solution(mesh):
    placed = (
        P("pipe", "ctx", "tp"),
        P("pipe", "ctx", "tp"),
        P("pipe", "ctx", "tp"),
        P("pipe", "ctx"),
        P("pipe", "ctx", None),
    )
    return jax.shard_map(
        local,
        mesh=mesh,
        in_specs=placed,
        out_specs=(P("pipe", "ctx", "tp"), P("pipe", "ctx", "tp")),
        check_vma=False,
    )
```

```python
import functools
import math

import jax
import jax.numpy as jnp
from jax import lax
from jax.experimental import pallas as pl
from jax.experimental.pallas import tpu as pltpu
from jax.sharding import PartitionSpec as P

HQ = 32
HK = 8
HD = 128
TAG = 16
TILE = 256
VMEM = pl.BlockSpec(memory_space=pltpu.VMEM)
SMEM = pl.BlockSpec(memory_space=pltpu.SMEM)
ANY = pl.BlockSpec(memory_space=pl.ANY)


def ring_order(n):
    return list(range(0, n, 2)) + list(range(1, n, 2))[::-1]


def around(x, shift):
    n = lax.axis_size("ctx")
    order = ring_order(n)
    return lax.ppermute(x, "ctx", [(order[q], order[(q + shift) % n]) for q in range(n)])


def swap(x, axis, mask):
    return lax.ppermute(x, axis, [(i, i ^ mask) for i in range(lax.axis_size(axis))])


def params(mib):
    return pltpu.CompilerParams(vmem_limit_bytes=mib * 2**20)


def pack_kernel(span_ref, key_ref, value_ref, packed_ref):
    tokens, width = key_ref.shape[1:]
    spans = span_ref.shape[1]
    packed_ref[:tokens, :width] = key_ref[0]
    packed_ref[:tokens, width:] = value_ref[0]
    lane = lax.broadcasted_iota(jnp.int32, (TAG, 2 * width), 1)
    ids = jnp.zeros((TAG, 2 * width), jnp.float32)
    for j in range(spans):
        ids = jnp.where(lane // (tokens // spans) == j, span_ref[0, j].astype(jnp.float32), ids)
    packed_ref[tokens:, :] = ids.astype(jnp.bfloat16)


def turn_kernel(n, cot_ref, out_ref):
    me = lax.axis_index("ctx")
    side = lax.axis_index("tp") & 1
    half = cot_ref.shape[2] // n // 2
    place = jnp.where(me % 2 == 0, me // 2, n - 1 - me // 2)
    for s in range(n):
        to = (place + s) % n
        block = jnp.where(to < (n + 1) // 2, 2 * to, 2 * (n - to) - 1)
        at = pl.multiple_of((block * 2 + side) * half, 128)
        out_ref[s * half : (s + 1) * half, :] = cot_ref[0, :, pl.ds(at, half)].T


def join_kernel(near_ref, far_ref, *out_refs):
    half, tokens = out_refs[0].shape[0], near_ref.shape[1]
    for s, ref in enumerate(out_refs):
        ref[:, :tokens] = near_ref[s * half : (s + 1) * half]
        ref[:, tokens:] = far_ref[s * half : (s + 1) * half]


def attention_kernel(group, scale, span_ref, query_ref, *refs):
    kv_refs, out_ref = refs[:-1], refs[-1]
    tokens = query_ref.shape[1]
    width = kv_refs[0].shape[1] // 2
    spans = span_ref.shape[1]
    span = tokens // spans
    lane = lax.broadcasted_iota(jnp.int32, (1, tokens), 1)
    inner = (lane % span).astype(jnp.float32)
    key_pos = jnp.concatenate(
        [ref[tokens : tokens + 1, :tokens].astype(jnp.float32) * span + inner for ref in kv_refs],
        axis=1,
    )
    row = lax.broadcasted_iota(jnp.int32, (tokens, 1), 0)
    base = jnp.zeros((tokens, 1), jnp.int32)
    for j in range(spans):
        base = jnp.where(row // span == j, span_ref[0, j] * span, base)
    query_pos = (base + row % span).astype(jnp.float32)
    hidden = jnp.where(key_pos <= query_pos, 0.0, -1e30)
    hidden = jnp.concatenate([hidden] * group, axis=0)
    for j in range(width // HD):
        columns = slice(j * HD, (j + 1) * HD)
        key_block = jnp.concatenate([ref[:tokens, columns] for ref in kv_refs], axis=0)
        value_block = jnp.concatenate(
            [ref[:tokens, width + j * HD : width + (j + 1) * HD] for ref in kv_refs], axis=0
        )
        queries = jnp.concatenate(
            [query_ref[0, :, (j * group + g) * HD : (j * group + g + 1) * HD] for g in range(group)],
            axis=0,
        )
        scores = lax.dot_general(
            queries, key_block, (((1,), (1,)), ((), ())), preferred_element_type=jnp.float32
        )
        scores = jnp.where(hidden < 0.0, hidden, scores)
        top = jnp.max(scores, axis=1, keepdims=True)
        weights = jnp.exp2((scores - top) * (scale * math.log2(math.e)))
        total = jnp.sum(weights, axis=1, keepdims=True)
        mixed = jnp.dot(
            weights.astype(jnp.bfloat16), value_block, preferred_element_type=jnp.float32
        )
        mixed = (mixed / total).astype(jnp.bfloat16)
        for g in range(group):
            out_ref[0, :, (j * group + g) * HD : (j * group + g + 1) * HD] = mixed[
                g * tokens : (g + 1) * tokens
            ]


def early_kernel(slots, *refs):
    near, far, mine, other = (refs[i * slots : (i + 1) * slots] for i in range(4))
    total_ref = refs[-1]
    half = mine[0].shape[0]
    side = lax.axis_index("tp") & 1
    wide = TILE if total_ref.shape[1] % TILE == 0 else total_ref.shape[1]

    def column(j, _):
        columns = pl.ds(pl.multiple_of(j * wide, wide), wide)
        rows = jnp.concatenate(
            [ref[0, :, columns] for pair in zip(near, far) for ref in pair], axis=0
        )
        for at, pieces in ((side, mine), (1 - side, other)):
            left = jnp.concatenate([ref[...] for ref in pieces], axis=1)
            total_ref[pl.ds(pl.multiple_of(at * half, half), half), columns] = jnp.dot(
                left, rows, preferred_element_type=jnp.float32
            )
        return 0

    lax.fori_loop(0, total_ref.shape[1] // wide, column, 0)


def late_kernel(total_ref, near_ref, far_ref, mine_ref, other_ref, out_ref, held, sems):
    half = mine_ref.shape[0]
    side = lax.axis_index("tp") & 1
    wide = held.shape[2]
    count = total_ref.shape[1] // wide
    copies = []
    for j in range(count):
        columns = slice(j * wide, (j + 1) * wide)
        rows = jnp.concatenate([near_ref[0, :, columns], far_ref[0, :, columns]], axis=0)
        if j >= 2:
            copies[j - 2].wait()
        for at, ref in ((side, mine_ref), (1 - side, other_ref)):
            here = pl.ds(pl.multiple_of(at * half, half), half)
            held[j % 2, here, :] = (
                total_ref[here, columns]
                + jnp.dot(ref[...], rows, preferred_element_type=jnp.float32)
            ).astype(jnp.bfloat16)
        copies.append(
            pltpu.make_async_copy(held.at[j % 2], out_ref.at[0, :, columns], sems.at[j % 2])
        )
        copies[-1].start()
    for copy in copies[-2:]:
        copy.wait()


def local(queries, keys, values, span_ids, cotangent):
    n = lax.axis_size("ctx")
    far = lax.axis_size("pipe") // 2
    tokens, width = keys.shape[1:]
    heads = queries.shape[2]
    features = cotangent.shape[2] // n
    half = features // 2
    wide = TILE if heads % TILE == 0 else heads
    packed = pl.pallas_call(
        pack_kernel,
        out_shape=jax.ShapeDtypeStruct((tokens + TAG, 2 * width), jnp.bfloat16),
        in_specs=[SMEM, VMEM, VMEM],
        out_specs=VMEM,
        compiler_params=params(16),
        name="pack",
    )(span_ids, keys, values)
    turned = pl.pallas_call(
        functools.partial(turn_kernel, n),
        out_shape=jax.ShapeDtypeStruct((n * half, tokens), jnp.bfloat16),
        in_specs=[VMEM],
        out_specs=VMEM,
        compiler_params=params(16),
        name="turn",
    )(cotangent)
    kv = [packed, around(packed, 1)]
    kv[1], turned = lax.optimization_barrier((kv[1], turned))
    for _ in range(n - 2):
        kv.append(around(kv[-1], 1))
    joined = pl.pallas_call(
        join_kernel,
        out_shape=[jax.ShapeDtypeStruct((half, 2 * tokens), jnp.bfloat16)] * n,
        in_specs=[VMEM] * 2,
        out_specs=[VMEM] * n,
        compiler_params=params(16),
        name="join",
    )(turned, swap(turned, "pipe", far))
    attention = pl.pallas_call(
        functools.partial(attention_kernel, HQ // HK, 1.0 / math.sqrt(HD)),
        out_shape=jax.ShapeDtypeStruct(queries.shape, jnp.bfloat16),
        in_specs=[SMEM] + [VMEM] * (n + 1),
        out_specs=VMEM,
        compiler_params=params(40),
        name="attend",
    )(span_ids, queries, *kv)
    near = [attention]
    for _ in range(n - 1):
        near.append(around(near[-1], 1))
    mirrored = [swap(piece, "pipe", far) for piece in near]
    mine = [joined[0]] + [around(joined[s], s) for s in range(1, n)]
    other = [swap(piece, "tp", 1) for piece in mine]
    total = pl.pallas_call(
        functools.partial(early_kernel, n - 1),
        out_shape=jax.ShapeDtypeStruct((features, heads), jnp.float32),
        in_specs=[VMEM] * (4 * (n - 1)),
        out_specs=VMEM,
        compiler_params=params(40),
        cost_estimate=pl.CostEstimate(
            flops=4 * features * heads * (n - 1) * tokens,
            bytes_accessed=12 * 2**20,
            transcendentals=0,
        ),
        name="early",
    )(*near[:-1], *mirrored[:-1], *mine[:-1], *other[:-1])
    grad_out = pl.pallas_call(
        late_kernel,
        out_shape=jax.ShapeDtypeStruct((1, features, heads), jnp.bfloat16),
        in_specs=[VMEM] * 5,
        out_specs=ANY,
        scratch_shapes=[
            pltpu.VMEM((2, features, wide), jnp.bfloat16),
            pltpu.SemaphoreType.DMA((2,)),
        ],
        compiler_params=params(40),
        name="late",
    )(total, near[-1], mirrored[-1], mine[-1], other[-1])
    return (attention, grad_out)


def solution(mesh):
    placed = (
        P("pipe", "ctx", "tp"),
        P("pipe", "ctx", "tp"),
        P("pipe", "ctx", "tp"),
        P("pipe", "ctx"),
        P("pipe", "ctx", None),
    )
    return jax.shard_map(
        local,
        mesh=mesh,
        in_specs=placed,
        out_specs=(P("pipe", "ctx", "tp"), P("pipe", "ctx", "tp")),
        check_vma=False,
    )
```

```python
import functools
import math

import jax
import jax.numpy as jnp
from jax import lax
from jax.experimental import pallas as pl
from jax.experimental.pallas import tpu as pltpu
from jax.sharding import PartitionSpec as P

HQ = 32
HK = 8
HD = 128
TAG = 16
TILE = 256
VMEM = pl.BlockSpec(memory_space=pltpu.VMEM)
SMEM = pl.BlockSpec(memory_space=pltpu.SMEM)
ANY = pl.BlockSpec(memory_space=pl.ANY)


def ring_order(n):
    return list(range(0, n, 2)) + list(range(1, n, 2))[::-1]


def around(x, shift):
    n = lax.axis_size("ctx")
    order = ring_order(n)
    return lax.ppermute(x, "ctx", [(order[q], order[(q + shift) % n]) for q in range(n)])


def swap(x, axis, mask):
    return lax.ppermute(x, axis, [(i, i ^ mask) for i in range(lax.axis_size(axis))])


def params(mib):
    return pltpu.CompilerParams(vmem_limit_bytes=mib * 2**20)


def after(x, *others):
    return lax.optimization_barrier((x, *others))[0]


def pack_kernel(span_ref, key_ref, value_ref, packed_ref, place_ref):
    tokens, width = key_ref.shape[1:]
    packed_ref[:tokens, :width] = key_ref[0]
    packed_ref[:tokens, width:] = value_ref[0]
    spans = span_ref.shape[1]
    span = tokens // spans
    lane = lax.broadcasted_iota(jnp.int32, (TAG, 2 * width), 1)
    row = lax.broadcasted_iota(jnp.int32, place_ref.shape, 0)
    ids = jnp.zeros(lane.shape, jnp.float32)
    base = jnp.zeros(row.shape, jnp.int32)
    for j in range(spans):
        ids = jnp.where(lane // span == j, span_ref[0, j].astype(jnp.float32), ids)
        base = jnp.where(row // span == j, span_ref[0, j] * span, base)
    packed_ref[tokens:, :] = ids.astype(jnp.bfloat16)
    place_ref[...] = (base + row % span).astype(jnp.float32)


def fetch_kernel(place_ref, query_ref, out_ref):
    out_ref[...] = query_ref[...]


def turn_kernel(n, ready_ref, cot_ref, *out_refs):
    me = lax.axis_index("ctx")
    side = lax.axis_index("tp") & 1
    half = cot_ref.shape[2] // n // 2
    place = jnp.where(me % 2 == 0, me // 2, n - 1 - me // 2)
    for s in range(n):
        to = (place + s) % n
        block = jnp.where(to < (n + 1) // 2, 2 * to, 2 * (n - to) - 1)
        at = pl.multiple_of((block * 2 + side) * half, 128)
        out_refs[s][...] = cot_ref[0, :, pl.ds(at, half)].T


def join_kernel(*refs):
    tokens = refs[0].shape[1]
    for s, ref in enumerate(refs[:-1]):
        refs[-1][:, s * tokens : (s + 1) * tokens] = ref[...]


def attention_kernel(group, scale, n, spans, place_ref, query_ref, *refs):
    kv_refs, (whole_ref, *part_refs) = refs[:n], refs[n:]
    tokens = query_ref.shape[1]
    width = kv_refs[0].shape[1] // 2
    heads = width // HD
    span = tokens // spans
    lane = lax.broadcasted_iota(jnp.int32, (1, tokens), 1)
    inner = (lane % span).astype(jnp.float32)
    key_pos = jnp.concatenate(
        [ref[tokens : tokens + 1, :tokens].astype(jnp.float32) * span + inner for ref in kv_refs],
        axis=1,
    )
    hidden = jnp.where(key_pos <= place_ref[:, :1], 0.0, -1e30)
    hidden = jnp.concatenate([hidden] * group, axis=0)
    for j in range(heads):
        first = j * group * HD
        out_ref = part_refs[j * len(part_refs) // heads]
        key_block = jnp.concatenate([ref[:tokens, j * HD : (j + 1) * HD] for ref in kv_refs], axis=0)
        value_block = jnp.concatenate(
            [ref[:tokens, width + j * HD : width + (j + 1) * HD] for ref in kv_refs], axis=0
        )
        queries = jnp.concatenate(
            [query_ref[0, :, first + g * HD : first + (g + 1) * HD] for g in range(group)], axis=0
        )
        scores = lax.dot_general(
            queries, key_block, (((1,), (1,)), ((), ())), preferred_element_type=jnp.float32
        )
        scores = jnp.where(hidden < 0.0, hidden, scores)
        top = jnp.max(scores, axis=1, keepdims=True)
        weights = jnp.exp2((scores - top) * (scale * math.log2(math.e)))
        total = jnp.sum(weights, axis=1, keepdims=True)
        mixed = jnp.dot(
            weights.astype(jnp.bfloat16), value_block, preferred_element_type=jnp.float32
        )
        mixed = (mixed / total).astype(jnp.bfloat16)
        for g in range(group):
            at, piece = first + g * HD, mixed[g * tokens : (g + 1) * tokens]
            whole_ref[0, :, at : at + HD] = piece
            at %= out_ref.shape[2]
            out_ref[0, :, at : at + HD] = piece


def left_sides(refs, tokens, first, slots):
    near, far, near_other, far_other = refs
    here = slice(first * tokens, (first + slots) * tokens)
    side = lax.axis_index("tp") & 1
    return (
        (side, jnp.concatenate([near[:, here], far[:, here]], axis=1)),
        (1 - side, jnp.concatenate([near_other[:, here], far_other[:, here]], axis=1)),
    )


def early_kernel(slots, *refs):
    att_refs, cot_refs, total_ref = refs[: 2 * slots], refs[2 * slots : -1], refs[-1]
    half = cot_refs[0].shape[0]
    tokens = att_refs[0].shape[1]
    wide = TILE if total_ref.shape[1] % TILE == 0 else total_ref.shape[1]
    for j in range(total_ref.shape[1] // wide):
        columns = slice(j * wide, (j + 1) * wide)
        rows = jnp.concatenate([ref[0, :, columns] for ref in att_refs], axis=0)
        for at, left in left_sides(cot_refs, tokens, 0, slots):
            total_ref[pl.ds(pl.multiple_of(at * half, half), half), columns] = jnp.dot(
                left, rows, preferred_element_type=jnp.float32
            )


def finish_kernel(slots, first, start, carried, width, *refs):
    att_refs, cot_refs = refs[: 2 * slots], refs[2 * slots : 2 * slots + 4]
    out_ref, held, sems = refs[-3:]
    total_ref = refs[2 * slots + 4] if carried else None
    half = cot_refs[0].shape[0]
    tokens = att_refs[0].shape[1]
    wide = held.shape[2]
    copies = []
    for j in range(width // wide):
        columns = slice(j * wide, (j + 1) * wide)
        rows = jnp.concatenate([ref[0, :, columns] for ref in att_refs], axis=0)
        if j >= 2:
            copies[j - 2].wait()
        for at, left in left_sides(cot_refs, tokens, first, slots):
            here = pl.ds(pl.multiple_of(at * half, half), half)
            value = jnp.dot(left, rows, preferred_element_type=jnp.float32)
            if carried:
                value = value + total_ref[here, columns]
            held[j % 2, here, :] = value.astype(jnp.bfloat16)
        copies.append(
            pltpu.make_async_copy(
                held.at[j % 2],
                out_ref.at[0, :, start + j * wide : start + (j + 1) * wide],
                sems.at[j % 2],
            )
        )
        copies[-1].start()
    for copy in copies[-2:]:
        copy.wait()


def local(queries, keys, values, span_ids, cotangent):
    n = lax.axis_size("ctx")
    far = lax.axis_size("pipe") // 2
    tokens, width = keys.shape[1:]
    spans = span_ids.shape[1]
    heads = queries.shape[2]
    parts = 2 if width % (2 * HD) == 0 else 1
    chunk = heads // parts
    features = cotangent.shape[2] // n
    half = features // 2

    packed, place = pl.pallas_call(
        pack_kernel,
        out_shape=[
            jax.ShapeDtypeStruct((tokens + TAG, 2 * width), jnp.bfloat16),
            jax.ShapeDtypeStruct((tokens, 128), jnp.float32),
        ],
        in_specs=[SMEM, VMEM, VMEM],
        out_specs=[VMEM] * 2,
        compiler_params=params(16),
        name="pack",
    )(span_ids, keys, values)
    kv = [packed] + [around(packed, s) for s in range(1, n)]
    query_held = pl.pallas_call(
        fetch_kernel,
        out_shape=jax.ShapeDtypeStruct(queries.shape, jnp.bfloat16),
        in_specs=[ANY, VMEM],
        out_specs=VMEM,
        compiler_params=params(16),
        name="fetch",
    )(place, queries)
    turned = pl.pallas_call(
        functools.partial(turn_kernel, n),
        out_shape=[jax.ShapeDtypeStruct((half, tokens), jnp.bfloat16)] * n,
        in_specs=[ANY, VMEM],
        out_specs=[VMEM] * n,
        compiler_params=params(16),
        name="turn",
    )(place, cotangent)
    query_held = after(query_held, *turned)
    attention, *pieces = pl.pallas_call(
        functools.partial(attention_kernel, HQ // HK, 1.0 / math.sqrt(HD), n, spans),
        out_shape=[jax.ShapeDtypeStruct(queries.shape, jnp.bfloat16)]
        + [jax.ShapeDtypeStruct((1, tokens, chunk), jnp.bfloat16)] * parts,
        in_specs=[VMEM] * (2 + n),
        out_specs=[VMEM] * (1 + parts),
        compiler_params=params(40),
        name="attend",
    )(place, query_held, *kv)

    near, mirrored = [], []
    for c in range(parts):
        held, sent = [pieces[c]], []
        for s in range(n):
            sent.append(swap(held[s], "pipe", far))
            if s < n - 1:
                arrived = around(held[s], 1)
                held.append(after(arrived, sent[s]) if s < n - 2 else arrived)
        near.append(held)
        mirrored.append(sent)

    turned = [turned[0]] + [around(turned[s], s) for s in range(1, n)]
    mine = pl.pallas_call(
        join_kernel,
        out_shape=jax.ShapeDtypeStruct((half, n * tokens), jnp.bfloat16),
        in_specs=[VMEM] * n,
        out_specs=VMEM,
        compiler_params=params(16),
        name="join",
    )(*turned)
    mine_far = swap(mine, "pipe", far)
    cots = [mine, mine_far, swap(mine, "tp", 1), swap(mine_far, "tp", 1)]

    def attended(c, first, last):
        return near[c][first:last] + mirrored[c][first:last]

    tile = TILE if chunk % TILE == 0 else chunk
    total = pl.pallas_call(
        functools.partial(early_kernel, n - 1),
        out_shape=jax.ShapeDtypeStruct((features, chunk), jnp.float32),
        in_specs=[VMEM] * (2 * n + 2),
        out_specs=VMEM,
        compiler_params=params(40),
        cost_estimate=pl.CostEstimate(
            flops=4 * features * chunk * (n - 1) * tokens,
            bytes_accessed=8 * 2**20,
            transcendentals=0,
        ),
        name="early",
    )(*attended(parts - 1, 0, n - 1), *cots)
    grad_out = None
    for c in range(parts):
        last = c == parts - 1
        slots = 1 if last else n
        operands = attended(c, n - slots, n) + cots + ([total] if last else [])
        specs = [VMEM] * len(operands)
        aliases = {}
        if grad_out is not None:
            aliases = {len(operands): 0}
            operands.append(grad_out)
            specs.append(ANY)
        grad_out = pl.pallas_call(
            functools.partial(finish_kernel, slots, n - slots, c * chunk, last, chunk),
            out_shape=jax.ShapeDtypeStruct((1, features, heads), jnp.bfloat16),
            in_specs=specs,
            out_specs=ANY,
            scratch_shapes=[
                pltpu.VMEM((2, features, tile), jnp.bfloat16),
                pltpu.SemaphoreType.DMA((2,)),
            ],
            input_output_aliases=aliases,
            compiler_params=params(40),
            cost_estimate=pl.CostEstimate(
                flops=4 * features * chunk * slots * tokens,
                bytes_accessed=8 * 2**20,
                transcendentals=0,
            ),
            name="finish",
        )(*operands)
    return (attention, grad_out)


def solution(mesh):
    placed = (
        P("pipe", "ctx", "tp"),
        P("pipe", "ctx", "tp"),
        P("pipe", "ctx", "tp"),
        P("pipe", "ctx"),
        P("pipe", "ctx", None),
    )
    return jax.shard_map(
        local,
        mesh=mesh,
        in_specs=placed,
        out_specs=(P("pipe", "ctx", "tp"), P("pipe", "ctx", "tp")),
        check_vma=False,
    )
```

```python
import functools
import math

import jax
import jax.numpy as jnp
from jax import lax
from jax.experimental import pallas as pl
from jax.experimental.pallas import tpu as pltpu
from jax.sharding import PartitionSpec as P

HQ = 32
HK = 8
HD = 128
TAG = 16
TILE = 256
VMEM = pl.BlockSpec(memory_space=pltpu.VMEM)
SMEM = pl.BlockSpec(memory_space=pltpu.SMEM)
ANY = pl.BlockSpec(memory_space=pl.ANY)


def ring_order(n):
    return list(range(0, n, 2)) + list(range(1, n, 2))[::-1]


def around(x, shift):
    n = lax.axis_size("ctx")
    order = ring_order(n)
    return lax.ppermute(x, "ctx", [(order[q], order[(q + shift) % n]) for q in range(n)])


def swap(x, axis, mask):
    return lax.ppermute(x, axis, [(i, i ^ mask) for i in range(lax.axis_size(axis))])


def params(mib):
    return pltpu.CompilerParams(vmem_limit_bytes=mib * 2**20)


def after(x, *others):
    return lax.optimization_barrier((x, *others))[0]


def pack_kernel(span_ref, key_ref, value_ref, packed_ref, place_ref):
    tokens, width = key_ref.shape[1:]
    packed_ref[:tokens, :width] = key_ref[0]
    packed_ref[:tokens, width:] = value_ref[0]
    spans = span_ref.shape[1]
    span = tokens // spans
    lane = lax.broadcasted_iota(jnp.int32, (TAG, 2 * width), 1)
    row = lax.broadcasted_iota(jnp.int32, place_ref.shape, 0)
    ids = jnp.zeros(lane.shape, jnp.float32)
    base = jnp.zeros(row.shape, jnp.int32)
    for j in range(spans):
        ids = jnp.where(lane // span == j, span_ref[0, j].astype(jnp.float32), ids)
        base = jnp.where(row // span == j, span_ref[0, j] * span, base)
    packed_ref[tokens:, :] = ids.astype(jnp.bfloat16)
    place_ref[...] = (base + row % span).astype(jnp.float32)


def fetch_kernel(place_ref, query_ref, out_ref):
    out_ref[...] = query_ref[...]


def turn_kernel(n, ready_ref, cot_ref, *out_refs):
    me = lax.axis_index("ctx")
    side = lax.axis_index("tp") & 1
    half = cot_ref.shape[2] // n // 2
    place = jnp.where(me % 2 == 0, me // 2, n - 1 - me // 2)
    for s in range(n):
        to = (place + s) % n
        block = jnp.where(to < (n + 1) // 2, 2 * to, 2 * (n - to) - 1)
        at = pl.multiple_of((block * 2 + side) * half, 128)
        out_refs[s][...] = cot_ref[0, :, pl.ds(at, half)].T


def join_kernel(*refs):
    tokens = refs[0].shape[1]
    for s, ref in enumerate(refs[:-1]):
        refs[-1][:, s * tokens : (s + 1) * tokens] = ref[...]


def attention_kernel(group, scale, n, spans, place_ref, query_ref, *refs):
    kv_refs, (whole_ref, *part_refs) = refs[:n], refs[n:]
    tokens = query_ref.shape[1]
    width = kv_refs[0].shape[1] // 2
    heads = width // HD
    span = tokens // spans
    lane = lax.broadcasted_iota(jnp.int32, (1, tokens), 1)
    inner = (lane % span).astype(jnp.float32)
    key_pos = jnp.concatenate(
        [ref[tokens : tokens + 1, :tokens].astype(jnp.float32) * span + inner for ref in kv_refs],
        axis=1,
    )
    hidden = jnp.where(key_pos <= place_ref[:, :1], 0.0, -1e30)
    hidden = jnp.concatenate([hidden] * group, axis=0)
    for j in range(heads):
        first = j * group * HD
        out_ref = part_refs[j * len(part_refs) // heads]
        key_block = jnp.concatenate([ref[:tokens, j * HD : (j + 1) * HD] for ref in kv_refs], axis=0)
        value_block = jnp.concatenate(
            [ref[:tokens, width + j * HD : width + (j + 1) * HD] for ref in kv_refs], axis=0
        )
        queries = jnp.concatenate(
            [query_ref[0, :, first + g * HD : first + (g + 1) * HD] for g in range(group)], axis=0
        )
        scores = lax.dot_general(
            queries, key_block, (((1,), (1,)), ((), ())), preferred_element_type=jnp.float32
        )
        scores = jnp.where(hidden < 0.0, hidden, scores)
        top = jnp.max(scores, axis=1, keepdims=True)
        weights = jnp.exp2((scores - top) * (scale * math.log2(math.e)))
        total = jnp.sum(weights, axis=1, keepdims=True)
        mixed = jnp.dot(
            weights.astype(jnp.bfloat16), value_block, preferred_element_type=jnp.float32
        )
        mixed = (mixed / total).astype(jnp.bfloat16)
        for g in range(group):
            at, piece = first + g * HD, mixed[g * tokens : (g + 1) * tokens]
            whole_ref[0, :, at : at + HD] = piece
            at %= out_ref.shape[2]
            out_ref[0, :, at : at + HD] = piece


def left_sides(refs, tokens, first, slots):
    near, far, near_other, far_other = refs
    here = slice(first * tokens, (first + slots) * tokens)
    side = lax.axis_index("tp") & 1
    return (
        (side, jnp.concatenate([near[:, here], far[:, here]], axis=1)),
        (1 - side, jnp.concatenate([near_other[:, here], far_other[:, here]], axis=1)),
    )


def early_kernel(slots, *refs):
    att_refs, cot_refs, total_ref = refs[: 2 * slots], refs[2 * slots : -1], refs[-1]
    half = cot_refs[0].shape[0]
    tokens = att_refs[0].shape[1]
    wide = TILE if total_ref.shape[1] % TILE == 0 else total_ref.shape[1]
    for j in range(total_ref.shape[1] // wide):
        columns = slice(j * wide, (j + 1) * wide)
        rows = jnp.concatenate([ref[0, :, columns] for ref in att_refs], axis=0)
        for at, left in left_sides(cot_refs, tokens, 0, slots):
            total_ref[pl.ds(pl.multiple_of(at * half, half), half), columns] = jnp.dot(
                left, rows, preferred_element_type=jnp.float32
            )


def finish_kernel(slots, first, start, carried, width, *refs):
    att_refs, cot_refs = refs[: 2 * slots], refs[2 * slots : 2 * slots + 4]
    out_ref, held, sems = refs[-3:]
    total_ref = refs[2 * slots + 4] if carried else None
    half = cot_refs[0].shape[0]
    tokens = att_refs[0].shape[1]
    wide = held.shape[2]
    copies = []
    for j in range(width // wide):
        columns = slice(j * wide, (j + 1) * wide)
        rows = jnp.concatenate([ref[0, :, columns] for ref in att_refs], axis=0)
        if j >= 2:
            copies[j - 2].wait()
        for at, left in left_sides(cot_refs, tokens, first, slots):
            here = pl.ds(pl.multiple_of(at * half, half), half)
            value = jnp.dot(left, rows, preferred_element_type=jnp.float32)
            if carried:
                value = value + total_ref[here, columns]
            held[j % 2, here, :] = value.astype(jnp.bfloat16)
        copies.append(
            pltpu.make_async_copy(
                held.at[j % 2],
                out_ref.at[0, :, start + j * wide : start + (j + 1) * wide],
                sems.at[j % 2],
            )
        )
        copies[-1].start()
    for copy in copies[-2:]:
        copy.wait()


def local(queries, keys, values, span_ids, cotangent):
    n = lax.axis_size("ctx")
    far = lax.axis_size("pipe") // 2
    tokens, width = keys.shape[1:]
    spans = span_ids.shape[1]
    heads = queries.shape[2]
    parts = 2 if width % (2 * HD) == 0 else 1
    chunk = heads // parts
    features = cotangent.shape[2] // n
    half = features // 2

    packed, place = pl.pallas_call(
        pack_kernel,
        out_shape=[
            jax.ShapeDtypeStruct((tokens + TAG, 2 * width), jnp.bfloat16),
            jax.ShapeDtypeStruct((tokens, 128), jnp.float32),
        ],
        in_specs=[SMEM, VMEM, VMEM],
        out_specs=[VMEM] * 2,
        compiler_params=params(16),
        name="pack",
    )(span_ids, keys, values)
    kv = [packed] + [around(packed, s) for s in range(1, n)]
    query_held = pl.pallas_call(
        fetch_kernel,
        out_shape=jax.ShapeDtypeStruct(queries.shape, jnp.bfloat16),
        in_specs=[ANY, VMEM],
        out_specs=VMEM,
        compiler_params=params(16),
        name="fetch",
    )(place, queries)
    turned = pl.pallas_call(
        functools.partial(turn_kernel, n),
        out_shape=[jax.ShapeDtypeStruct((half, tokens), jnp.bfloat16)] * n,
        in_specs=[ANY, VMEM],
        out_specs=[VMEM] * n,
        compiler_params=params(16),
        name="turn",
    )(place, cotangent)
    query_held = after(query_held, *turned)
    attention, *pieces = pl.pallas_call(
        functools.partial(attention_kernel, HQ // HK, 1.0 / math.sqrt(HD), n, spans),
        out_shape=[jax.ShapeDtypeStruct(queries.shape, jnp.bfloat16)]
        + [jax.ShapeDtypeStruct((1, tokens, chunk), jnp.bfloat16)] * parts,
        in_specs=[VMEM] * (2 + n),
        out_specs=[VMEM] * (1 + parts),
        compiler_params=params(40),
        name="attend",
    )(place, query_held, *kv)

    near, mirrored = [], []
    for c in range(parts):
        held, sent = [pieces[c]], []
        for s in range(n):
            by_ring = s == n - 1 and c < parts - 1
            sent.append(around(sent[-1], 1) if by_ring else swap(held[s], "pipe", far))
            if s < n - 1:
                arrived = around(held[s], 1)
                held.append(after(arrived, sent[s]) if s < n - 2 else arrived)
        near.append(held)
        mirrored.append(sent)

    turned = [turned[0]] + [around(after(turned[s], attention), s) for s in range(1, n)]
    mine = pl.pallas_call(
        join_kernel,
        out_shape=jax.ShapeDtypeStruct((half, n * tokens), jnp.bfloat16),
        in_specs=[VMEM] * n,
        out_specs=VMEM,
        compiler_params=params(16),
        name="join",
    )(*turned[:-1], after(turned[-1], *[sent[0] for sent in mirrored]))
    mine_far = swap(mine, "pipe", far)
    cots = [mine, mine_far, swap(mine, "tp", 1), swap(mine_far, "tp", 1)]

    def attended(c, first, last):
        return near[c][first:last] + mirrored[c][first:last]

    tile = TILE if chunk % TILE == 0 else chunk
    total = pl.pallas_call(
        functools.partial(early_kernel, n - 1),
        out_shape=jax.ShapeDtypeStruct((features, chunk), jnp.float32),
        in_specs=[VMEM] * (2 * n + 2),
        out_specs=VMEM,
        compiler_params=params(40),
        cost_estimate=pl.CostEstimate(
            flops=4 * features * chunk * (n - 1) * tokens,
            bytes_accessed=8 * 2**20,
            transcendentals=0,
        ),
        name="early",
    )(*attended(parts - 1, 0, n - 1), *cots)
    grad_out = None
    for c in range(parts):
        last = c == parts - 1
        slots = 1 if last else n
        operands = attended(c, n - slots, n) + cots + ([total] if last else [])
        specs = [VMEM] * len(operands)
        aliases = {}
        if grad_out is not None:
            aliases = {len(operands): 0}
            operands.append(grad_out)
            specs.append(ANY)
        grad_out = pl.pallas_call(
            functools.partial(finish_kernel, slots, n - slots, c * chunk, last, chunk),
            out_shape=jax.ShapeDtypeStruct((1, features, heads), jnp.bfloat16),
            in_specs=specs,
            out_specs=ANY,
            scratch_shapes=[
                pltpu.VMEM((2, features, tile), jnp.bfloat16),
                pltpu.SemaphoreType.DMA((2,)),
            ],
            input_output_aliases=aliases,
            compiler_params=params(40),
            cost_estimate=pl.CostEstimate(
                flops=4 * features * chunk * slots * tokens,
                bytes_accessed=8 * 2**20,
                transcendentals=0,
            ),
            name="finish",
        )(*operands)
    return (attention, grad_out)


def solution(mesh):
    placed = (
        P("pipe", "ctx", "tp"),
        P("pipe", "ctx", "tp"),
        P("pipe", "ctx", "tp"),
        P("pipe", "ctx"),
        P("pipe", "ctx", None),
    )
    return jax.shard_map(
        local,
        mesh=mesh,
        in_specs=placed,
        out_specs=(P("pipe", "ctx", "tp"), P("pipe", "ctx", "tp")),
        check_vma=False,
    )
```

```python
import functools
import math

import jax
import jax.numpy as jnp
from jax import lax
from jax.experimental import pallas as pl
from jax.experimental.pallas import tpu as pltpu
from jax.sharding import PartitionSpec as P

HQ = 32
HK = 8
HD = 128
TAG = 16
TILE = 256
VMEM = pl.BlockSpec(memory_space=pltpu.VMEM)
SMEM = pl.BlockSpec(memory_space=pltpu.SMEM)
ANY = pl.BlockSpec(memory_space=pl.ANY)


def ring_order(n):
    return list(range(0, n, 2)) + list(range(1, n, 2))[::-1]


def around(x, shift):
    n = lax.axis_size("ctx")
    order = ring_order(n)
    return lax.ppermute(x, "ctx", [(order[q], order[(q + shift) % n]) for q in range(n)])


def swap(x, axis, mask):
    return lax.ppermute(x, axis, [(i, i ^ mask) for i in range(lax.axis_size(axis))])


def params(mib):
    return pltpu.CompilerParams(vmem_limit_bytes=mib * 2**20)


def after(x, *others):
    return lax.optimization_barrier((x, *others))[0]


def pack_kernel(span_ref, key_ref, packed_ref, place_ref):
    tokens, width = key_ref.shape[1:]
    packed_ref[0, :tokens, :] = key_ref[0]
    spans = span_ref.shape[1]
    span = tokens // spans
    lane = lax.broadcasted_iota(jnp.int32, (TAG, width), 1)
    row = lax.broadcasted_iota(jnp.int32, place_ref.shape, 0)
    ids = jnp.zeros(lane.shape, jnp.float32)
    base = jnp.zeros(row.shape, jnp.int32)
    for j in range(spans):
        ids = jnp.where(lane // span == j, span_ref[0, j].astype(jnp.float32), ids)
        base = jnp.where(row // span == j, span_ref[0, j] * span, base)
    packed_ref[0, tokens:, :] = ids.astype(jnp.bfloat16)
    place_ref[...] = (base + row % span).astype(jnp.float32)


def fetch_kernel(place_ref, query_ref, value_ref, query_held, value_held):
    query_held[...] = query_ref[...]
    value_held[...] = value_ref[...]


def turn_kernel(n, ready_ref, cot_ref, *out_refs):
    me = lax.axis_index("ctx")
    side = lax.axis_index("tp") & 1
    half = cot_ref.shape[2] // n // 2
    place = jnp.where(me % 2 == 0, me // 2, n - 1 - me // 2)
    for s in range(n):
        to = (place + s) % n
        block = jnp.where(to < (n + 1) // 2, 2 * to, 2 * (n - to) - 1)
        at = pl.multiple_of((block * 2 + side) * half, 128)
        out_refs[s][...] = cot_ref[0, :, pl.ds(at, half)].T


def join_kernel(*refs):
    tokens = refs[0].shape[1]
    for s, ref in enumerate(refs[:-1]):
        refs[-1][:, s * tokens : (s + 1) * tokens] = ref[...]


def attention_kernel(group, scale, n, spans, place_ref, query_ref, *refs):
    key_refs, value_refs, (whole_ref, *part_refs) = refs[:n], refs[n : 2 * n], refs[2 * n :]
    tokens, width = value_refs[0].shape[1:]
    heads = width // HD
    span = tokens // spans
    lane = lax.broadcasted_iota(jnp.int32, (1, tokens), 1)
    inner = (lane % span).astype(jnp.float32)
    key_pos = jnp.concatenate(
        [
            ref[0, tokens : tokens + 1, :tokens].astype(jnp.float32) * span + inner
            for ref in key_refs
        ],
        axis=1,
    )
    hidden = jnp.where(key_pos <= place_ref[:, :1], 0.0, -1e30)
    hidden = jnp.concatenate([hidden] * group, axis=0)
    for j in range(heads):
        first = j * group * HD
        out_ref = part_refs[j * len(part_refs) // heads]
        columns = slice(j * HD, (j + 1) * HD)
        key_block = jnp.concatenate([ref[0, :tokens, columns] for ref in key_refs], axis=0)
        value_block = jnp.concatenate([ref[0, :, columns] for ref in value_refs], axis=0)
        queries = jnp.concatenate(
            [query_ref[0, :, first + g * HD : first + (g + 1) * HD] for g in range(group)], axis=0
        )
        scores = lax.dot_general(
            queries, key_block, (((1,), (1,)), ((), ())), preferred_element_type=jnp.float32
        )
        scores = jnp.where(hidden < 0.0, hidden, scores)
        top = jnp.max(scores, axis=1, keepdims=True)
        weights = jnp.exp2((scores - top) * (scale * math.log2(math.e)))
        total = jnp.sum(weights, axis=1, keepdims=True)
        mixed = jnp.dot(
            weights.astype(jnp.bfloat16), value_block, preferred_element_type=jnp.float32
        )
        mixed = (mixed / total).astype(jnp.bfloat16)
        for g in range(group):
            at, piece = first + g * HD, mixed[g * tokens : (g + 1) * tokens]
            whole_ref[0, :, at : at + HD] = piece
            at %= out_ref.shape[2]
            out_ref[0, :, at : at + HD] = piece


def left_sides(refs, tokens, first, slots):
    near, far, near_other, far_other = refs
    here = slice(first * tokens, (first + slots) * tokens)
    side = lax.axis_index("tp") & 1
    return (
        (side, jnp.concatenate([near[:, here], far[:, here]], axis=1)),
        (1 - side, jnp.concatenate([near_other[:, here], far_other[:, here]], axis=1)),
    )


def early_kernel(slots, *refs):
    att_refs, cot_refs, total_ref = refs[: 2 * slots], refs[2 * slots : -1], refs[-1]
    half = cot_refs[0].shape[0]
    tokens = att_refs[0].shape[1]
    wide = TILE if total_ref.shape[1] % TILE == 0 else total_ref.shape[1]
    for j in range(total_ref.shape[1] // wide):
        columns = slice(j * wide, (j + 1) * wide)
        rows = jnp.concatenate([ref[0, :, columns] for ref in att_refs], axis=0)
        for at, left in left_sides(cot_refs, tokens, 0, slots):
            total_ref[pl.ds(pl.multiple_of(at * half, half), half), columns] = jnp.dot(
                left, rows, preferred_element_type=jnp.float32
            )


def finish_kernel(slots, first, start, carried, width, *refs):
    att_refs, cot_refs = refs[: 2 * slots], refs[2 * slots : 2 * slots + 4]
    out_ref, held, sems = refs[-3:]
    total_ref = refs[2 * slots + 4] if carried else None
    half = cot_refs[0].shape[0]
    tokens = att_refs[0].shape[1]
    wide = held.shape[2]
    copies = []
    for j in range(width // wide):
        columns = slice(j * wide, (j + 1) * wide)
        rows = jnp.concatenate([ref[0, :, columns] for ref in att_refs], axis=0)
        if j >= 2:
            copies[j - 2].wait()
        for at, left in left_sides(cot_refs, tokens, first, slots):
            here = pl.ds(pl.multiple_of(at * half, half), half)
            value = jnp.dot(left, rows, preferred_element_type=jnp.float32)
            if carried:
                value = value + total_ref[here, columns]
            held[j % 2, here, :] = value.astype(jnp.bfloat16)
        copies.append(
            pltpu.make_async_copy(
                held.at[j % 2],
                out_ref.at[0, :, start + j * wide : start + (j + 1) * wide],
                sems.at[j % 2],
            )
        )
        copies[-1].start()
    for copy in copies[-2:]:
        copy.wait()


def local(queries, keys, values, span_ids, cotangent):
    n = lax.axis_size("ctx")
    far = lax.axis_size("pipe") // 2
    tokens, width = keys.shape[1:]
    spans = span_ids.shape[1]
    heads = queries.shape[2]
    parts = 2 if width % (2 * HD) == 0 else 1
    chunk = heads // parts
    features = cotangent.shape[2] // n
    half = features // 2

    packed, place = pl.pallas_call(
        pack_kernel,
        out_shape=[
            jax.ShapeDtypeStruct((1, tokens + TAG, width), jnp.bfloat16),
            jax.ShapeDtypeStruct((tokens, 128), jnp.float32),
        ],
        in_specs=[SMEM, VMEM],
        out_specs=[VMEM] * 2,
        compiler_params=params(16),
        name="pack",
    )(span_ids, keys)
    key_ring, value_ring = [packed], [values]
    for _ in range(n - 1):
        value_ring.append(around(value_ring[-1], 1))
        key_ring.append(around(key_ring[-1], 1))
    query_held, value_held = pl.pallas_call(
        fetch_kernel,
        out_shape=[jax.ShapeDtypeStruct(x.shape, jnp.bfloat16) for x in (queries, values)],
        in_specs=[ANY, VMEM, VMEM],
        out_specs=[VMEM] * 2,
        compiler_params=params(16),
        name="fetch",
    )(place, queries, values)
    turned = pl.pallas_call(
        functools.partial(turn_kernel, n),
        out_shape=[jax.ShapeDtypeStruct((half, tokens), jnp.bfloat16)] * n,
        in_specs=[ANY, VMEM],
        out_specs=[VMEM] * n,
        compiler_params=params(16),
        name="turn",
    )(place, cotangent)
    query_held = after(query_held, *turned)
    attention, *pieces = pl.pallas_call(
        functools.partial(attention_kernel, HQ // HK, 1.0 / math.sqrt(HD), n, spans),
        out_shape=[jax.ShapeDtypeStruct(queries.shape, jnp.bfloat16)]
        + [jax.ShapeDtypeStruct((1, tokens, chunk), jnp.bfloat16)] * parts,
        in_specs=[VMEM] * (2 + 2 * n),
        out_specs=[VMEM] * (1 + parts),
        compiler_params=params(40),
        name="attend",
    )(place, query_held, *key_ring, value_held, *value_ring[1:])

    near, mirrored = [], []
    for c in range(parts):
        held, sent = [pieces[c]], []
        for s in range(n):
            by_ring = s == n - 1 and c < parts - 1
            sent.append(around(sent[-1], 1) if by_ring else swap(held[s], "pipe", far))
            if s < n - 1:
                arrived = around(held[s], 1)
                held.append(after(arrived, sent[s]) if s < n - 2 else arrived)
        near.append(held)
        mirrored.append(sent)

    turned = [turned[0]] + [around(after(turned[s], value_ring[n - 2]), s) for s in range(1, n)]
    mine = pl.pallas_call(
        join_kernel,
        out_shape=jax.ShapeDtypeStruct((half, n * tokens), jnp.bfloat16),
        in_specs=[VMEM] * n,
        out_specs=VMEM,
        compiler_params=params(16),
        name="join",
    )(*turned[:-1], after(turned[-1], *[sent[0] for sent in mirrored]))
    mine_far = swap(mine, "pipe", far)
    cots = [mine, mine_far, swap(mine, "tp", 1), swap(mine_far, "tp", 1)]

    def attended(c, first, last):
        return near[c][first:last] + mirrored[c][first:last]

    tile = TILE if chunk % TILE == 0 else chunk
    total = pl.pallas_call(
        functools.partial(early_kernel, n - 1),
        out_shape=jax.ShapeDtypeStruct((features, chunk), jnp.float32),
        in_specs=[VMEM] * (2 * n + 2),
        out_specs=VMEM,
        compiler_params=params(40),
        cost_estimate=pl.CostEstimate(
            flops=4 * features * chunk * (n - 1) * tokens,
            bytes_accessed=8 * 2**20,
            transcendentals=0,
        ),
        name="early",
    )(*attended(parts - 1, 0, n - 1), *cots)
    grad_out = None
    for c in range(parts):
        last = c == parts - 1
        slots = 1 if last else n
        operands = attended(c, n - slots, n) + cots + ([total] if last else [])
        specs = [VMEM] * len(operands)
        aliases = {}
        if grad_out is not None:
            aliases = {len(operands): 0}
            operands.append(grad_out)
            specs.append(ANY)
        grad_out = pl.pallas_call(
            functools.partial(finish_kernel, slots, n - slots, c * chunk, last, chunk),
            out_shape=jax.ShapeDtypeStruct((1, features, heads), jnp.bfloat16),
            in_specs=specs,
            out_specs=ANY,
            scratch_shapes=[
                pltpu.VMEM((2, features, tile), jnp.bfloat16),
                pltpu.SemaphoreType.DMA((2,)),
            ],
            input_output_aliases=aliases,
            compiler_params=params(40),
            cost_estimate=pl.CostEstimate(
                flops=4 * features * chunk * slots * tokens,
                bytes_accessed=8 * 2**20,
                transcendentals=0,
            ),
            name="finish",
        )(*operands)
    return (attention, grad_out)


def solution(mesh):
    placed = (
        P("pipe", "ctx", "tp"),
        P("pipe", "ctx", "tp"),
        P("pipe", "ctx", "tp"),
        P("pipe", "ctx"),
        P("pipe", "ctx", None),
    )
    return jax.shard_map(
        local,
        mesh=mesh,
        in_specs=placed,
        out_specs=(P("pipe", "ctx", "tp"), P("pipe", "ctx", "tp")),
        check_vma=False,
    )
```

```python
import functools
import math

import jax
import jax.numpy as jnp
from jax import lax
from jax.experimental import pallas as pl
from jax.experimental.pallas import tpu as pltpu
from jax.sharding import PartitionSpec as P

HQ = 32
HK = 8
HD = 128
TAG = 16
TILE = 256
VMEM = pl.BlockSpec(memory_space=pltpu.VMEM)
SMEM = pl.BlockSpec(memory_space=pltpu.SMEM)
ANY = pl.BlockSpec(memory_space=pl.ANY)


def ring_order(n):
    return list(range(0, n, 2)) + list(range(1, n, 2))[::-1]


def around(x, shift):
    n = lax.axis_size("ctx")
    order = ring_order(n)
    return lax.ppermute(x, "ctx", [(order[q], order[(q + shift) % n]) for q in range(n)])


def gather(x, ways, gate):
    n = lax.axis_size("ctx")
    middle = n // 2 if ways > 0 else (n - 1) // 2
    held = [x] + [None] * (n - 1)
    for s in range(1, max(middle, n - 1 - middle) + 1):
        if s <= middle:
            held[s] = around(gate(held[s - 1]) if s > 1 else x, 1)
        if s <= n - 1 - middle:
            held[n - s] = around(gate(held[n - s + 1]) if s > 1 else x, -1)
    return held


def swap(x, axis, mask):
    return lax.ppermute(x, axis, [(i, i ^ mask) for i in range(lax.axis_size(axis))])


def params(mib):
    return pltpu.CompilerParams(vmem_limit_bytes=mib * 2**20)


def after(x, *others):
    return lax.optimization_barrier((x, *others))[0]


def pack_kernel(span_ref, key_ref, packed_ref, place_ref):
    tokens, width = key_ref.shape[1:]
    packed_ref[0, :tokens, :] = key_ref[0]
    spans = span_ref.shape[1]
    span = tokens // spans
    lane = lax.broadcasted_iota(jnp.int32, (TAG, width), 1)
    row = lax.broadcasted_iota(jnp.int32, place_ref.shape, 0)
    ids = jnp.zeros(lane.shape, jnp.float32)
    base = jnp.zeros(row.shape, jnp.int32)
    for j in range(spans):
        ids = jnp.where(lane // span == j, span_ref[0, j].astype(jnp.float32), ids)
        base = jnp.where(row // span == j, span_ref[0, j] * span, base)
    packed_ref[0, tokens:, :] = ids.astype(jnp.bfloat16)
    place_ref[...] = (base + row % span).astype(jnp.float32)


def fetch_kernel(place_ref, query_ref, value_ref, query_held, value_held):
    query_held[...] = query_ref[...]
    value_held[...] = value_ref[...]


def turn_kernel(n, ready_ref, cot_ref, *out_refs):
    me = lax.axis_index("ctx")
    side = lax.axis_index("tp") & 1
    half = cot_ref.shape[2] // n // 2
    place = jnp.where(me % 2 == 0, me // 2, n - 1 - me // 2)
    for s in range(n):
        to = (place + s) % n
        block = jnp.where(to < (n + 1) // 2, 2 * to, 2 * (n - to) - 1)
        at = pl.multiple_of((block * 2 + side) * half, 128)
        out_refs[s][...] = cot_ref[0, :, pl.ds(at, half)].T


def join_kernel(*refs):
    tokens = refs[0].shape[1]
    for s, ref in enumerate(refs[:-1]):
        refs[-1][:, s * tokens : (s + 1) * tokens] = ref[...]


def attention_kernel(group, scale, n, spans, place_ref, query_ref, *refs):
    key_refs, value_refs, (whole_ref, *part_refs) = refs[:n], refs[n : 2 * n], refs[2 * n :]
    tokens, width = value_refs[0].shape[1:]
    heads = width // HD
    span = tokens // spans
    lane = lax.broadcasted_iota(jnp.int32, (1, tokens), 1)
    inner = (lane % span).astype(jnp.float32)
    key_pos = jnp.concatenate(
        [
            ref[0, tokens : tokens + 1, :tokens].astype(jnp.float32) * span + inner
            for ref in key_refs
        ],
        axis=1,
    )
    hidden = jnp.where(key_pos <= place_ref[:, :1], 0.0, -1e30)
    hidden = jnp.concatenate([hidden] * group, axis=0)
    for j in range(heads):
        first = j * group * HD
        out_ref = part_refs[j * len(part_refs) // heads]
        columns = slice(j * HD, (j + 1) * HD)
        key_block = jnp.concatenate([ref[0, :tokens, columns] for ref in key_refs], axis=0)
        value_block = jnp.concatenate([ref[0, :, columns] for ref in value_refs], axis=0)
        queries = jnp.concatenate(
            [query_ref[0, :, first + g * HD : first + (g + 1) * HD] for g in range(group)], axis=0
        )
        scores = lax.dot_general(
            queries, key_block, (((1,), (1,)), ((), ())), preferred_element_type=jnp.float32
        )
        scores = jnp.where(hidden < 0.0, hidden, scores)
        top = jnp.max(scores, axis=1, keepdims=True)
        weights = jnp.exp2((scores - top) * (scale * math.log2(math.e)))
        total = jnp.sum(weights, axis=1, keepdims=True)
        mixed = jnp.dot(
            weights.astype(jnp.bfloat16), value_block, preferred_element_type=jnp.float32
        )
        mixed = (mixed / total).astype(jnp.bfloat16)
        for g in range(group):
            at, piece = first + g * HD, mixed[g * tokens : (g + 1) * tokens]
            whole_ref[0, :, at : at + HD] = piece
            at %= out_ref.shape[2]
            out_ref[0, :, at : at + HD] = piece


def left_sides(refs, tokens, slots):
    near, far, near_other, far_other = refs
    side = lax.axis_index("tp") & 1
    columns = [slice(s * tokens, (s + 1) * tokens) for s in slots]
    return tuple(
        (at, jnp.concatenate([ref[:, here] for ref in pair for here in columns], axis=1))
        for at, pair in ((side, (near, far)), (1 - side, (near_other, far_other)))
    )


def early_kernel(slots, *refs):
    att_refs, cot_refs, total_ref = refs[: 2 * len(slots)], refs[2 * len(slots) : -1], refs[-1]
    half = cot_refs[0].shape[0]
    tokens = att_refs[0].shape[1]
    wide = TILE if total_ref.shape[1] % TILE == 0 else total_ref.shape[1]
    for j in range(total_ref.shape[1] // wide):
        columns = slice(j * wide, (j + 1) * wide)
        rows = jnp.concatenate([ref[0, :, columns] for ref in att_refs], axis=0)
        for at, left in left_sides(cot_refs, tokens, slots):
            total_ref[pl.ds(pl.multiple_of(at * half, half), half), columns] = jnp.dot(
                left, rows, preferred_element_type=jnp.float32
            )


def finish_kernel(slots, start, carried, width, *refs):
    count = 2 * len(slots)
    att_refs, cot_refs = refs[:count], refs[count : count + 4]
    out_ref, held, sems = refs[-3:]
    total_ref = refs[count + 4] if carried else None
    half = cot_refs[0].shape[0]
    tokens = att_refs[0].shape[1]
    wide = held.shape[2]
    copies = []
    for j in range(width // wide):
        columns = slice(j * wide, (j + 1) * wide)
        rows = jnp.concatenate([ref[0, :, columns] for ref in att_refs], axis=0)
        if j >= 2:
            copies[j - 2].wait()
        for at, left in left_sides(cot_refs, tokens, slots):
            here = pl.ds(pl.multiple_of(at * half, half), half)
            value = jnp.dot(left, rows, preferred_element_type=jnp.float32)
            if carried:
                value = value + total_ref[here, columns]
            held[j % 2, here, :] = value.astype(jnp.bfloat16)
        copies.append(
            pltpu.make_async_copy(
                held.at[j % 2],
                out_ref.at[0, :, start + j * wide : start + (j + 1) * wide],
                sems.at[j % 2],
            )
        )
        copies[-1].start()
    for copy in copies[-2:]:
        copy.wait()


def local(queries, keys, values, span_ids, cotangent):
    n = lax.axis_size("ctx")
    far = lax.axis_size("pipe") // 2
    tokens, width = keys.shape[1:]
    spans = span_ids.shape[1]
    heads = queries.shape[2]
    parts = 2 if width % (2 * HD) == 0 else 1
    chunk = heads // parts
    features = cotangent.shape[2] // n
    half = features // 2

    packed, place = pl.pallas_call(
        pack_kernel,
        out_shape=[
            jax.ShapeDtypeStruct((1, tokens + TAG, width), jnp.bfloat16),
            jax.ShapeDtypeStruct((tokens, 128), jnp.float32),
        ],
        in_specs=[SMEM, VMEM],
        out_specs=[VMEM] * 2,
        compiler_params=params(16),
        name="pack",
    )(span_ids, keys)
    query_held, value_held = pl.pallas_call(
        fetch_kernel,
        out_shape=[jax.ShapeDtypeStruct(x.shape, jnp.bfloat16) for x in (queries, values)],
        in_specs=[ANY, VMEM, VMEM],
        out_specs=[VMEM] * 2,
        compiler_params=params(16),
        name="fetch",
    )(place, queries, values)
    turned = pl.pallas_call(
        functools.partial(turn_kernel, n),
        out_shape=[jax.ShapeDtypeStruct((half, tokens), jnp.bfloat16)] * n,
        in_specs=[ANY, VMEM],
        out_specs=[VMEM] * n,
        compiler_params=params(16),
        name="turn",
    )(place, cotangent)
    key_ring = gather(packed, 1, lambda x: after(x, query_held))
    value_ring = gather(values, -1, lambda x: after(x, turned[0]))
    attention, *pieces = pl.pallas_call(
        functools.partial(attention_kernel, HQ // HK, 1.0 / math.sqrt(HD), n, spans),
        out_shape=[jax.ShapeDtypeStruct(queries.shape, jnp.bfloat16)]
        + [jax.ShapeDtypeStruct((1, tokens, chunk), jnp.bfloat16)] * parts,
        in_specs=[VMEM] * (2 + 2 * n),
        out_specs=[VMEM] * (1 + parts),
        compiler_params=params(40),
        name="attend",
    )(place, query_held, *key_ring, value_held, *value_ring[1:])

    mirrored = [[swap(piece, "pipe", far)] + [None] * (n - 1) for piece in pieces]
    near = []
    for c, piece in enumerate(pieces):
        sent = mirrored[c][:1]
        if c:
            piece = after(piece, near[0][1], near[0][-1])
            sent = sent + [mirrored[0][1], mirrored[0][-1]]
        near.append(gather(piece, 1 - 2 * c, lambda x, sent=sent: after(x, *sent)))
        for s in range(1, n):
            by_ring = s == n // 2 and c < parts - 1
            mirrored[c][s] = (
                around(mirrored[c][s - 1], 1) if by_ring else swap(near[c][s], "pipe", far)
            )
    turned = [turned[0]] + [around(after(turned[s], value_ring[n // 2]), s) for s in range(1, n)]
    mine = pl.pallas_call(
        join_kernel,
        out_shape=jax.ShapeDtypeStruct((half, n * tokens), jnp.bfloat16),
        in_specs=[VMEM] * n,
        out_specs=VMEM,
        compiler_params=params(16),
        name="join",
    )(*turned[:-1], after(turned[-1], near[0][1], near[0][-1], *[sent[0] for sent in mirrored]))
    mine_far = swap(mine, "pipe", far)
    cots = [mine, mine_far, swap(mine, "tp", 1), swap(mine_far, "tp", 1)]

    def attended(c, slots):
        return [side[c][s] for side in (near, mirrored) for s in slots]

    first_slots = [s for s in range(n) if s != n // 2]

    tile = TILE if chunk % TILE == 0 else chunk
    total = pl.pallas_call(
        functools.partial(early_kernel, first_slots),
        out_shape=jax.ShapeDtypeStruct((features, chunk), jnp.float32),
        in_specs=[VMEM] * (2 * n + 2),
        out_specs=VMEM,
        compiler_params=params(40),
        cost_estimate=pl.CostEstimate(
            flops=4 * features * chunk * (n - 1) * tokens,
            bytes_accessed=8 * 2**20,
            transcendentals=0,
        ),
        name="early",
    )(*attended(parts - 1, first_slots), *cots)
    grad_out = None
    for c in range(parts):
        last = c == parts - 1
        slots = [n // 2] if last else list(range(n))
        operands = attended(c, slots) + cots + ([total] if last else [])
        specs = [VMEM] * len(operands)
        aliases = {}
        if grad_out is not None:
            aliases = {len(operands): 0}
            operands.append(grad_out)
            specs.append(ANY)
        grad_out = pl.pallas_call(
            functools.partial(finish_kernel, slots, c * chunk, last, chunk),
            out_shape=jax.ShapeDtypeStruct((1, features, heads), jnp.bfloat16),
            in_specs=specs,
            out_specs=ANY,
            scratch_shapes=[
                pltpu.VMEM((2, features, tile), jnp.bfloat16),
                pltpu.SemaphoreType.DMA((2,)),
            ],
            input_output_aliases=aliases,
            compiler_params=params(40),
            cost_estimate=pl.CostEstimate(
                flops=4 * features * chunk * len(slots) * tokens,
                bytes_accessed=8 * 2**20,
                transcendentals=0,
            ),
            name="finish",
        )(*operands)
    return (attention, grad_out)


def solution(mesh):
    placed = (
        P("pipe", "ctx", "tp"),
        P("pipe", "ctx", "tp"),
        P("pipe", "ctx", "tp"),
        P("pipe", "ctx"),
        P("pipe", "ctx", None),
    )
    return jax.shard_map(
        local,
        mesh=mesh,
        in_specs=placed,
        out_specs=(P("pipe", "ctx", "tp"), P("pipe", "ctx", "tp")),
        check_vma=False,
    )
```

```python
import functools
import math

import jax
import jax.numpy as jnp
from jax import lax
from jax.experimental import pallas as pl
from jax.experimental.pallas import tpu as pltpu
from jax.sharding import PartitionSpec as P

HQ = 32
HK = 8
HD = 128
TAG = 16
TILE = 256
VMEM = pl.BlockSpec(memory_space=pltpu.VMEM)
SMEM = pl.BlockSpec(memory_space=pltpu.SMEM)
ANY = pl.BlockSpec(memory_space=pl.ANY)


def ring_order(n):
    return list(range(0, n, 2)) + list(range(1, n, 2))[::-1]


def around(x, shift):
    n = lax.axis_size("ctx")
    order = ring_order(n)
    return lax.ppermute(x, "ctx", [(order[q], order[(q + shift) % n]) for q in range(n)])


def gather(x, ways, gate):
    n = lax.axis_size("ctx")
    middle = n // 2 if ways > 0 else (n - 1) // 2
    held = [x] + [None] * (n - 1)
    for s in range(1, max(middle, n - 1 - middle) + 1):
        if s <= middle:
            held[s] = around(gate(held[s - 1]) if s > 1 else x, 1)
        if s <= n - 1 - middle:
            held[n - s] = around(gate(held[n - s + 1]) if s > 1 else x, -1)
    return held


def swap(x, axis, mask):
    return lax.ppermute(x, axis, [(i, i ^ mask) for i in range(lax.axis_size(axis))])


def params(mib):
    return pltpu.CompilerParams(vmem_limit_bytes=mib * 2**20)


def after(x, *others):
    return lax.optimization_barrier((x, *others))[0]


def pack_kernel(span_ref, key_ref, packed_ref, place_ref):
    tokens, width = key_ref.shape[1:]
    packed_ref[0, :tokens, :] = key_ref[0]
    spans = span_ref.shape[1]
    span = tokens // spans
    lane = lax.broadcasted_iota(jnp.int32, (TAG, width), 1)
    row = lax.broadcasted_iota(jnp.int32, place_ref.shape, 0)
    ids = jnp.zeros(lane.shape, jnp.float32)
    base = jnp.zeros(row.shape, jnp.int32)
    for j in range(spans):
        ids = jnp.where(lane // span == j, span_ref[0, j].astype(jnp.float32), ids)
        base = jnp.where(row // span == j, span_ref[0, j] * span, base)
    packed_ref[0, tokens:, :] = ids.astype(jnp.bfloat16)
    place_ref[...] = (base + row % span).astype(jnp.float32)


def fetch_kernel(place_ref, query_ref, value_ref, query_held, value_held):
    query_held[...] = query_ref[...]
    value_held[...] = value_ref[...]


def turn_kernel(n, ready_ref, cot_ref, *out_refs):
    me = lax.axis_index("ctx")
    side = lax.axis_index("tp") & 1
    half = cot_ref.shape[2] // n // 2
    place = jnp.where(me % 2 == 0, me // 2, n - 1 - me // 2)
    for s in range(n):
        to = (place + s) % n
        block = jnp.where(to < (n + 1) // 2, 2 * to, 2 * (n - to) - 1)
        at = pl.multiple_of((block * 2 + side) * half, 128)
        out_refs[s][...] = cot_ref[0, :, pl.ds(at, half)].T


def join_kernel(*refs):
    tokens = refs[0].shape[1]
    for s, ref in enumerate(refs[:-1]):
        refs[-1][:, s * tokens : (s + 1) * tokens] = ref[...]


def attention_kernel(group, scale, n, spans, place_ref, query_ref, *refs):
    key_refs, value_refs, (whole_ref, *part_refs) = refs[:n], refs[n : 2 * n], refs[2 * n :]
    tokens, width = value_refs[0].shape[1:]
    heads = width // HD
    span = tokens // spans
    lane = lax.broadcasted_iota(jnp.int32, (1, tokens), 1)
    inner = (lane % span).astype(jnp.float32)
    key_pos = jnp.concatenate(
        [
            ref[0, tokens : tokens + 1, :tokens].astype(jnp.float32) * span + inner
            for ref in key_refs
        ],
        axis=1,
    )
    hidden = jnp.where(key_pos <= place_ref[:, :1], 0.0, -1e30)
    hidden = jnp.concatenate([hidden] * group, axis=0)
    for j in range(heads):
        first = j * group * HD
        out_ref = part_refs[j * len(part_refs) // heads]
        columns = slice(j * HD, (j + 1) * HD)
        key_block = jnp.concatenate([ref[0, :tokens, columns] for ref in key_refs], axis=0)
        value_block = jnp.concatenate([ref[0, :, columns] for ref in value_refs], axis=0)
        queries = jnp.concatenate(
            [query_ref[0, :, first + g * HD : first + (g + 1) * HD] for g in range(group)], axis=0
        )
        scores = lax.dot_general(
            queries, key_block, (((1,), (1,)), ((), ())), preferred_element_type=jnp.float32
        )
        scores = jnp.where(hidden < 0.0, hidden, scores)
        top = jnp.max(scores, axis=1, keepdims=True)
        weights = jnp.exp2((scores - top) * (scale * math.log2(math.e)))
        total = jnp.sum(weights, axis=1, keepdims=True)
        mixed = jnp.dot(
            weights.astype(jnp.bfloat16), value_block, preferred_element_type=jnp.float32
        )
        mixed = (mixed / total).astype(jnp.bfloat16)
        for g in range(group):
            at, piece = first + g * HD, mixed[g * tokens : (g + 1) * tokens]
            whole_ref[0, :, at : at + HD] = piece
            at %= out_ref.shape[2]
            out_ref[0, :, at : at + HD] = piece


def left_sides(refs, tokens, slots):
    near, far, near_other, far_other = refs
    side = lax.axis_index("tp") & 1
    columns = [slice(s * tokens, (s + 1) * tokens) for s in slots]
    return tuple(
        (at, jnp.concatenate([ref[:, here] for ref in pair for here in columns], axis=1))
        for at, pair in ((side, (near, far)), (1 - side, (near_other, far_other)))
    )


def early_kernel(slots, *refs):
    att_refs, cot_refs, total_ref = refs[: 2 * len(slots)], refs[2 * len(slots) : -1], refs[-1]
    half = cot_refs[0].shape[0]
    tokens = att_refs[0].shape[1]
    wide = TILE if total_ref.shape[1] % TILE == 0 else total_ref.shape[1]
    for j in range(total_ref.shape[1] // wide):
        columns = slice(j * wide, (j + 1) * wide)
        rows = jnp.concatenate([ref[0, :, columns] for ref in att_refs], axis=0)
        for at, left in left_sides(cot_refs, tokens, slots):
            total_ref[pl.ds(pl.multiple_of(at * half, half), half), columns] = jnp.dot(
                left, rows, preferred_element_type=jnp.float32
            )


def finish_kernel(slots, start, width, *refs):
    count = 2 * len(slots)
    att_refs, cot_refs = refs[:count], refs[count : count + 4]
    out_ref, held, sems = refs[-3:]
    total_ref = refs[count + 4]
    half = cot_refs[0].shape[0]
    tokens = att_refs[0].shape[1]
    wide = held.shape[2]
    copies = []
    for j in range(width // wide):
        columns = slice(j * wide, (j + 1) * wide)
        rows = jnp.concatenate([ref[0, :, columns] for ref in att_refs], axis=0)
        if j >= 2:
            copies[j - 2].wait()
        for at, left in left_sides(cot_refs, tokens, slots):
            here = pl.ds(pl.multiple_of(at * half, half), half)
            value = jnp.dot(left, rows, preferred_element_type=jnp.float32)
            held[j % 2, here, :] = (value + total_ref[here, columns]).astype(jnp.bfloat16)
        copies.append(
            pltpu.make_async_copy(
                held.at[j % 2],
                out_ref.at[0, :, start + j * wide : start + (j + 1) * wide],
                sems.at[j % 2],
            )
        )
        copies[-1].start()
    for copy in copies[-2:]:
        copy.wait()


def local(queries, keys, values, span_ids, cotangent):
    n = lax.axis_size("ctx")
    far = lax.axis_size("pipe") // 2
    tokens, width = keys.shape[1:]
    spans = span_ids.shape[1]
    heads = queries.shape[2]
    parts = 2 if width % (2 * HD) == 0 else 1
    chunk = heads // parts
    features = cotangent.shape[2] // n
    half = features // 2

    packed, place = pl.pallas_call(
        pack_kernel,
        out_shape=[
            jax.ShapeDtypeStruct((1, tokens + TAG, width), jnp.bfloat16),
            jax.ShapeDtypeStruct((tokens, 128), jnp.float32),
        ],
        in_specs=[SMEM, VMEM],
        out_specs=[VMEM] * 2,
        compiler_params=params(16),
        name="pack",
    )(span_ids, keys)
    query_held, value_held = pl.pallas_call(
        fetch_kernel,
        out_shape=[jax.ShapeDtypeStruct(x.shape, jnp.bfloat16) for x in (queries, values)],
        in_specs=[ANY, VMEM, VMEM],
        out_specs=[VMEM] * 2,
        compiler_params=params(16),
        name="fetch",
    )(place, queries, values)
    turned = pl.pallas_call(
        functools.partial(turn_kernel, n),
        out_shape=[jax.ShapeDtypeStruct((half, tokens), jnp.bfloat16)] * n,
        in_specs=[ANY, VMEM],
        out_specs=[VMEM] * n,
        compiler_params=params(16),
        name="turn",
    )(place, cotangent)
    key_ring = gather(packed, 1, lambda x: after(x, query_held))
    value_ring = gather(values, -1, lambda x: after(x, turned[0]))
    attention, *pieces = pl.pallas_call(
        functools.partial(attention_kernel, HQ // HK, 1.0 / math.sqrt(HD), n, spans),
        out_shape=[jax.ShapeDtypeStruct(queries.shape, jnp.bfloat16)]
        + [jax.ShapeDtypeStruct((1, tokens, chunk), jnp.bfloat16)] * parts,
        in_specs=[VMEM] * (2 + 2 * n),
        out_specs=[VMEM] * (1 + parts),
        compiler_params=params(40),
        name="attend",
    )(place, query_held, *key_ring, value_held, *value_ring[1:])

    near, mirrored = [], []
    for c in range(parts):
        held, sent = [pieces[c]], []
        for s in range(n):
            by_ring = s == n - 1 and c < parts - 1
            sent.append(around(sent[-1], 1) if by_ring else swap(held[s], "pipe", far))
            if s < n - 1:
                arrived = around(held[s], 1)
                held.append(after(arrived, sent[s]) if s < n - 2 else arrived)
        near.append(held)
        mirrored.append(sent)
    turned = [turned[0]] + [around(after(turned[s], value_ring[n // 2]), s) for s in range(1, n)]
    mine = pl.pallas_call(
        join_kernel,
        out_shape=jax.ShapeDtypeStruct((half, n * tokens), jnp.bfloat16),
        in_specs=[VMEM] * n,
        out_specs=VMEM,
        compiler_params=params(16),
        name="join",
    )(*turned[:-1], after(turned[-1], *[sent[0] for sent in mirrored]))
    mine_far = swap(mine, "pipe", far)
    cots = [mine, mine_far, swap(mine, "tp", 1), swap(mine_far, "tp", 1)]

    def attended(c, slots):
        return [side[c][s] for side in (near, mirrored) for s in slots]

    first_slots = list(range(n - 1))

    tile = TILE if chunk % TILE == 0 else chunk
    totals = [
        pl.pallas_call(
        functools.partial(early_kernel, first_slots),
        out_shape=jax.ShapeDtypeStruct((features, chunk), jnp.float32),
        in_specs=[VMEM] * (2 * n + 2),
        out_specs=VMEM,
        compiler_params=params(40),
        cost_estimate=pl.CostEstimate(
            flops=4 * features * chunk * (n - 1) * tokens,
            bytes_accessed=8 * 2**20,
            transcendentals=0,
        ),
        name="early",
    )(*attended(c, first_slots), *cots)
        for c in range(parts)
    ]
    grad_out = None
    for c in range(parts):
        slots = [n - 1]
        operands = attended(c, slots) + cots + [totals[c]]
        specs = [VMEM] * len(operands)
        aliases = {}
        if grad_out is not None:
            aliases = {len(operands): 0}
            operands.append(grad_out)
            specs.append(ANY)
        grad_out = pl.pallas_call(
            functools.partial(finish_kernel, slots, c * chunk, chunk),
            out_shape=jax.ShapeDtypeStruct((1, features, heads), jnp.bfloat16),
            in_specs=specs,
            out_specs=ANY,
            scratch_shapes=[
                pltpu.VMEM((2, features, tile), jnp.bfloat16),
                pltpu.SemaphoreType.DMA((2,)),
            ],
            input_output_aliases=aliases,
            compiler_params=params(40),
            cost_estimate=pl.CostEstimate(
                flops=4 * features * chunk * len(slots) * tokens,
                bytes_accessed=8 * 2**20,
                transcendentals=0,
            ),
            name="finish",
        )(*operands)
    return (attention, grad_out)


def solution(mesh):
    placed = (
        P("pipe", "ctx", "tp"),
        P("pipe", "ctx", "tp"),
        P("pipe", "ctx", "tp"),
        P("pipe", "ctx"),
        P("pipe", "ctx", None),
    )
    return jax.shard_map(
        local,
        mesh=mesh,
        in_specs=placed,
        out_specs=(P("pipe", "ctx", "tp"), P("pipe", "ctx", "tp")),
        check_vma=False,
    )
```

```python
import functools
import math

import jax
import jax.numpy as jnp
from jax import lax
from jax.experimental import pallas as pl
from jax.experimental.pallas import tpu as pltpu
from jax.sharding import PartitionSpec as P

HQ = 32
HK = 8
HD = 128
TAG = 16
TILE = 256
VMEM = pl.BlockSpec(memory_space=pltpu.VMEM)
SMEM = pl.BlockSpec(memory_space=pltpu.SMEM)
ANY = pl.BlockSpec(memory_space=pl.ANY)


def ring_order(n):
    return list(range(0, n, 2)) + list(range(1, n, 2))[::-1]


def around(x, shift):
    n = lax.axis_size("ctx")
    order = ring_order(n)
    return lax.ppermute(x, "ctx", [(order[q], order[(q + shift) % n]) for q in range(n)])


def gather(x, ways, gate):
    n = lax.axis_size("ctx")
    middle = n // 2 if ways > 0 else (n - 1) // 2
    held = [x] + [None] * (n - 1)
    for s in range(1, max(middle, n - 1 - middle) + 1):
        if s <= middle:
            held[s] = around(gate(held[s - 1]) if s > 1 else x, 1)
        if s <= n - 1 - middle:
            held[n - s] = around(gate(held[n - s + 1]) if s > 1 else x, -1)
    return held


def swap(x, axis, mask):
    return lax.ppermute(x, axis, [(i, i ^ mask) for i in range(lax.axis_size(axis))])


def params(mib):
    return pltpu.CompilerParams(vmem_limit_bytes=mib * 2**20)


def after(x, *others):
    return lax.optimization_barrier((x, *others))[0]


def pack_kernel(span_ref, key_ref, packed_ref, place_ref):
    tokens, width = key_ref.shape[1:]
    packed_ref[0, :tokens, :] = key_ref[0]
    spans = span_ref.shape[1]
    span = tokens // spans
    lane = lax.broadcasted_iota(jnp.int32, (TAG, width), 1)
    row = lax.broadcasted_iota(jnp.int32, place_ref.shape, 0)
    ids = jnp.zeros(lane.shape, jnp.float32)
    base = jnp.zeros(row.shape, jnp.int32)
    for j in range(spans):
        ids = jnp.where(lane // span == j, span_ref[0, j].astype(jnp.float32), ids)
        base = jnp.where(row // span == j, span_ref[0, j] * span, base)
    packed_ref[0, tokens:, :] = ids.astype(jnp.bfloat16)
    place_ref[...] = (base + row % span).astype(jnp.float32)


def fetch_kernel(place_ref, query_ref, value_ref, query_held, value_held):
    query_held[...] = query_ref[...]
    value_held[...] = value_ref[...]


def turn_kernel(n, ready_ref, cot_ref, *out_refs):
    me = lax.axis_index("ctx")
    side = lax.axis_index("tp") & 1
    half = cot_ref.shape[2] // n // 2
    place = jnp.where(me % 2 == 0, me // 2, n - 1 - me // 2)
    for s in range(n):
        to = (place + s) % n
        block = jnp.where(to < (n + 1) // 2, 2 * to, 2 * (n - to) - 1)
        at = pl.multiple_of((block * 2 + side) * half, 128)
        out_refs[s][...] = cot_ref[0, :, pl.ds(at, half)].T


def join_kernel(*refs):
    tokens = refs[0].shape[1]
    for s, ref in enumerate(refs[:-1]):
        refs[-1][:, s * tokens : (s + 1) * tokens] = ref[...]


def attention_kernel(group, scale, n, spans, place_ref, query_ref, *refs):
    key_refs, value_refs, (whole_ref, *part_refs) = refs[:n], refs[n : 2 * n], refs[2 * n :]
    tokens, width = value_refs[0].shape[1:]
    heads = width // HD
    span = tokens // spans
    lane = lax.broadcasted_iota(jnp.int32, (1, tokens), 1)
    inner = (lane % span).astype(jnp.float32)
    key_pos = jnp.concatenate(
        [
            ref[0, tokens : tokens + 1, :tokens].astype(jnp.float32) * span + inner
            for ref in key_refs
        ],
        axis=1,
    )
    hidden = jnp.where(key_pos <= place_ref[:, :1], 0.0, -1e30)
    hidden = jnp.concatenate([hidden] * group, axis=0)
    for j in range(heads):
        first = j * group * HD
        out_ref = part_refs[j * len(part_refs) // heads]
        columns = slice(j * HD, (j + 1) * HD)
        key_block = jnp.concatenate([ref[0, :tokens, columns] for ref in key_refs], axis=0)
        value_block = jnp.concatenate([ref[0, :, columns] for ref in value_refs], axis=0)
        queries = jnp.concatenate(
            [query_ref[0, :, first + g * HD : first + (g + 1) * HD] for g in range(group)], axis=0
        )
        scores = lax.dot_general(
            queries, key_block, (((1,), (1,)), ((), ())), preferred_element_type=jnp.float32
        )
        scores = jnp.where(hidden < 0.0, hidden, scores)
        top = jnp.max(scores, axis=1, keepdims=True)
        weights = jnp.exp2((scores - top) * (scale * math.log2(math.e)))
        total = jnp.sum(weights, axis=1, keepdims=True)
        mixed = jnp.dot(
            weights.astype(jnp.bfloat16), value_block, preferred_element_type=jnp.float32
        )
        mixed = (mixed / total).astype(jnp.bfloat16)
        for g in range(group):
            at, piece = first + g * HD, mixed[g * tokens : (g + 1) * tokens]
            whole_ref[0, :, at : at + HD] = piece
            at %= out_ref.shape[2]
            out_ref[0, :, at : at + HD] = piece


def left_sides(refs, tokens, slots):
    near, far, near_other, far_other = refs
    side = lax.axis_index("tp") & 1
    columns = [slice(s * tokens, (s + 1) * tokens) for s in slots]
    return tuple(
        (at, jnp.concatenate([ref[:, here] for ref in pair for here in columns], axis=1))
        for at, pair in ((side, (near, far)), (1 - side, (near_other, far_other)))
    )


def early_kernel(slots, *refs):
    att_refs, cot_refs, total_ref = refs[: 2 * len(slots)], refs[2 * len(slots) : -1], refs[-1]
    half = cot_refs[0].shape[0]
    tokens = att_refs[0].shape[1]
    wide = TILE if total_ref.shape[1] % TILE == 0 else total_ref.shape[1]
    for j in range(total_ref.shape[1] // wide):
        columns = slice(j * wide, (j + 1) * wide)
        rows = jnp.concatenate([ref[0, :, columns] for ref in att_refs], axis=0)
        for at, left in left_sides(cot_refs, tokens, slots):
            total_ref[pl.ds(pl.multiple_of(at * half, half), half), columns] = jnp.dot(
                left, rows, preferred_element_type=jnp.float32
            )


def finish_kernel(slots, start, width, *refs):
    count = 2 * len(slots)
    att_refs, cot_refs = refs[:count], refs[count : count + 4]
    out_ref, held, sems = refs[-3:]
    total_ref = refs[count + 4]
    half = cot_refs[0].shape[0]
    tokens = att_refs[0].shape[1]
    wide = held.shape[2]
    copies = []
    for j in range(width // wide):
        columns = slice(j * wide, (j + 1) * wide)
        rows = jnp.concatenate([ref[0, :, columns] for ref in att_refs], axis=0)
        if j >= 2:
            copies[j - 2].wait()
        for at, left in left_sides(cot_refs, tokens, slots):
            here = pl.ds(pl.multiple_of(at * half, half), half)
            value = jnp.dot(left, rows, preferred_element_type=jnp.float32)
            held[j % 2, here, :] = (value + total_ref[here, columns]).astype(jnp.bfloat16)
        copies.append(
            pltpu.make_async_copy(
                held.at[j % 2],
                out_ref.at[0, :, start + j * wide : start + (j + 1) * wide],
                sems.at[j % 2],
            )
        )
        copies[-1].start()
    for copy in copies[-2:]:
        copy.wait()


def local(queries, keys, values, span_ids, cotangent):
    n = lax.axis_size("ctx")
    far = lax.axis_size("pipe") // 2
    tokens, width = keys.shape[1:]
    spans = span_ids.shape[1]
    heads = queries.shape[2]
    parts = 2 if width % (2 * HD) == 0 else 1
    chunk = heads // parts
    features = cotangent.shape[2] // n
    half = features // 2

    packed, place = pl.pallas_call(
        pack_kernel,
        out_shape=[
            jax.ShapeDtypeStruct((1, tokens + TAG, width), jnp.bfloat16),
            jax.ShapeDtypeStruct((tokens, 128), jnp.float32),
        ],
        in_specs=[SMEM, VMEM],
        out_specs=[VMEM] * 2,
        compiler_params=params(16),
        name="pack",
    )(span_ids, keys)
    query_held, value_held = pl.pallas_call(
        fetch_kernel,
        out_shape=[jax.ShapeDtypeStruct(x.shape, jnp.bfloat16) for x in (queries, values)],
        in_specs=[ANY, VMEM, VMEM],
        out_specs=[VMEM] * 2,
        compiler_params=params(16),
        name="fetch",
    )(place, queries, values)
    turned = pl.pallas_call(
        functools.partial(turn_kernel, n),
        out_shape=[jax.ShapeDtypeStruct((half, tokens), jnp.bfloat16)] * n,
        in_specs=[ANY, VMEM],
        out_specs=[VMEM] * n,
        compiler_params=params(16),
        name="turn",
    )(place, cotangent)
    key_ring = gather(packed, 1, lambda x: after(x, query_held))
    value_ring = gather(values, -1, lambda x: after(x, turned[0]))
    turned = [turned[0]] + [around(turned[s], s) for s in range(1, n)]
    mine = pl.pallas_call(
        join_kernel,
        out_shape=jax.ShapeDtypeStruct((half, n * tokens), jnp.bfloat16),
        in_specs=[VMEM] * n,
        out_specs=VMEM,
        compiler_params=params(16),
        name="join",
    )(*turned)
    mine_far = swap(mine, "pipe", far)
    query_held = after(query_held, mine)
    attention, *pieces = pl.pallas_call(
        functools.partial(attention_kernel, HQ // HK, 1.0 / math.sqrt(HD), n, spans),
        out_shape=[jax.ShapeDtypeStruct(queries.shape, jnp.bfloat16)]
        + [jax.ShapeDtypeStruct((1, tokens, chunk), jnp.bfloat16)] * parts,
        in_specs=[VMEM] * (2 + 2 * n),
        out_specs=[VMEM] * (1 + parts),
        compiler_params=params(40),
        name="attend",
    )(place, query_held, *key_ring, value_held, *value_ring[1:])

    near, mirrored = [], []
    for c in range(parts):
        held, sent = [pieces[c]], []
        for s in range(n):
            by_ring = s == n - 1 and c < parts - 1
            sent.append(around(sent[-1], 1) if by_ring else swap(held[s], "pipe", far))
            if s < n - 1:
                arrived = around(held[s], 1)
                held.append(after(arrived, sent[s]) if s < n - 2 else arrived)
        near.append(held)
        mirrored.append(sent)
    cots = [mine, mine_far, swap(mine, "tp", 1), swap(mine_far, "tp", 1)]

    def attended(c, slots):
        return [side[c][s] for side in (near, mirrored) for s in slots]

    first_slots = list(range(n - 1))

    tile = TILE if chunk % TILE == 0 else chunk
    totals = [
        pl.pallas_call(
        functools.partial(early_kernel, first_slots),
        out_shape=jax.ShapeDtypeStruct((features, chunk), jnp.float32),
        in_specs=[VMEM] * (2 * n + 2),
        out_specs=VMEM,
        compiler_params=params(40),
        cost_estimate=pl.CostEstimate(
            flops=4 * features * chunk * (n - 1) * tokens,
            bytes_accessed=8 * 2**20,
            transcendentals=0,
        ),
        name="early",
    )(*attended(c, first_slots), *cots)
        for c in range(parts)
    ]
    grad_out = None
    for c in range(parts):
        slots = [n - 1]
        operands = attended(c, slots) + cots + [totals[c]]
        specs = [VMEM] * len(operands)
        aliases = {}
        if grad_out is not None:
            aliases = {len(operands): 0}
            operands.append(grad_out)
            specs.append(ANY)
        grad_out = pl.pallas_call(
            functools.partial(finish_kernel, slots, c * chunk, chunk),
            out_shape=jax.ShapeDtypeStruct((1, features, heads), jnp.bfloat16),
            in_specs=specs,
            out_specs=ANY,
            scratch_shapes=[
                pltpu.VMEM((2, features, tile), jnp.bfloat16),
                pltpu.SemaphoreType.DMA((2,)),
            ],
            input_output_aliases=aliases,
            compiler_params=params(40),
            cost_estimate=pl.CostEstimate(
                flops=4 * features * chunk * len(slots) * tokens,
                bytes_accessed=8 * 2**20,
                transcendentals=0,
            ),
            name="finish",
        )(*operands)
    return (attention, grad_out)


def solution(mesh):
    placed = (
        P("pipe", "ctx", "tp"),
        P("pipe", "ctx", "tp"),
        P("pipe", "ctx", "tp"),
        P("pipe", "ctx"),
        P("pipe", "ctx", None),
    )
    return jax.shard_map(
        local,
        mesh=mesh,
        in_specs=placed,
        out_specs=(P("pipe", "ctx", "tp"), P("pipe", "ctx", "tp")),
        check_vma=False,
    )
```

```python
import functools
import math

import jax
import jax.numpy as jnp
from jax import lax
from jax.experimental import pallas as pl
from jax.experimental.pallas import tpu as pltpu
from jax.sharding import PartitionSpec as P

HQ = 32
HK = 8
HD = 128
TAG = 16
TILE = 256
VMEM = pl.BlockSpec(memory_space=pltpu.VMEM)
SMEM = pl.BlockSpec(memory_space=pltpu.SMEM)
ANY = pl.BlockSpec(memory_space=pl.ANY)


def ring_order(n):
    return list(range(0, n, 2)) + list(range(1, n, 2))[::-1]


def around(x, shift):
    n = lax.axis_size("ctx")
    order = ring_order(n)
    return lax.ppermute(x, "ctx", [(order[q], order[(q + shift) % n]) for q in range(n)])


def gather(x, ways, gate):
    n = lax.axis_size("ctx")
    middle = n // 2 if ways > 0 else (n - 1) // 2
    held = [x] + [None] * (n - 1)
    for s in range(1, max(middle, n - 1 - middle) + 1):
        if s <= middle:
            held[s] = around(gate(held[s - 1]) if s > 1 else x, 1)
        if s <= n - 1 - middle:
            held[n - s] = around(gate(held[n - s + 1]) if s > 1 else x, -1)
    return held


def swap(x, axis, mask):
    return lax.ppermute(x, axis, [(i, i ^ mask) for i in range(lax.axis_size(axis))])


def params(mib):
    return pltpu.CompilerParams(vmem_limit_bytes=mib * 2**20)


def after(x, *others):
    return lax.optimization_barrier((x, *others))[0]


def pack_kernel(turned_ref, span_ref, key_ref, packed_ref, place_ref):
    tokens, width = key_ref.shape[1:]
    packed_ref[0, :tokens, :] = key_ref[0]
    spans = span_ref.shape[1]
    span = tokens // spans
    lane = lax.broadcasted_iota(jnp.int32, (TAG, width), 1)
    row = lax.broadcasted_iota(jnp.int32, place_ref.shape, 0)
    ids = jnp.zeros(lane.shape, jnp.float32)
    base = jnp.zeros(row.shape, jnp.int32)
    for j in range(spans):
        ids = jnp.where(lane // span == j, span_ref[0, j].astype(jnp.float32), ids)
        base = jnp.where(row // span == j, span_ref[0, j] * span, base)
    packed_ref[0, tokens:, :] = ids.astype(jnp.bfloat16)
    place_ref[...] = (base + row % span).astype(jnp.float32)


def fetch_kernel(place_ref, query_ref, value_ref, query_held, value_held):
    query_held[...] = query_ref[...]
    value_held[...] = value_ref[...]


def turn_kernel(n, cot_ref, *out_refs):
    me = lax.axis_index("ctx")
    side = lax.axis_index("tp") & 1
    half = cot_ref.shape[2] // n // 2
    place = jnp.where(me % 2 == 0, me // 2, n - 1 - me // 2)
    for s in range(n):
        to = (place + s) % n
        block = jnp.where(to < (n + 1) // 2, 2 * to, 2 * (n - to) - 1)
        at = pl.multiple_of((block * 2 + side) * half, 128)
        out_refs[s][...] = cot_ref[0, :, pl.ds(at, half)].T


def join_kernel(*refs):
    tokens = refs[0].shape[1]
    for s, ref in enumerate(refs[:-1]):
        refs[-1][:, s * tokens : (s + 1) * tokens] = ref[...]


def attention_kernel(group, scale, n, spans, place_ref, query_ref, *refs):
    key_refs, value_refs, (whole_ref, *part_refs) = refs[:n], refs[n : 2 * n], refs[2 * n :]
    tokens, width = value_refs[0].shape[1:]
    heads = width // HD
    span = tokens // spans
    lane = lax.broadcasted_iota(jnp.int32, (1, tokens), 1)
    inner = (lane % span).astype(jnp.float32)
    key_pos = jnp.concatenate(
        [
            ref[0, tokens : tokens + 1, :tokens].astype(jnp.float32) * span + inner
            for ref in key_refs
        ],
        axis=1,
    )
    hidden = jnp.where(key_pos <= place_ref[:, :1], 0.0, -1e30)
    hidden = jnp.concatenate([hidden] * group, axis=0)
    for j in range(heads):
        first = j * group * HD
        out_ref = part_refs[j * len(part_refs) // heads]
        columns = slice(j * HD, (j + 1) * HD)
        key_block = jnp.concatenate([ref[0, :tokens, columns] for ref in key_refs], axis=0)
        value_block = jnp.concatenate([ref[0, :, columns] for ref in value_refs], axis=0)
        queries = jnp.concatenate(
            [query_ref[0, :, first + g * HD : first + (g + 1) * HD] for g in range(group)], axis=0
        )
        scores = lax.dot_general(
            queries, key_block, (((1,), (1,)), ((), ())), preferred_element_type=jnp.float32
        )
        scores = jnp.where(hidden < 0.0, hidden, scores)
        top = jnp.max(scores, axis=1, keepdims=True)
        weights = jnp.exp2((scores - top) * (scale * math.log2(math.e)))
        total = jnp.sum(weights, axis=1, keepdims=True)
        mixed = jnp.dot(
            weights.astype(jnp.bfloat16), value_block, preferred_element_type=jnp.float32
        )
        mixed = (mixed / total).astype(jnp.bfloat16)
        for g in range(group):
            at, piece = first + g * HD, mixed[g * tokens : (g + 1) * tokens]
            whole_ref[0, :, at : at + HD] = piece
            at %= out_ref.shape[2]
            out_ref[0, :, at : at + HD] = piece


def left_sides(refs, tokens, slots):
    near, far, near_other, far_other = refs
    side = lax.axis_index("tp") & 1
    columns = [slice(s * tokens, (s + 1) * tokens) for s in slots]
    return tuple(
        (at, jnp.concatenate([ref[:, here] for ref in pair for here in columns], axis=1))
        for at, pair in ((side, (near, far)), (1 - side, (near_other, far_other)))
    )


def early_kernel(slots, *refs):
    att_refs, cot_refs, total_ref = refs[: 2 * len(slots)], refs[2 * len(slots) : -1], refs[-1]
    half = cot_refs[0].shape[0]
    tokens = att_refs[0].shape[1]
    wide = TILE if total_ref.shape[1] % TILE == 0 else total_ref.shape[1]
    for j in range(total_ref.shape[1] // wide):
        columns = slice(j * wide, (j + 1) * wide)
        rows = jnp.concatenate([ref[0, :, columns] for ref in att_refs], axis=0)
        for at, left in left_sides(cot_refs, tokens, slots):
            total_ref[pl.ds(pl.multiple_of(at * half, half), half), columns] = jnp.dot(
                left, rows, preferred_element_type=jnp.float32
            )


def finish_kernel(slots, start, *refs):
    count = 2 * len(slots)
    att_refs, cot_refs, total_ref = refs[:count], refs[count : count + 4], refs[count + 4]
    out_ref, held, sems = refs[-3:]
    tokens, width = att_refs[0].shape[1:]
    tall = held.shape[1]
    half = cot_refs[0].shape[0]
    rows = jnp.concatenate([ref[0] for ref in att_refs], axis=0)
    copies = []
    for at, left in left_sides(cot_refs, tokens, slots):
        for i in range(half // tall):
            here = pl.ds(pl.multiple_of(at * half + i * tall, tall), tall)
            slot = len(copies) % 2
            if len(copies) >= 2:
                copies[-2].wait()
            held[slot] = (
                total_ref[here, :]
                + jnp.dot(
                    left[i * tall : (i + 1) * tall], rows, preferred_element_type=jnp.float32
                )
            ).astype(jnp.bfloat16)
            copies.append(
                pltpu.make_async_copy(
                    held.at[slot], out_ref.at[0, here, start : start + width], sems.at[slot]
                )
            )
            copies[-1].start()
    for copy in copies[-2:]:
        copy.wait()


def local(queries, keys, values, span_ids, cotangent):
    n = lax.axis_size("ctx")
    far = lax.axis_size("pipe") // 2
    tokens, width = keys.shape[1:]
    spans = span_ids.shape[1]
    heads = queries.shape[2]
    parts = 2 if width % (2 * HD) == 0 else 1
    chunk = heads // parts
    features = cotangent.shape[2] // n
    half = features // 2

    turned = pl.pallas_call(
        functools.partial(turn_kernel, n),
        out_shape=[jax.ShapeDtypeStruct((half, tokens), jnp.bfloat16)] * n,
        in_specs=[VMEM],
        out_specs=[VMEM] * n,
        compiler_params=params(16),
        name="turn",
    )(cotangent)
    packed, place = pl.pallas_call(
        pack_kernel,
        out_shape=[
            jax.ShapeDtypeStruct((1, tokens + TAG, width), jnp.bfloat16),
            jax.ShapeDtypeStruct((tokens, 128), jnp.float32),
        ],
        in_specs=[ANY, SMEM, VMEM],
        out_specs=[VMEM] * 2,
        compiler_params=params(16),
        name="pack",
    )(turned[0], span_ids, keys)
    query_held, value_held = pl.pallas_call(
        fetch_kernel,
        out_shape=[jax.ShapeDtypeStruct(x.shape, jnp.bfloat16) for x in (queries, values)],
        in_specs=[ANY, VMEM, VMEM],
        out_specs=[VMEM] * 2,
        compiler_params=params(16),
        name="fetch",
    )(place, queries, values)
    turned = [turned[0]] + [around(turned[s], s) for s in range(1, n)]
    mine = pl.pallas_call(
        join_kernel,
        out_shape=jax.ShapeDtypeStruct((half, n * tokens), jnp.bfloat16),
        in_specs=[VMEM] * n,
        out_specs=VMEM,
        compiler_params=params(16),
        name="join",
    )(*turned)
    mine_far = swap(mine, "pipe", far)
    key_ring = gather(packed, 1, lambda x: after(x, query_held, mine))
    value_ring = gather(values, -1, lambda x: after(x, value_held, mine))
    attention, *pieces = pl.pallas_call(
        functools.partial(attention_kernel, HQ // HK, 1.0 / math.sqrt(HD), n, spans),
        out_shape=[jax.ShapeDtypeStruct(queries.shape, jnp.bfloat16)]
        + [jax.ShapeDtypeStruct((1, tokens, chunk), jnp.bfloat16)] * parts,
        in_specs=[VMEM] * (2 + 2 * n),
        out_specs=[VMEM] * (1 + parts),
        compiler_params=params(40),
        name="attend",
    )(place, query_held, *key_ring, value_held, *value_ring[1:])

    near, mirrored = [], []
    for c in range(parts):
        held, sent = [pieces[c]], []
        for s in range(n):
            by_ring = s == n - 1 and c < parts - 1
            sent.append(around(sent[-1], 1) if by_ring else swap(held[s], "pipe", far))
            if s < n - 1:
                arrived = around(held[s], 1)
                held.append(after(arrived, sent[s]) if s < n - 2 else arrived)
        near.append(held)
        mirrored.append(sent)
    cots = [mine, mine_far, swap(mine, "tp", 1), swap(mine_far, "tp", 1)]

    def attended(c, slots):
        return [side[c][s] for side in (near, mirrored) for s in slots]

    first_slots = list(range(n - 1))

    tall = TILE if half % TILE == 0 else half
    totals = [
        pl.pallas_call(
        functools.partial(early_kernel, first_slots),
        out_shape=jax.ShapeDtypeStruct((features, chunk), jnp.float32),
        in_specs=[VMEM] * (2 * n + 2),
        out_specs=VMEM,
        compiler_params=params(40),
        cost_estimate=pl.CostEstimate(
            flops=4 * features * chunk * (n - 1) * tokens,
            bytes_accessed=8 * 2**20,
            transcendentals=0,
        ),
        name="early",
    )(*attended(c, first_slots), *cots)
        for c in range(parts)
    ]
    grad_out = None
    for c in range(parts):
        slots = [n - 1]
        operands = attended(c, slots) + cots + [totals[c]]
        specs = [VMEM] * len(operands)
        aliases = {}
        if grad_out is not None:
            aliases = {len(operands): 0}
            operands.append(grad_out)
            specs.append(ANY)
        grad_out = pl.pallas_call(
            functools.partial(finish_kernel, slots, c * chunk),
            out_shape=jax.ShapeDtypeStruct((1, features, heads), jnp.bfloat16),
            in_specs=specs,
            out_specs=ANY,
            scratch_shapes=[
                pltpu.VMEM((2, tall, chunk), jnp.bfloat16),
                pltpu.SemaphoreType.DMA((2,)),
            ],
            input_output_aliases=aliases,
            compiler_params=params(40),
            cost_estimate=pl.CostEstimate(
                flops=4 * features * chunk * len(slots) * tokens,
                bytes_accessed=8 * 2**20,
                transcendentals=0,
            ),
            name="finish",
        )(*operands)
    return (attention, grad_out)


def solution(mesh):
    placed = (
        P("pipe", "ctx", "tp"),
        P("pipe", "ctx", "tp"),
        P("pipe", "ctx", "tp"),
        P("pipe", "ctx"),
        P("pipe", "ctx", None),
    )
    return jax.shard_map(
        local,
        mesh=mesh,
        in_specs=placed,
        out_specs=(P("pipe", "ctx", "tp"), P("pipe", "ctx", "tp")),
        check_vma=False,
    )
```

```python
import functools
import math

import jax
import jax.numpy as jnp
from jax import lax
from jax.experimental import pallas as pl
from jax.experimental.pallas import tpu as pltpu
from jax.sharding import PartitionSpec as P

HQ = 32
HK = 8
HD = 128
TAG = 16
TILE = 256
VMEM = pl.BlockSpec(memory_space=pltpu.VMEM)
SMEM = pl.BlockSpec(memory_space=pltpu.SMEM)
ANY = pl.BlockSpec(memory_space=pl.ANY)


def ring_order(n):
    return list(range(0, n, 2)) + list(range(1, n, 2))[::-1]


def around(x, shift):
    n = lax.axis_size("ctx")
    order = ring_order(n)
    return lax.ppermute(x, "ctx", [(order[q], order[(q + shift) % n]) for q in range(n)])


def gather(x, edges, ways, gate):
    n = lax.axis_size("ctx")
    middle = n // 2 if ways > 0 else (n - 1) // 2
    held = [x] + [None] * (n - 1)
    held[1], held[-1] = edges
    for s in range(2, middle + 1):
        held[s] = around(gate(held[s - 1]), 1)
    for s in range(2, n - middle):
        held[n - s] = around(gate(held[n - s + 1]), -1)
    return held


def swap(x, axis, mask):
    return lax.ppermute(x, axis, [(i, i ^ mask) for i in range(lax.axis_size(axis))])


def params(mib):
    return pltpu.CompilerParams(vmem_limit_bytes=mib * 2**20)


def after(x, *others):
    return lax.optimization_barrier((x, *others))[0]


def pack_kernel(turned_ref, span_ref, key_ref, packed_ref, place_ref):
    tokens, width = key_ref.shape[1:]
    packed_ref[0, :tokens, :] = key_ref[0]
    spans = span_ref.shape[1]
    span = tokens // spans
    lane = lax.broadcasted_iota(jnp.int32, (TAG, width), 1)
    row = lax.broadcasted_iota(jnp.int32, place_ref.shape, 0)
    ids = jnp.zeros(lane.shape, jnp.float32)
    base = jnp.zeros(row.shape, jnp.int32)
    for j in range(spans):
        ids = jnp.where(lane // span == j, span_ref[0, j].astype(jnp.float32), ids)
        base = jnp.where(row // span == j, span_ref[0, j] * span, base)
    packed_ref[0, tokens:, :] = ids.astype(jnp.bfloat16)
    place_ref[...] = (base + row % span).astype(jnp.float32)


def fetch_kernel(place_ref, query_ref, value_ref, query_held, value_held):
    query_held[...] = query_ref[...]
    value_held[...] = value_ref[...]


def turn_kernel(n, cot_ref, *out_refs):
    me = lax.axis_index("ctx")
    side = lax.axis_index("tp") & 1
    half = cot_ref.shape[2] // n // 2
    place = jnp.where(me % 2 == 0, me // 2, n - 1 - me // 2)
    for s in range(n):
        to = (place + s) % n
        block = jnp.where(to < (n + 1) // 2, 2 * to, 2 * (n - to) - 1)
        at = pl.multiple_of((block * 2 + side) * half, 128)
        out_refs[s][...] = cot_ref[0, :, pl.ds(at, half)].T


def join_kernel(*refs):
    tokens = refs[0].shape[1]
    for s, ref in enumerate(refs[:-1]):
        refs[-1][:, s * tokens : (s + 1) * tokens] = ref[...]


def attention_kernel(group, scale, n, spans, place_ref, query_ref, *refs):
    key_refs, value_refs, (whole_ref, *part_refs) = refs[:n], refs[n : 2 * n], refs[2 * n :]
    tokens, width = value_refs[0].shape[1:]
    heads = width // HD
    span = tokens // spans
    lane = lax.broadcasted_iota(jnp.int32, (1, tokens), 1)
    inner = (lane % span).astype(jnp.float32)
    key_pos = jnp.concatenate(
        [
            ref[0, tokens : tokens + 1, :tokens].astype(jnp.float32) * span + inner
            for ref in key_refs
        ],
        axis=1,
    )
    hidden = jnp.where(key_pos <= place_ref[:, :1], 0.0, -1e30)
    hidden = jnp.concatenate([hidden] * group, axis=0)
    for j in range(heads):
        first = j * group * HD
        out_ref = part_refs[j * len(part_refs) // heads]
        columns = slice(j * HD, (j + 1) * HD)
        key_block = jnp.concatenate([ref[0, :tokens, columns] for ref in key_refs], axis=0)
        value_block = jnp.concatenate([ref[0, :, columns] for ref in value_refs], axis=0)
        queries = jnp.concatenate(
            [query_ref[0, :, first + g * HD : first + (g + 1) * HD] for g in range(group)], axis=0
        )
        scores = lax.dot_general(
            queries, key_block, (((1,), (1,)), ((), ())), preferred_element_type=jnp.float32
        )
        scores = jnp.where(hidden < 0.0, hidden, scores)
        top = jnp.max(scores, axis=1, keepdims=True)
        weights = jnp.exp2((scores - top) * (scale * math.log2(math.e)))
        total = jnp.sum(weights, axis=1, keepdims=True)
        mixed = jnp.dot(
            weights.astype(jnp.bfloat16), value_block, preferred_element_type=jnp.float32
        )
        mixed = (mixed / total).astype(jnp.bfloat16)
        for g in range(group):
            at, piece = first + g * HD, mixed[g * tokens : (g + 1) * tokens]
            whole_ref[0, :, at : at + HD] = piece
            at %= out_ref.shape[2]
            out_ref[0, :, at : at + HD] = piece


def left_sides(refs, tokens, slots):
    near, far, near_other, far_other = refs
    side = lax.axis_index("tp") & 1
    columns = [slice(s * tokens, (s + 1) * tokens) for s in slots]
    return tuple(
        (at, jnp.concatenate([ref[:, here] for ref in pair for here in columns], axis=1))
        for at, pair in ((side, (near, far)), (1 - side, (near_other, far_other)))
    )


def early_kernel(slots, *refs):
    att_refs, cot_refs, total_ref = refs[: 2 * len(slots)], refs[2 * len(slots) : -1], refs[-1]
    half = cot_refs[0].shape[0]
    tokens = att_refs[0].shape[1]
    wide = TILE if total_ref.shape[1] % TILE == 0 else total_ref.shape[1]
    for j in range(total_ref.shape[1] // wide):
        columns = slice(j * wide, (j + 1) * wide)
        rows = jnp.concatenate([ref[0, :, columns] for ref in att_refs], axis=0)
        for at, left in left_sides(cot_refs, tokens, slots):
            total_ref[pl.ds(pl.multiple_of(at * half, half), half), columns] = jnp.dot(
                left, rows, preferred_element_type=jnp.float32
            )


def finish_kernel(slots, start, *refs):
    count = 2 * len(slots)
    att_refs, cot_refs, total_ref = refs[:count], refs[count : count + 4], refs[count + 4]
    out_ref, held, sems = refs[-3:]
    tokens, width = att_refs[0].shape[1:]
    tall = held.shape[1]
    half = cot_refs[0].shape[0]
    rows = jnp.concatenate([ref[0] for ref in att_refs], axis=0)
    copies = []
    for at, left in left_sides(cot_refs, tokens, slots):
        for i in range(half // tall):
            here = pl.ds(pl.multiple_of(at * half + i * tall, tall), tall)
            slot = len(copies) % 2
            if len(copies) >= 2:
                copies[-2].wait()
            held[slot] = (
                total_ref[here, :]
                + jnp.dot(
                    left[i * tall : (i + 1) * tall], rows, preferred_element_type=jnp.float32
                )
            ).astype(jnp.bfloat16)
            copies.append(
                pltpu.make_async_copy(
                    held.at[slot], out_ref.at[0, here, start : start + width], sems.at[slot]
                )
            )
            copies[-1].start()
    for copy in copies[-2:]:
        copy.wait()


def local(queries, keys, values, span_ids, cotangent):
    n = lax.axis_size("ctx")
    far = lax.axis_size("pipe") // 2
    tokens, width = keys.shape[1:]
    spans = span_ids.shape[1]
    heads = queries.shape[2]
    parts = 2 if width % (2 * HD) == 0 else 1
    chunk = heads // parts
    features = cotangent.shape[2] // n
    half = features // 2

    turned = pl.pallas_call(
        functools.partial(turn_kernel, n),
        out_shape=[jax.ShapeDtypeStruct((half, tokens), jnp.bfloat16)] * n,
        in_specs=[VMEM],
        out_specs=[VMEM] * n,
        compiler_params=params(16),
        name="turn",
    )(cotangent)
    packed, place = pl.pallas_call(
        pack_kernel,
        out_shape=[
            jax.ShapeDtypeStruct((1, tokens + TAG, width), jnp.bfloat16),
            jax.ShapeDtypeStruct((tokens, 128), jnp.float32),
        ],
        in_specs=[ANY, SMEM, VMEM],
        out_specs=[VMEM] * 2,
        compiler_params=params(16),
        name="pack",
    )(turned[0], span_ids, keys)
    query_held, value_held = pl.pallas_call(
        fetch_kernel,
        out_shape=[jax.ShapeDtypeStruct(x.shape, jnp.bfloat16) for x in (queries, values)],
        in_specs=[ANY, VMEM, VMEM],
        out_specs=[VMEM] * 2,
        compiler_params=params(16),
        name="fetch",
    )(place, queries, values)
    turned = [turned[0]] + [around(turned[s], s) for s in range(1, n)]
    key_edges, value_edges = ([around(x, way) for way in (1, -1)] for x in (packed, values))
    turned[0] = after(turned[0], *key_edges, *value_edges)
    mine = pl.pallas_call(
        join_kernel,
        out_shape=jax.ShapeDtypeStruct((half, n * tokens), jnp.bfloat16),
        in_specs=[VMEM] * n,
        out_specs=VMEM,
        compiler_params=params(16),
        name="join",
    )(*turned)
    mine_far = swap(mine, "pipe", far)
    key_ring = gather(packed, key_edges, 1, lambda x: after(x, query_held))
    value_ring = gather(values, value_edges, -1, lambda x: after(x, value_held))
    query_held = after(query_held, mine)
    attention, *pieces = pl.pallas_call(
        functools.partial(attention_kernel, HQ // HK, 1.0 / math.sqrt(HD), n, spans),
        out_shape=[jax.ShapeDtypeStruct(queries.shape, jnp.bfloat16)]
        + [jax.ShapeDtypeStruct((1, tokens, chunk), jnp.bfloat16)] * parts,
        in_specs=[VMEM] * (2 + 2 * n),
        out_specs=[VMEM] * (1 + parts),
        compiler_params=params(40),
        name="attend",
    )(place, query_held, *key_ring, value_held, *value_ring[1:])

    near, mirrored = [], []
    for c in range(parts):
        held, sent = [pieces[c]], []
        for s in range(n):
            by_ring = s == n - 1 and c < parts - 1
            sent.append(around(sent[-1], 1) if by_ring else swap(held[s], "pipe", far))
            if s < n - 1:
                arrived = around(held[s], 1)
                held.append(after(arrived, sent[s]) if s < n - 2 else arrived)
        near.append(held)
        mirrored.append(sent)
    cots = [mine, mine_far, swap(mine, "tp", 1), swap(mine_far, "tp", 1)]

    def attended(c, slots):
        return [side[c][s] for side in (near, mirrored) for s in slots]

    first_slots = list(range(n - 1))

    tall = TILE if half % TILE == 0 else half
    totals = [
        pl.pallas_call(
        functools.partial(early_kernel, first_slots),
        out_shape=jax.ShapeDtypeStruct((features, chunk), jnp.float32),
        in_specs=[VMEM] * (2 * n + 2),
        out_specs=VMEM,
        compiler_params=params(40),
        cost_estimate=pl.CostEstimate(
            flops=4 * features * chunk * (n - 1) * tokens,
            bytes_accessed=8 * 2**20,
            transcendentals=0,
        ),
        name="early",
    )(*attended(c, first_slots), *cots)
        for c in range(parts)
    ]
    grad_out = None
    for c in range(parts):
        slots = [n - 1]
        operands = attended(c, slots) + cots + [totals[c]]
        specs = [VMEM] * len(operands)
        aliases = {}
        if grad_out is not None:
            aliases = {len(operands): 0}
            operands.append(grad_out)
            specs.append(ANY)
        grad_out = pl.pallas_call(
            functools.partial(finish_kernel, slots, c * chunk),
            out_shape=jax.ShapeDtypeStruct((1, features, heads), jnp.bfloat16),
            in_specs=specs,
            out_specs=ANY,
            scratch_shapes=[
                pltpu.VMEM((2, tall, chunk), jnp.bfloat16),
                pltpu.SemaphoreType.DMA((2,)),
            ],
            input_output_aliases=aliases,
            compiler_params=params(40),
            cost_estimate=pl.CostEstimate(
                flops=4 * features * chunk * len(slots) * tokens,
                bytes_accessed=8 * 2**20,
                transcendentals=0,
            ),
            name="finish",
        )(*operands)
    return (attention, grad_out)


def solution(mesh):
    placed = (
        P("pipe", "ctx", "tp"),
        P("pipe", "ctx", "tp"),
        P("pipe", "ctx", "tp"),
        P("pipe", "ctx"),
        P("pipe", "ctx", None),
    )
    return jax.shard_map(
        local,
        mesh=mesh,
        in_specs=placed,
        out_specs=(P("pipe", "ctx", "tp"), P("pipe", "ctx", "tp")),
        check_vma=False,
    )
```

```python
import functools
import math

import jax
import jax.numpy as jnp
from jax import lax
from jax.experimental import pallas as pl
from jax.experimental.pallas import tpu as pltpu
from jax.sharding import PartitionSpec as P

HQ = 32
HK = 8
HD = 128
TAG = 16
TILE = 256
VMEM = pl.BlockSpec(memory_space=pltpu.VMEM)
SMEM = pl.BlockSpec(memory_space=pltpu.SMEM)
ANY = pl.BlockSpec(memory_space=pl.ANY)


def ring_order(n):
    return list(range(0, n, 2)) + list(range(1, n, 2))[::-1]


def around(x, shift):
    n = lax.axis_size("ctx")
    order = ring_order(n)
    return lax.ppermute(x, "ctx", [(order[q], order[(q + shift) % n]) for q in range(n)])


def gather(x, edges, ways, gate):
    n = lax.axis_size("ctx")
    middle = n // 2 if ways > 0 else (n - 1) // 2
    held = [x] + [None] * (n - 1)
    held[1], held[-1] = edges
    for s in range(2, middle + 1):
        held[s] = around(gate(held[s - 1]), 1)
    for s in range(2, n - middle):
        held[n - s] = around(gate(held[n - s + 1]), -1)
    return held


def swap(x, axis, mask):
    return lax.ppermute(x, axis, [(i, i ^ mask) for i in range(lax.axis_size(axis))])


def params(mib):
    return pltpu.CompilerParams(vmem_limit_bytes=mib * 2**20)


def after(x, *others):
    return lax.optimization_barrier((x, *others))[0]


def pack_kernel(turned_ref, span_ref, key_ref, packed_ref, place_ref):
    tokens, width = key_ref.shape[1:]
    packed_ref[0, :tokens, :] = key_ref[0]
    spans = span_ref.shape[1]
    span = tokens // spans
    lane = lax.broadcasted_iota(jnp.int32, (TAG, width), 1)
    row = lax.broadcasted_iota(jnp.int32, place_ref.shape, 0)
    ids = jnp.zeros(lane.shape, jnp.float32)
    base = jnp.zeros(row.shape, jnp.int32)
    for j in range(spans):
        ids = jnp.where(lane // span == j, span_ref[0, j].astype(jnp.float32), ids)
        base = jnp.where(row // span == j, span_ref[0, j] * span, base)
    packed_ref[0, tokens:, :] = ids.astype(jnp.bfloat16)
    place_ref[...] = (base + row % span).astype(jnp.float32)


def fetch_kernel(place_ref, query_ref, value_ref, query_held, value_held):
    query_held[...] = query_ref[...]
    value_held[...] = value_ref[...]


def turn_kernel(n, cot_ref, *out_refs):
    me = lax.axis_index("ctx")
    side = lax.axis_index("tp") & 1
    half = cot_ref.shape[2] // n // 2
    place = jnp.where(me % 2 == 0, me // 2, n - 1 - me // 2)
    for s in range(n):
        to = (place + s) % n
        block = jnp.where(to < (n + 1) // 2, 2 * to, 2 * (n - to) - 1)
        at = pl.multiple_of((block * 2 + side) * half, 128)
        out_refs[s][...] = cot_ref[0, :, pl.ds(at, half)].T


def join_kernel(*refs):
    tokens = refs[0].shape[1]
    for s, ref in enumerate(refs[:-1]):
        refs[-1][:, s * tokens : (s + 1) * tokens] = ref[...]


def attention_kernel(group, scale, n, spans, place_ref, query_ref, *refs):
    key_refs, value_refs, (whole_ref, *part_refs) = refs[:n], refs[n : 2 * n], refs[2 * n :]
    tokens, width = value_refs[0].shape[1:]
    heads = width // HD
    span = tokens // spans
    lane = lax.broadcasted_iota(jnp.int32, (1, tokens), 1)
    inner = (lane % span).astype(jnp.float32)
    key_pos = jnp.concatenate(
        [
            ref[0, tokens : tokens + 1, :tokens].astype(jnp.float32) * span + inner
            for ref in key_refs
        ],
        axis=1,
    )
    hidden = jnp.where(key_pos <= place_ref[:, :1], 0.0, -1e30)
    hidden = jnp.concatenate([hidden] * group, axis=0)
    for j in range(heads):
        first = j * group * HD
        out_ref = part_refs[j * len(part_refs) // heads]
        columns = slice(j * HD, (j + 1) * HD)
        key_block = jnp.concatenate([ref[0, :tokens, columns] for ref in key_refs], axis=0)
        value_block = jnp.concatenate([ref[0, :, columns] for ref in value_refs], axis=0)
        queries = jnp.concatenate(
            [query_ref[0, :, first + g * HD : first + (g + 1) * HD] for g in range(group)], axis=0
        )
        scores = lax.dot_general(
            queries, key_block, (((1,), (1,)), ((), ())), preferred_element_type=jnp.float32
        )
        scores = jnp.where(hidden < 0.0, hidden, scores)
        top = jnp.max(scores, axis=1, keepdims=True)
        weights = jnp.exp2((scores - top) * (scale * math.log2(math.e)))
        total = jnp.sum(weights, axis=1, keepdims=True)
        mixed = jnp.dot(
            weights.astype(jnp.bfloat16), value_block, preferred_element_type=jnp.float32
        )
        mixed = (mixed / total).astype(jnp.bfloat16)
        for g in range(group):
            at, piece = first + g * HD, mixed[g * tokens : (g + 1) * tokens]
            whole_ref[0, :, at : at + HD] = piece
            at %= out_ref.shape[2]
            out_ref[0, :, at : at + HD] = piece


def left_sides(refs, tokens, slots):
    near, far, near_other, far_other = refs
    side = lax.axis_index("tp") & 1
    columns = [slice(s * tokens, (s + 1) * tokens) for s in slots]
    return tuple(
        (at, jnp.concatenate([ref[:, here] for ref in pair for here in columns], axis=1))
        for at, pair in ((side, (near, far)), (1 - side, (near_other, far_other)))
    )


def early_kernel(slots, *refs):
    att_refs, cot_refs, total_ref = refs[: 2 * len(slots)], refs[2 * len(slots) : -1], refs[-1]
    half = cot_refs[0].shape[0]
    tokens = att_refs[0].shape[1]
    wide = TILE if total_ref.shape[1] % TILE == 0 else total_ref.shape[1]
    for j in range(total_ref.shape[1] // wide):
        columns = slice(j * wide, (j + 1) * wide)
        rows = jnp.concatenate([ref[0, :, columns] for ref in att_refs], axis=0)
        for at, left in left_sides(cot_refs, tokens, slots):
            total_ref[pl.ds(pl.multiple_of(at * half, half), half), columns] = jnp.dot(
                left, rows, preferred_element_type=jnp.float32
            )


def finish_kernel(slots, start, *refs):
    count = 2 * len(slots)
    att_refs, cot_refs, total_ref = refs[:count], refs[count : count + 4], refs[count + 4]
    out_ref, held, sems = refs[-3:]
    tokens, width = att_refs[0].shape[1:]
    tall = held.shape[1]
    half = cot_refs[0].shape[0]
    rows = jnp.concatenate([ref[0] for ref in att_refs], axis=0)
    copies = []
    for at, left in left_sides(cot_refs, tokens, slots):
        for i in range(half // tall):
            here = pl.ds(pl.multiple_of(at * half + i * tall, tall), tall)
            slot = len(copies)
            held[slot] = (
                total_ref[here, :]
                + jnp.dot(
                    left[i * tall : (i + 1) * tall], rows, preferred_element_type=jnp.float32
                )
            ).astype(jnp.bfloat16)
            copies.append(
                pltpu.make_async_copy(
                    held.at[slot], out_ref.at[0, here, start : start + width], sems.at[slot]
                )
            )
            copies[-1].start()
    for copy in copies:
        copy.wait()


def local(queries, keys, values, span_ids, cotangent):
    n = lax.axis_size("ctx")
    far = lax.axis_size("pipe") // 2
    tokens, width = keys.shape[1:]
    spans = span_ids.shape[1]
    heads = queries.shape[2]
    parts = 2 if width % (2 * HD) == 0 else 1
    chunk = heads // parts
    features = cotangent.shape[2] // n
    half = features // 2

    turned = pl.pallas_call(
        functools.partial(turn_kernel, n),
        out_shape=[jax.ShapeDtypeStruct((half, tokens), jnp.bfloat16)] * n,
        in_specs=[VMEM],
        out_specs=[VMEM] * n,
        compiler_params=params(16),
        name="turn",
    )(cotangent)
    packed, place = pl.pallas_call(
        pack_kernel,
        out_shape=[
            jax.ShapeDtypeStruct((1, tokens + TAG, width), jnp.bfloat16),
            jax.ShapeDtypeStruct((tokens, 128), jnp.float32),
        ],
        in_specs=[ANY, SMEM, VMEM],
        out_specs=[VMEM] * 2,
        compiler_params=params(16),
        name="pack",
    )(turned[0], span_ids, keys)
    query_held, value_held = pl.pallas_call(
        fetch_kernel,
        out_shape=[jax.ShapeDtypeStruct(x.shape, jnp.bfloat16) for x in (queries, values)],
        in_specs=[ANY, VMEM, VMEM],
        out_specs=[VMEM] * 2,
        compiler_params=params(16),
        name="fetch",
    )(place, queries, values)
    turned = [turned[0]] + [around(turned[s], s) for s in range(1, n)]
    key_edges, value_edges = ([around(x, way) for way in (1, -1)] for x in (packed, values))
    turned[0] = after(turned[0], *value_edges)
    mine = pl.pallas_call(
        join_kernel,
        out_shape=jax.ShapeDtypeStruct((half, n * tokens), jnp.bfloat16),
        in_specs=[VMEM] * n,
        out_specs=VMEM,
        compiler_params=params(16),
        name="join",
    )(*turned)
    mine_far = swap(mine, "pipe", far)
    key_ring = gather(packed, key_edges, 1, lambda x: after(x, query_held, mine))
    value_ring = gather(values, value_edges, -1, lambda x: after(x, value_held, mine))
    attention, *pieces = pl.pallas_call(
        functools.partial(attention_kernel, HQ // HK, 1.0 / math.sqrt(HD), n, spans),
        out_shape=[jax.ShapeDtypeStruct(queries.shape, jnp.bfloat16)]
        + [jax.ShapeDtypeStruct((1, tokens, chunk), jnp.bfloat16)] * parts,
        in_specs=[VMEM] * (2 + 2 * n),
        out_specs=[VMEM] * (1 + parts),
        compiler_params=params(40),
        name="attend",
    )(place, query_held, *key_ring, value_held, *value_ring[1:])

    near, mirrored = [], []
    for c in range(parts):
        held, sent = [pieces[c]], []
        for s in range(n):
            by_ring = s == n - 1 and c < parts - 1
            sent.append(around(sent[-1], 1) if by_ring else swap(held[s], "pipe", far))
            if s < n - 1:
                arrived = around(held[s], 1)
                held.append(after(arrived, sent[s]) if s < n - 2 else arrived)
        near.append(held)
        mirrored.append(sent)
    cots = [mine, mine_far, swap(mine, "tp", 1), swap(mine_far, "tp", 1)]

    def attended(c, slots):
        return [side[c][s] for side in (near, mirrored) for s in slots]

    first_slots = list(range(n - 1))

    tall = TILE if half % TILE == 0 else half
    totals = [
        pl.pallas_call(
        functools.partial(early_kernel, first_slots),
        out_shape=jax.ShapeDtypeStruct((features, chunk), jnp.float32),
        in_specs=[VMEM] * (2 * n + 2),
        out_specs=VMEM,
        compiler_params=params(40),
        cost_estimate=pl.CostEstimate(
            flops=4 * features * chunk * (n - 1) * tokens,
            bytes_accessed=8 * 2**20,
            transcendentals=0,
        ),
        name="early",
    )(*attended(c, first_slots), *cots)
        for c in range(parts)
    ]
    grad_out = None
    for c in range(parts):
        slots = [n - 1]
        operands = attended(c, slots) + cots + [totals[c]]
        specs = [VMEM] * len(operands)
        aliases = {}
        if grad_out is not None:
            aliases = {len(operands): 0}
            operands.append(grad_out)
            specs.append(ANY)
        grad_out = pl.pallas_call(
            functools.partial(finish_kernel, slots, c * chunk),
            out_shape=jax.ShapeDtypeStruct((1, features, heads), jnp.bfloat16),
            in_specs=specs,
            out_specs=ANY,
            scratch_shapes=[
                pltpu.VMEM((features // tall, tall, chunk), jnp.bfloat16),
                pltpu.SemaphoreType.DMA((features // tall,)),
            ],
            input_output_aliases=aliases,
            compiler_params=params(40),
            cost_estimate=pl.CostEstimate(
                flops=4 * features * chunk * len(slots) * tokens,
                bytes_accessed=8 * 2**20,
                transcendentals=0,
            ),
            name="finish",
        )(*operands)
    return (attention, grad_out)


def solution(mesh):
    placed = (
        P("pipe", "ctx", "tp"),
        P("pipe", "ctx", "tp"),
        P("pipe", "ctx", "tp"),
        P("pipe", "ctx"),
        P("pipe", "ctx", None),
    )
    return jax.shard_map(
        local,
        mesh=mesh,
        in_specs=placed,
        out_specs=(P("pipe", "ctx", "tp"), P("pipe", "ctx", "tp")),
        check_vma=False,
    )
```

```python
import functools
import math

import jax
import jax.numpy as jnp
from jax import lax
from jax.experimental import pallas as pl
from jax.experimental.pallas import tpu as pltpu
from jax.sharding import PartitionSpec as P

HQ = 32
HK = 8
HD = 128
TAG = 16
TILE = 256
VMEM = pl.BlockSpec(memory_space=pltpu.VMEM)
SMEM = pl.BlockSpec(memory_space=pltpu.SMEM)
ANY = pl.BlockSpec(memory_space=pl.ANY)


def ring_order(n):
    return list(range(0, n, 2)) + list(range(1, n, 2))[::-1]


def around(x, shift):
    n = lax.axis_size("ctx")
    order = ring_order(n)
    return lax.ppermute(x, "ctx", [(order[q], order[(q + shift) % n]) for q in range(n)])


def gather(x, edges, ways, gate):
    n = lax.axis_size("ctx")
    middle = n // 2 if ways > 0 else (n - 1) // 2
    held = [x] + [None] * (n - 1)
    held[1], held[-1] = edges
    for s in range(2, middle + 1):
        held[s] = around(gate(held[s - 1]), 1)
    for s in range(2, n - middle):
        held[n - s] = around(gate(held[n - s + 1]), -1)
    return held


def swap(x, axis, mask):
    return lax.ppermute(x, axis, [(i, i ^ mask) for i in range(lax.axis_size(axis))])


def params(mib):
    return pltpu.CompilerParams(vmem_limit_bytes=mib * 2**20)


def after(x, *others):
    return lax.optimization_barrier((x, *others))[0]


def pack_kernel(turned_ref, span_ref, key_ref, packed_ref, place_ref):
    tokens, width = key_ref.shape[1:]
    packed_ref[0, :tokens, :] = key_ref[0]
    spans = span_ref.shape[1]
    span = tokens // spans
    lane = lax.broadcasted_iota(jnp.int32, (TAG, width), 1)
    row = lax.broadcasted_iota(jnp.int32, place_ref.shape, 0)
    ids = jnp.zeros(lane.shape, jnp.float32)
    base = jnp.zeros(row.shape, jnp.int32)
    for j in range(spans):
        ids = jnp.where(lane // span == j, span_ref[0, j].astype(jnp.float32), ids)
        base = jnp.where(row // span == j, span_ref[0, j] * span, base)
    packed_ref[0, tokens:, :] = ids.astype(jnp.bfloat16)
    place_ref[...] = (base + row % span).astype(jnp.float32)


def fetch_kernel(place_ref, query_ref, value_ref, query_held, value_held):
    query_held[...] = query_ref[...]
    value_held[...] = value_ref[...]


def turn_kernel(n, cot_ref, *out_refs):
    me = lax.axis_index("ctx")
    side = lax.axis_index("tp") & 1
    half = cot_ref.shape[2] // n // 2
    place = jnp.where(me % 2 == 0, me // 2, n - 1 - me // 2)
    for s in range(n):
        to = (place + s) % n
        block = jnp.where(to < (n + 1) // 2, 2 * to, 2 * (n - to) - 1)
        at = pl.multiple_of((block * 2 + side) * half, 128)
        out_refs[s][...] = cot_ref[0, :, pl.ds(at, half)].T


def join_kernel(*refs):
    tokens = refs[0].shape[1]
    for s, ref in enumerate(refs[:-1]):
        refs[-1][:, s * tokens : (s + 1) * tokens] = ref[...]


def attention_kernel(group, scale, n, spans, place_ref, query_ref, *refs):
    key_refs, value_refs, (whole_ref, *part_refs) = refs[:n], refs[n : 2 * n], refs[2 * n :]
    tokens, width = value_refs[0].shape[1:]
    heads = width // HD
    span = tokens // spans
    lane = lax.broadcasted_iota(jnp.int32, (1, tokens), 1)
    inner = (lane % span).astype(jnp.float32)
    key_pos = jnp.concatenate(
        [
            ref[0, tokens : tokens + 1, :tokens].astype(jnp.float32) * span + inner
            for ref in key_refs
        ],
        axis=1,
    )
    hidden = jnp.where(key_pos <= place_ref[:, :1], 0.0, -1e30)
    hidden = jnp.concatenate([hidden] * group, axis=0)
    for j in range(heads):
        first = j * group * HD
        out_ref = part_refs[j * len(part_refs) // heads]
        columns = slice(j * HD, (j + 1) * HD)
        key_block = jnp.concatenate([ref[0, :tokens, columns] for ref in key_refs], axis=0)
        value_block = jnp.concatenate([ref[0, :, columns] for ref in value_refs], axis=0)
        queries = jnp.concatenate(
            [query_ref[0, :, first + g * HD : first + (g + 1) * HD] for g in range(group)], axis=0
        )
        scores = lax.dot_general(
            queries, key_block, (((1,), (1,)), ((), ())), preferred_element_type=jnp.float32
        )
        scores = jnp.where(hidden < 0.0, hidden, scores)
        top = jnp.max(scores, axis=1, keepdims=True)
        weights = jnp.exp2((scores - top) * (scale * math.log2(math.e)))
        total = jnp.sum(weights, axis=1, keepdims=True)
        mixed = jnp.dot(
            weights.astype(jnp.bfloat16), value_block, preferred_element_type=jnp.float32
        )
        mixed = (mixed / total).astype(jnp.bfloat16)
        for g in range(group):
            at, piece = first + g * HD, mixed[g * tokens : (g + 1) * tokens]
            whole_ref[0, :, at : at + HD] = piece
            at %= out_ref.shape[2]
            out_ref[0, :, at : at + HD] = piece


def left_sides(refs, tokens, slots):
    near, far, near_other, far_other = refs
    side = lax.axis_index("tp") & 1
    columns = [slice(s * tokens, (s + 1) * tokens) for s in slots]
    return tuple(
        (at, jnp.concatenate([ref[:, here] for ref in pair for here in columns], axis=1))
        for at, pair in ((side, (near, far)), (1 - side, (near_other, far_other)))
    )


def early_kernel(slots, *refs):
    att_refs, cot_refs, total_ref = refs[: 2 * len(slots)], refs[2 * len(slots) : -1], refs[-1]
    half = cot_refs[0].shape[0]
    tokens = att_refs[0].shape[1]
    wide = TILE if total_ref.shape[1] % TILE == 0 else total_ref.shape[1]
    for j in range(total_ref.shape[1] // wide):
        columns = slice(j * wide, (j + 1) * wide)
        rows = jnp.concatenate([ref[0, :, columns] for ref in att_refs], axis=0)
        for at, left in left_sides(cot_refs, tokens, slots):
            total_ref[pl.ds(pl.multiple_of(at * half, half), half), columns] = jnp.dot(
                left, rows, preferred_element_type=jnp.float32
            )


def finish_kernel(slots, start, *refs):
    count = 2 * len(slots)
    att_refs, cot_refs, total_ref = refs[:count], refs[count : count + 4], refs[count + 4]
    out_ref, held, sems = refs[-3:]
    tokens, width = att_refs[0].shape[1:]
    tall = held.shape[1]
    half = cot_refs[0].shape[0]
    rows = jnp.concatenate([ref[0] for ref in att_refs], axis=0)
    copies = []
    for at, left in left_sides(cot_refs, tokens, slots):
        for i in range(half // tall):
            here = pl.ds(pl.multiple_of(at * half + i * tall, tall), tall)
            slot = len(copies)
            held[slot] = (
                total_ref[here, :]
                + jnp.dot(
                    left[i * tall : (i + 1) * tall], rows, preferred_element_type=jnp.float32
                )
            ).astype(jnp.bfloat16)
            copies.append(
                pltpu.make_async_copy(
                    held.at[slot], out_ref.at[0, here, start : start + width], sems.at[slot]
                )
            )
            copies[-1].start()
    for copy in copies:
        copy.wait()


def local(queries, keys, values, span_ids, cotangent):
    n = lax.axis_size("ctx")
    far = lax.axis_size("pipe") // 2
    tokens, width = keys.shape[1:]
    spans = span_ids.shape[1]
    heads = queries.shape[2]
    parts = 2 if width % (2 * HD) == 0 else 1
    chunk = heads // parts
    features = cotangent.shape[2] // n
    half = features // 2

    turned = pl.pallas_call(
        functools.partial(turn_kernel, n),
        out_shape=[jax.ShapeDtypeStruct((half, tokens), jnp.bfloat16)] * n,
        in_specs=[VMEM],
        out_specs=[VMEM] * n,
        compiler_params=params(16),
        name="turn",
    )(cotangent)
    packed, place = pl.pallas_call(
        pack_kernel,
        out_shape=[
            jax.ShapeDtypeStruct((1, tokens + TAG, width), jnp.bfloat16),
            jax.ShapeDtypeStruct((tokens, 128), jnp.float32),
        ],
        in_specs=[ANY, SMEM, VMEM],
        out_specs=[VMEM] * 2,
        compiler_params=params(16),
        name="pack",
    )(turned[0], span_ids, keys)
    query_held, value_held = pl.pallas_call(
        fetch_kernel,
        out_shape=[jax.ShapeDtypeStruct(x.shape, jnp.bfloat16) for x in (queries, values)],
        in_specs=[ANY, VMEM, VMEM],
        out_specs=[VMEM] * 2,
        compiler_params=params(16),
        name="fetch",
    )(place, queries, values)
    turned = [turned[0]] + [around(turned[s], s) for s in range(1, n)]
    key_edges, value_edges = ([around(x, way) for way in (1, -1)] for x in (packed, values))
    value_ring = gather(values, value_edges, -1, lambda x: after(x, value_held))
    turned[0] = after(turned[0], key_edges[1], *value_ring[1:])
    mine = pl.pallas_call(
        join_kernel,
        out_shape=jax.ShapeDtypeStruct((half, n * tokens), jnp.bfloat16),
        in_specs=[VMEM] * n,
        out_specs=VMEM,
        compiler_params=params(16),
        name="join",
    )(*turned)
    mine_far = swap(mine, "pipe", far)
    key_ring = gather(packed, key_edges, 1, lambda x: after(x, query_held, mine))
    attention, *pieces = pl.pallas_call(
        functools.partial(attention_kernel, HQ // HK, 1.0 / math.sqrt(HD), n, spans),
        out_shape=[jax.ShapeDtypeStruct(queries.shape, jnp.bfloat16)]
        + [jax.ShapeDtypeStruct((1, tokens, chunk), jnp.bfloat16)] * parts,
        in_specs=[VMEM] * (2 + 2 * n),
        out_specs=[VMEM] * (1 + parts),
        compiler_params=params(40),
        name="attend",
    )(place, query_held, *key_ring, value_held, *value_ring[1:])

    near, mirrored = [], []
    for c in range(parts):
        held, sent = [pieces[c]], []
        for s in range(n):
            by_ring = s == n - 1 and c < parts - 1
            sent.append(around(sent[-1], 1) if by_ring else swap(held[s], "pipe", far))
            if s < n - 1:
                arrived = around(held[s], 1)
                held.append(after(arrived, sent[s]) if s < n - 2 else arrived)
        near.append(held)
        mirrored.append(sent)
    cots = [mine, mine_far, swap(mine, "tp", 1), swap(mine_far, "tp", 1)]

    def attended(c, slots):
        return [side[c][s] for side in (near, mirrored) for s in slots]

    first_slots = list(range(n - 1))

    tall = TILE if half % TILE == 0 else half
    totals = [
        pl.pallas_call(
        functools.partial(early_kernel, first_slots),
        out_shape=jax.ShapeDtypeStruct((features, chunk), jnp.float32),
        in_specs=[VMEM] * (2 * n + 2),
        out_specs=VMEM,
        compiler_params=params(40),
        cost_estimate=pl.CostEstimate(
            flops=4 * features * chunk * (n - 1) * tokens,
            bytes_accessed=8 * 2**20,
            transcendentals=0,
        ),
        name="early",
    )(*attended(c, first_slots), *cots)
        for c in range(parts)
    ]
    grad_out = None
    for c in range(parts):
        slots = [n - 1]
        operands = attended(c, slots) + cots + [totals[c]]
        specs = [VMEM] * len(operands)
        aliases = {}
        if grad_out is not None:
            aliases = {len(operands): 0}
            operands.append(grad_out)
            specs.append(ANY)
        grad_out = pl.pallas_call(
            functools.partial(finish_kernel, slots, c * chunk),
            out_shape=jax.ShapeDtypeStruct((1, features, heads), jnp.bfloat16),
            in_specs=specs,
            out_specs=ANY,
            scratch_shapes=[
                pltpu.VMEM((features // tall, tall, chunk), jnp.bfloat16),
                pltpu.SemaphoreType.DMA((features // tall,)),
            ],
            input_output_aliases=aliases,
            compiler_params=params(40),
            cost_estimate=pl.CostEstimate(
                flops=4 * features * chunk * len(slots) * tokens,
                bytes_accessed=8 * 2**20,
                transcendentals=0,
            ),
            name="finish",
        )(*operands)
    return (attention, grad_out)


def solution(mesh):
    placed = (
        P("pipe", "ctx", "tp"),
        P("pipe", "ctx", "tp"),
        P("pipe", "ctx", "tp"),
        P("pipe", "ctx"),
        P("pipe", "ctx", None),
    )
    return jax.shard_map(
        local,
        mesh=mesh,
        in_specs=placed,
        out_specs=(P("pipe", "ctx", "tp"), P("pipe", "ctx", "tp")),
        check_vma=False,
    )
```

```python
import functools
import math

import jax
import jax.numpy as jnp
from jax import lax
from jax.experimental import pallas as pl
from jax.experimental.pallas import tpu as pltpu
from jax.sharding import PartitionSpec as P

HQ = 32
HK = 8
HD = 128
TAG = 16
TILE = 256
VMEM = pl.BlockSpec(memory_space=pltpu.VMEM)
SMEM = pl.BlockSpec(memory_space=pltpu.SMEM)
ANY = pl.BlockSpec(memory_space=pl.ANY)


def ring_order(n):
    return list(range(0, n, 2)) + list(range(1, n, 2))[::-1]


def around(x, shift):
    n = lax.axis_size("ctx")
    order = ring_order(n)
    return lax.ppermute(x, "ctx", [(order[q], order[(q + shift) % n]) for q in range(n)])


def gather(x, edges, ways, gate):
    n = lax.axis_size("ctx")
    middle = n // 2 if ways > 0 else (n - 1) // 2
    held = [x] + [None] * (n - 1)
    held[1], held[-1] = edges
    for s in range(2, middle + 1):
        held[s] = around(gate(held[s - 1]), 1)
    for s in range(2, n - middle):
        held[n - s] = around(gate(held[n - s + 1]), -1)
    return held


def swap(x, axis, mask):
    return lax.ppermute(x, axis, [(i, i ^ mask) for i in range(lax.axis_size(axis))])


def params(mib):
    return pltpu.CompilerParams(vmem_limit_bytes=mib * 2**20)


def after(x, *others):
    return lax.optimization_barrier((x, *others))[0]


def prepare_kernel(n, span_source, key_ref, cot_source, packed_ref, place_ref, *refs):
    out_refs, (span_ref, cot_ref, sems) = refs[:n], refs[n:]
    tokens, width = key_ref.shape[1:]
    copies = [
        pltpu.make_async_copy(cot_source, cot_ref, sems.at[0]),
        pltpu.make_async_copy(key_ref.at[0], packed_ref.at[0, :tokens], sems.at[1]),
        pltpu.make_async_copy(span_source, span_ref, sems.at[2]),
    ]
    for copy in copies:
        copy.start()
    copies[2].wait()
    spans = span_ref.shape[1]
    span = tokens // spans
    lane = lax.broadcasted_iota(jnp.int32, (TAG, width), 1)
    row = lax.broadcasted_iota(jnp.int32, place_ref.shape, 0)
    ids = jnp.zeros(lane.shape, jnp.float32)
    base = jnp.zeros(row.shape, jnp.int32)
    for j in range(spans):
        ids = jnp.where(lane // span == j, span_ref[0, j].astype(jnp.float32), ids)
        base = jnp.where(row // span == j, span_ref[0, j] * span, base)
    packed_ref[0, tokens:, :] = ids.astype(jnp.bfloat16)
    place_ref[...] = (base + row % span).astype(jnp.float32)
    me = lax.axis_index("ctx")
    side = lax.axis_index("tp") & 1
    half = cot_ref.shape[2] // n // 2
    copies[0].wait()
    place = jnp.where(me % 2 == 0, me // 2, n - 1 - me // 2)
    for s in range(n):
        to = (place + s) % n
        block = jnp.where(to < (n + 1) // 2, 2 * to, 2 * (n - to) - 1)
        at = pl.multiple_of((block * 2 + side) * half, 128)
        out_refs[s][...] = cot_ref[0, :, pl.ds(at, half)].T
    copies[1].wait()


def fetch_kernel(*refs):
    half = len(refs) // 2
    for ref, held_ref in zip(refs[:half], refs[half:]):
        held_ref[...] = ref[...]


def join_kernel(*refs):
    tokens = refs[0].shape[1]
    for s, ref in enumerate(refs[:-1]):
        refs[-1][:, s * tokens : (s + 1) * tokens] = ref[...]


def attention_kernel(group, scale, n, spans, place_ref, query_ref, *refs):
    key_refs, value_refs, (whole_ref, *part_refs) = refs[:n], refs[n : 2 * n], refs[2 * n :]
    tokens, width = value_refs[0].shape[1:]
    heads = width // HD
    span = tokens // spans
    lane = lax.broadcasted_iota(jnp.int32, (1, tokens), 1)
    inner = (lane % span).astype(jnp.float32)
    key_pos = jnp.concatenate(
        [
            ref[0, tokens : tokens + 1, :tokens].astype(jnp.float32) * span + inner
            for ref in key_refs
        ],
        axis=1,
    )
    hidden = jnp.where(key_pos <= place_ref[:, :1], 0.0, -1e30)
    hidden = jnp.concatenate([hidden] * group, axis=0)
    for j in range(heads):
        first = j * group * HD
        out_ref = part_refs[j * len(part_refs) // heads]
        columns = slice(j * HD, (j + 1) * HD)
        key_block = jnp.concatenate([ref[0, :tokens, columns] for ref in key_refs], axis=0)
        value_block = jnp.concatenate([ref[0, :, columns] for ref in value_refs], axis=0)
        queries = jnp.concatenate(
            [query_ref[0, :, first + g * HD : first + (g + 1) * HD] for g in range(group)], axis=0
        )
        scores = lax.dot_general(
            queries, key_block, (((1,), (1,)), ((), ())), preferred_element_type=jnp.float32
        )
        scores = jnp.where(hidden < 0.0, hidden, scores)
        top = jnp.max(scores, axis=1, keepdims=True)
        weights = jnp.exp2((scores - top) * (scale * math.log2(math.e)))
        total = jnp.sum(weights, axis=1, keepdims=True)
        mixed = jnp.dot(
            weights.astype(jnp.bfloat16), value_block, preferred_element_type=jnp.float32
        )
        mixed = (mixed / total).astype(jnp.bfloat16)
        for g in range(group):
            at, piece = first + g * HD, mixed[g * tokens : (g + 1) * tokens]
            whole_ref[0, :, at : at + HD] = piece
            at %= out_ref.shape[2]
            out_ref[0, :, at : at + HD] = piece


def left_sides(refs, tokens, slots):
    near, far, near_other, far_other = refs
    side = lax.axis_index("tp") & 1
    columns = [slice(s * tokens, (s + 1) * tokens) for s in slots]
    return tuple(
        (at, jnp.concatenate([ref[:, here] for ref in pair for here in columns], axis=1))
        for at, pair in ((side, (near, far)), (1 - side, (near_other, far_other)))
    )


def early_kernel(slots, *refs):
    att_refs, cot_refs, total_ref = refs[: 2 * len(slots)], refs[2 * len(slots) : -1], refs[-1]
    half = cot_refs[0].shape[0]
    tokens = att_refs[0].shape[1]
    wide = TILE if total_ref.shape[1] % TILE == 0 else total_ref.shape[1]
    for j in range(total_ref.shape[1] // wide):
        columns = slice(j * wide, (j + 1) * wide)
        rows = jnp.concatenate([ref[0, :, columns] for ref in att_refs], axis=0)
        for at, left in left_sides(cot_refs, tokens, slots):
            total_ref[pl.ds(pl.multiple_of(at * half, half), half), columns] = jnp.dot(
                left, rows, preferred_element_type=jnp.float32
            )


def finish_kernel(slots, start, *refs):
    count = 2 * len(slots)
    att_refs, cot_refs, total_ref = refs[:count], refs[count : count + 4], refs[count + 4]
    out_ref, held, sems = refs[-3:]
    tokens, width = att_refs[0].shape[1:]
    tall = held.shape[1]
    half = cot_refs[0].shape[0]
    rows = jnp.concatenate([ref[0] for ref in att_refs], axis=0)
    copies = []
    for at, left in left_sides(cot_refs, tokens, slots):
        for i in range(half // tall):
            here = pl.ds(pl.multiple_of(at * half + i * tall, tall), tall)
            slot = len(copies)
            held[slot] = (
                total_ref[here, :]
                + jnp.dot(
                    left[i * tall : (i + 1) * tall], rows, preferred_element_type=jnp.float32
                )
            ).astype(jnp.bfloat16)
            copies.append(
                pltpu.make_async_copy(
                    held.at[slot], out_ref.at[0, here, start : start + width], sems.at[slot]
                )
            )
            copies[-1].start()
    for copy in copies:
        copy.wait()


def local(queries, keys, values, span_ids, cotangent):
    n = lax.axis_size("ctx")
    far = lax.axis_size("pipe") // 2
    tokens, width = keys.shape[1:]
    spans = span_ids.shape[1]
    heads = queries.shape[2]
    parts = 2 if width % (2 * HD) == 0 else 1
    chunk = heads // parts
    features = cotangent.shape[2] // n
    half = features // 2

    packed, place, *turned = pl.pallas_call(
        functools.partial(prepare_kernel, n),
        out_shape=[
            jax.ShapeDtypeStruct((1, tokens + TAG, width), jnp.bfloat16),
            jax.ShapeDtypeStruct((tokens, 128), jnp.float32),
        ]
        + [jax.ShapeDtypeStruct((half, tokens), jnp.bfloat16)] * n,
        in_specs=[ANY] * 3,
        out_specs=[VMEM] * (n + 2),
        scratch_shapes=[
            pltpu.SMEM(span_ids.shape, jnp.int32),
            pltpu.VMEM(cotangent.shape, jnp.bfloat16),
            pltpu.SemaphoreType.DMA((3,)),
        ],
        compiler_params=params(56),
        name="prepare",
    )(span_ids, keys, cotangent)
    fetched = (place, packed, queries, values, turned[0])
    place, key_held, query_held, value_held, turned[0] = pl.pallas_call(
        fetch_kernel,
        out_shape=[jax.ShapeDtypeStruct(x.shape, x.dtype) for x in fetched],
        in_specs=[VMEM] * 5,
        out_specs=[VMEM] * 5,
        compiler_params=params(16),
        name="fetch",
    )(*fetched)
    turned = [turned[0]] + [around(turned[s], s) for s in range(1, n)]
    key_edges, value_edges = ([around(x, way) for way in (1, -1)] for x in (packed, values))
    turned[0] = after(turned[0], *value_edges)
    mine = pl.pallas_call(
        join_kernel,
        out_shape=jax.ShapeDtypeStruct((half, n * tokens), jnp.bfloat16),
        in_specs=[VMEM] * n,
        out_specs=VMEM,
        compiler_params=params(16),
        name="join",
    )(*turned)
    mine_far = swap(mine, "pipe", far)
    key_ring = gather(packed, key_edges, 1, lambda x: after(x, query_held, mine))
    value_ring = gather(values, value_edges, -1, lambda x: after(x, value_held, mine))
    attention, *pieces = pl.pallas_call(
        functools.partial(attention_kernel, HQ // HK, 1.0 / math.sqrt(HD), n, spans),
        out_shape=[jax.ShapeDtypeStruct(queries.shape, jnp.bfloat16)]
        + [jax.ShapeDtypeStruct((1, tokens, chunk), jnp.bfloat16)] * parts,
        in_specs=[VMEM] * (2 + 2 * n),
        out_specs=[VMEM] * (1 + parts),
        compiler_params=params(40),
        name="attend",
    )(place, query_held, key_held, *key_ring[1:], value_held, *value_ring[1:])

    near, mirrored = [], []
    for c in range(parts):
        held, sent = [pieces[c]], []
        for s in range(n):
            by_ring = s == n - 1 and c < parts - 1
            sent.append(around(sent[-1], 1) if by_ring else swap(held[s], "pipe", far))
            if s < n - 1:
                arrived = around(held[s], 1)
                held.append(after(arrived, sent[s]) if s < n - 2 else arrived)
        near.append(held)
        mirrored.append(sent)
    cots = [mine, mine_far, swap(mine, "tp", 1), swap(mine_far, "tp", 1)]

    def attended(c, slots):
        return [side[c][s] for side in (near, mirrored) for s in slots]

    first_slots = list(range(n - 1))

    tall = TILE if half % TILE == 0 else half
    totals = [
        pl.pallas_call(
        functools.partial(early_kernel, first_slots),
        out_shape=jax.ShapeDtypeStruct((features, chunk), jnp.float32),
        in_specs=[VMEM] * (2 * n + 2),
        out_specs=VMEM,
        compiler_params=params(40),
        cost_estimate=pl.CostEstimate(
            flops=4 * features * chunk * (n - 1) * tokens,
            bytes_accessed=8 * 2**20,
            transcendentals=0,
        ),
        name="early",
    )(*attended(c, first_slots), *cots)
        for c in range(parts)
    ]
    grad_out = None
    for c in range(parts):
        slots = [n - 1]
        operands = attended(c, slots) + cots + [totals[c]]
        specs = [VMEM] * len(operands)
        aliases = {}
        if grad_out is not None:
            aliases = {len(operands): 0}
            operands.append(grad_out)
            specs.append(ANY)
        grad_out = pl.pallas_call(
            functools.partial(finish_kernel, slots, c * chunk),
            out_shape=jax.ShapeDtypeStruct((1, features, heads), jnp.bfloat16),
            in_specs=specs,
            out_specs=ANY,
            scratch_shapes=[
                pltpu.VMEM((features // tall, tall, chunk), jnp.bfloat16),
                pltpu.SemaphoreType.DMA((features // tall,)),
            ],
            input_output_aliases=aliases,
            compiler_params=params(40),
            cost_estimate=pl.CostEstimate(
                flops=4 * features * chunk * len(slots) * tokens,
                bytes_accessed=8 * 2**20,
                transcendentals=0,
            ),
            name="finish",
        )(*operands)
    return (attention, grad_out)


def solution(mesh):
    placed = (
        P("pipe", "ctx", "tp"),
        P("pipe", "ctx", "tp"),
        P("pipe", "ctx", "tp"),
        P("pipe", "ctx"),
        P("pipe", "ctx", None),
    )
    return jax.shard_map(
        local,
        mesh=mesh,
        in_specs=placed,
        out_specs=(P("pipe", "ctx", "tp"), P("pipe", "ctx", "tp")),
        check_vma=False,
    )
```

```python
import functools
import math

import jax
import jax.numpy as jnp
from jax import lax
from jax.experimental import pallas as pl
from jax.experimental.pallas import tpu as pltpu
from jax.sharding import PartitionSpec as P

HQ = 32
HK = 8
HD = 128
TAG = 16
TILE = 256
VMEM = pl.BlockSpec(memory_space=pltpu.VMEM)
SMEM = pl.BlockSpec(memory_space=pltpu.SMEM)
ANY = pl.BlockSpec(memory_space=pl.ANY)


def ring_order(n):
    return list(range(0, n, 2)) + list(range(1, n, 2))[::-1]


def around(x, shift):
    n = lax.axis_size("ctx")
    order = ring_order(n)
    return lax.ppermute(x, "ctx", [(order[q], order[(q + shift) % n]) for q in range(n)])


def gather(x, edges, ways, gate):
    n = lax.axis_size("ctx")
    middle = n // 2 if ways > 0 else (n - 1) // 2
    held = [x] + [None] * (n - 1)
    held[1], held[-1] = edges
    for s in range(2, middle + 1):
        held[s] = around(gate(held[s - 1]), 1)
    for s in range(2, n - middle):
        held[n - s] = around(gate(held[n - s + 1]), -1)
    return held


def swap(x, axis, mask):
    return lax.ppermute(x, axis, [(i, i ^ mask) for i in range(lax.axis_size(axis))])


def params(mib):
    return pltpu.CompilerParams(vmem_limit_bytes=mib * 2**20)


def after(x, *others):
    return lax.optimization_barrier((x, *others))[0]


def prepare_kernel(n, span_source, key_ref, cot_source, packed_ref, place_ref, *refs):
    out_refs, (span_ref, cot_ref, sems) = refs[:n], refs[n:]
    tokens, width = key_ref.shape[1:]
    copies = [
        pltpu.make_async_copy(cot_source, cot_ref, sems.at[0]),
        pltpu.make_async_copy(key_ref.at[0], packed_ref.at[0, :tokens], sems.at[1]),
        pltpu.make_async_copy(span_source, span_ref, sems.at[2]),
    ]
    for copy in copies:
        copy.start()
    copies[2].wait()
    spans = span_ref.shape[1]
    span = tokens // spans
    lane = lax.broadcasted_iota(jnp.int32, (TAG, width), 1)
    row = lax.broadcasted_iota(jnp.int32, place_ref.shape, 0)
    ids = jnp.zeros(lane.shape, jnp.float32)
    base = jnp.zeros(row.shape, jnp.int32)
    for j in range(spans):
        ids = jnp.where(lane // span == j, span_ref[0, j].astype(jnp.float32), ids)
        base = jnp.where(row // span == j, span_ref[0, j] * span, base)
    packed_ref[0, tokens:, :] = ids.astype(jnp.bfloat16)
    place_ref[...] = (base + row % span).astype(jnp.float32)
    me = lax.axis_index("ctx")
    side = lax.axis_index("tp") & 1
    half = cot_ref.shape[2] // n // 2
    copies[0].wait()
    place = jnp.where(me % 2 == 0, me // 2, n - 1 - me // 2)
    for s in range(n):
        to = (place + s) % n
        block = jnp.where(to < (n + 1) // 2, 2 * to, 2 * (n - to) - 1)
        at = pl.multiple_of((block * 2 + side) * half, 128)
        out_refs[s][...] = cot_ref[0, :, pl.ds(at, half)].T
    copies[1].wait()


def fetch_kernel(*refs):
    half = len(refs) // 2
    for ref, held_ref in zip(refs[:half], refs[half:]):
        held_ref[...] = ref[...]


def join_kernel(*refs):
    tokens = refs[0].shape[1]
    for s, ref in enumerate(refs[:-1]):
        refs[-1][:, s * tokens : (s + 1) * tokens] = ref[...]


def attention_kernel(group, scale, n, spans, place_ref, query_ref, *refs):
    key_refs, value_refs, (whole_ref, *part_refs) = refs[:n], refs[n : 2 * n], refs[2 * n :]
    tokens, width = value_refs[0].shape[1:]
    heads = width // HD
    span = tokens // spans
    lane = lax.broadcasted_iota(jnp.int32, (1, tokens), 1)
    inner = (lane % span).astype(jnp.float32)
    key_pos = jnp.concatenate(
        [
            ref[0, tokens : tokens + 1, :tokens].astype(jnp.float32) * span + inner
            for ref in key_refs
        ],
        axis=1,
    )
    hidden = jnp.where(key_pos <= place_ref[:, :1], 0.0, -1e30)
    hidden = jnp.concatenate([hidden] * group, axis=0)
    for j in range(heads):
        first = j * group * HD
        out_ref = part_refs[j * len(part_refs) // heads]
        columns = slice(j * HD, (j + 1) * HD)
        key_block = jnp.concatenate([ref[0, :tokens, columns] for ref in key_refs], axis=0)
        value_block = jnp.concatenate([ref[0, :, columns] for ref in value_refs], axis=0)
        queries = jnp.concatenate(
            [query_ref[0, :, first + g * HD : first + (g + 1) * HD] for g in range(group)], axis=0
        )
        scores = lax.dot_general(
            queries, key_block, (((1,), (1,)), ((), ())), preferred_element_type=jnp.float32
        )
        scores = jnp.where(hidden < 0.0, hidden, scores)
        top = jnp.max(scores, axis=1, keepdims=True)
        weights = jnp.exp2((scores - top) * (scale * math.log2(math.e)))
        total = jnp.sum(weights, axis=1, keepdims=True)
        mixed = jnp.dot(
            weights.astype(jnp.bfloat16), value_block, preferred_element_type=jnp.float32
        )
        mixed = (mixed / total).astype(jnp.bfloat16)
        for g in range(group):
            at, piece = first + g * HD, mixed[g * tokens : (g + 1) * tokens]
            whole_ref[0, :, at : at + HD] = piece
            at %= out_ref.shape[2]
            out_ref[0, :, at : at + HD] = piece


def left_sides(refs, tokens, slots):
    near, far, near_other, far_other = refs
    side = lax.axis_index("tp") & 1
    columns = [slice(s * tokens, (s + 1) * tokens) for s in slots]
    return tuple(
        (at, jnp.concatenate([ref[:, here] for ref in pair for here in columns], axis=1))
        for at, pair in ((side, (near, far)), (1 - side, (near_other, far_other)))
    )


def early_kernel(slots, *refs):
    att_refs, cot_refs, total_ref = refs[: 2 * len(slots)], refs[2 * len(slots) : -1], refs[-1]
    half = cot_refs[0].shape[0]
    tokens = att_refs[0].shape[1]
    wide = TILE if total_ref.shape[1] % TILE == 0 else total_ref.shape[1]
    for j in range(total_ref.shape[1] // wide):
        columns = slice(j * wide, (j + 1) * wide)
        rows = jnp.concatenate([ref[0, :, columns] for ref in att_refs], axis=0)
        for at, left in left_sides(cot_refs, tokens, slots):
            total_ref[pl.ds(pl.multiple_of(at * half, half), half), columns] = jnp.dot(
                left, rows, preferred_element_type=jnp.float32
            )


def finish_kernel(slots, start, *refs):
    count = 2 * len(slots)
    att_refs, cot_refs, total_ref = refs[:count], refs[count : count + 4], refs[count + 4]
    out_ref, held, sems = refs[-3:]
    tokens, width = att_refs[0].shape[1:]
    tall = held.shape[1]
    half = cot_refs[0].shape[0]
    rows = jnp.concatenate([ref[0] for ref in att_refs], axis=0)
    copies = []
    for at, left in left_sides(cot_refs, tokens, slots):
        for i in range(half // tall):
            here = pl.ds(pl.multiple_of(at * half + i * tall, tall), tall)
            slot = len(copies)
            held[slot] = (
                total_ref[here, :]
                + jnp.dot(
                    left[i * tall : (i + 1) * tall], rows, preferred_element_type=jnp.float32
                )
            ).astype(jnp.bfloat16)
            copies.append(
                pltpu.make_async_copy(
                    held.at[slot], out_ref.at[0, here, start : start + width], sems.at[slot]
                )
            )
            copies[-1].start()
    for copy in copies:
        copy.wait()


def local(queries, keys, values, span_ids, cotangent):
    n = lax.axis_size("ctx")
    far = lax.axis_size("pipe") // 2
    tokens, width = keys.shape[1:]
    spans = span_ids.shape[1]
    heads = queries.shape[2]
    parts = 2 if width % (2 * HD) == 0 else 1
    chunk = heads // parts
    features = cotangent.shape[2] // n
    half = features // 2

    packed, place, *turned = pl.pallas_call(
        functools.partial(prepare_kernel, n),
        out_shape=[
            jax.ShapeDtypeStruct((1, tokens + TAG, width), jnp.bfloat16),
            jax.ShapeDtypeStruct((tokens, 128), jnp.float32),
        ]
        + [jax.ShapeDtypeStruct((half, tokens), jnp.bfloat16)] * n,
        in_specs=[ANY] * 3,
        out_specs=[VMEM] * (n + 2),
        scratch_shapes=[
            pltpu.SMEM(span_ids.shape, jnp.int32),
            pltpu.VMEM(cotangent.shape, jnp.bfloat16),
            pltpu.SemaphoreType.DMA((3,)),
        ],
        compiler_params=params(56),
        name="prepare",
    )(span_ids, keys, cotangent)
    fetched = (place, packed, queries, values, turned[0])
    place, key_held, query_held, value_held, turned[0] = pl.pallas_call(
        fetch_kernel,
        out_shape=[jax.ShapeDtypeStruct(x.shape, x.dtype) for x in fetched],
        in_specs=[VMEM] * 5,
        out_specs=[VMEM] * 5,
        compiler_params=params(16),
        name="fetch",
    )(*fetched)
    turned = [turned[0]] + [around(turned[s], s) for s in range(1, n)]
    key_edges, value_edges = ([around(x, way) for way in (1, -1)] for x in (packed, values))
    turned[0] = after(turned[0], *value_edges, key_edges[1])
    mine = pl.pallas_call(
        join_kernel,
        out_shape=jax.ShapeDtypeStruct((half, n * tokens), jnp.bfloat16),
        in_specs=[VMEM] * n,
        out_specs=VMEM,
        compiler_params=params(16),
        name="join",
    )(*turned)
    mine_far = swap(mine, "pipe", far)
    key_ring = gather(packed, key_edges, 1, lambda x: after(x, query_held, mine))
    value_ring = gather(values, value_edges, -1, lambda x: after(x, value_held, mine))
    attention, *pieces = pl.pallas_call(
        functools.partial(attention_kernel, HQ // HK, 1.0 / math.sqrt(HD), n, spans),
        out_shape=[jax.ShapeDtypeStruct(queries.shape, jnp.bfloat16)]
        + [jax.ShapeDtypeStruct((1, tokens, chunk), jnp.bfloat16)] * parts,
        in_specs=[VMEM] * (2 + 2 * n),
        out_specs=[VMEM] * (1 + parts),
        compiler_params=params(40),
        name="attend",
    )(place, query_held, key_held, *key_ring[1:], value_held, *value_ring[1:])

    near, mirrored = [], []
    for c in range(parts):
        held, sent = [pieces[c]], []
        for s in range(n):
            by_ring = s == n - 1 and c < parts - 1
            sent.append(around(sent[-1], 1) if by_ring else swap(held[s], "pipe", far))
            if s < n - 1:
                arrived = around(held[s], 1)
                held.append(after(arrived, sent[s]) if s < n - 2 else arrived)
        near.append(held)
        mirrored.append(sent)
    cots = [mine, mine_far, swap(mine, "tp", 1), swap(mine_far, "tp", 1)]

    def attended(c, slots):
        return [side[c][s] for side in (near, mirrored) for s in slots]

    first_slots = list(range(n - 1))

    tall = TILE if half % TILE == 0 else half
    totals = [
        pl.pallas_call(
        functools.partial(early_kernel, first_slots),
        out_shape=jax.ShapeDtypeStruct((features, chunk), jnp.float32),
        in_specs=[VMEM] * (2 * n + 2),
        out_specs=VMEM,
        compiler_params=params(40),
        cost_estimate=pl.CostEstimate(
            flops=4 * features * chunk * (n - 1) * tokens,
            bytes_accessed=8 * 2**20,
            transcendentals=0,
        ),
        name="early",
    )(*attended(c, first_slots), *cots)
        for c in range(parts)
    ]
    grad_out = None
    for c in range(parts):
        slots = [n - 1]
        operands = attended(c, slots) + cots + [totals[c]]
        specs = [VMEM] * len(operands)
        aliases = {}
        if grad_out is not None:
            aliases = {len(operands): 0}
            operands.append(grad_out)
            specs.append(ANY)
        grad_out = pl.pallas_call(
            functools.partial(finish_kernel, slots, c * chunk),
            out_shape=jax.ShapeDtypeStruct((1, features, heads), jnp.bfloat16),
            in_specs=specs,
            out_specs=ANY,
            scratch_shapes=[
                pltpu.VMEM((features // tall, tall, chunk), jnp.bfloat16),
                pltpu.SemaphoreType.DMA((features // tall,)),
            ],
            input_output_aliases=aliases,
            compiler_params=params(40),
            cost_estimate=pl.CostEstimate(
                flops=4 * features * chunk * len(slots) * tokens,
                bytes_accessed=8 * 2**20,
                transcendentals=0,
            ),
            name="finish",
        )(*operands)
    return (attention, grad_out)


def solution(mesh):
    placed = (
        P("pipe", "ctx", "tp"),
        P("pipe", "ctx", "tp"),
        P("pipe", "ctx", "tp"),
        P("pipe", "ctx"),
        P("pipe", "ctx", None),
    )
    return jax.shard_map(
        local,
        mesh=mesh,
        in_specs=placed,
        out_specs=(P("pipe", "ctx", "tp"), P("pipe", "ctx", "tp")),
        check_vma=False,
    )
```

```python
import functools
import math

import jax
import jax.numpy as jnp
from jax import lax
from jax.experimental import pallas as pl
from jax.experimental.pallas import tpu as pltpu
from jax.sharding import PartitionSpec as P

HQ = 32
HK = 8
HD = 128
TAG = 16
TILE = 256
VMEM = pl.BlockSpec(memory_space=pltpu.VMEM)
SMEM = pl.BlockSpec(memory_space=pltpu.SMEM)
ANY = pl.BlockSpec(memory_space=pl.ANY)


def ring_order(n):
    return list(range(0, n, 2)) + list(range(1, n, 2))[::-1]


def around(x, shift):
    n = lax.axis_size("ctx")
    order = ring_order(n)
    return lax.ppermute(x, "ctx", [(order[q], order[(q + shift) % n]) for q in range(n)])


def gather(x, edges, ways, gate):
    n = lax.axis_size("ctx")
    middle = n // 2 if ways > 0 else (n - 1) // 2
    held = [x] + [None] * (n - 1)
    held[1], held[-1] = edges
    for s in range(2, middle + 1):
        held[s] = around(gate(held[s - 1]), 1)
    for s in range(2, n - middle):
        held[n - s] = around(gate(held[n - s + 1]), -1)
    return held


def swap(x, axis, mask):
    return lax.ppermute(x, axis, [(i, i ^ mask) for i in range(lax.axis_size(axis))])


def params(mib):
    return pltpu.CompilerParams(vmem_limit_bytes=mib * 2**20)


def after(x, *others):
    return lax.optimization_barrier((x, *others))[0]


def prepare_kernel(n, span_source, key_ref, cot_source, packed_ref, place_ref, *refs):
    out_refs, (span_ref, cot_ref, sems) = refs[:n], refs[n:]
    tokens, width = key_ref.shape[1:]
    copies = [
        pltpu.make_async_copy(cot_source, cot_ref, sems.at[0]),
        pltpu.make_async_copy(key_ref.at[0], packed_ref.at[0, :tokens], sems.at[1]),
        pltpu.make_async_copy(span_source, span_ref, sems.at[2]),
    ]
    for copy in copies:
        copy.start()
    copies[2].wait()
    spans = span_ref.shape[1]
    span = tokens // spans
    lane = lax.broadcasted_iota(jnp.int32, (TAG, width), 1)
    row = lax.broadcasted_iota(jnp.int32, place_ref.shape, 0)
    ids = jnp.zeros(lane.shape, jnp.float32)
    base = jnp.zeros(row.shape, jnp.int32)
    for j in range(spans):
        ids = jnp.where(lane // span == j, span_ref[0, j].astype(jnp.float32), ids)
        base = jnp.where(row // span == j, span_ref[0, j] * span, base)
    packed_ref[0, tokens:, :] = ids.astype(jnp.bfloat16)
    place_ref[...] = (base + row % span).astype(jnp.float32)
    me = lax.axis_index("ctx")
    side = lax.axis_index("tp") & 1
    half = cot_ref.shape[2] // n // 2
    copies[0].wait()
    place = jnp.where(me % 2 == 0, me // 2, n - 1 - me // 2)
    for s in range(n):
        to = (place + s) % n
        block = jnp.where(to < (n + 1) // 2, 2 * to, 2 * (n - to) - 1)
        at = pl.multiple_of((block * 2 + side) * half, 128)
        out_refs[s][...] = cot_ref[0, :, pl.ds(at, half)].T
    copies[1].wait()


def fetch_kernel(*refs):
    half = len(refs) // 2
    for ref, held_ref in zip(refs[:half], refs[half:]):
        held_ref[...] = ref[...]


def join_kernel(*refs):
    tokens = refs[0].shape[1]
    for s, ref in enumerate(refs[:-1]):
        refs[-1][:, s * tokens : (s + 1) * tokens] = ref[...]


def attention_kernel(group, scale, n, spans, place_ref, query_ref, *refs):
    key_refs, value_refs, (whole_ref, *part_refs) = refs[:n], refs[n : 2 * n], refs[2 * n :]
    tokens, width = value_refs[0].shape[1:]
    heads = width // HD
    span = tokens // spans
    lane = lax.broadcasted_iota(jnp.int32, (1, tokens), 1)
    inner = (lane % span).astype(jnp.float32)
    key_pos = jnp.concatenate(
        [
            ref[0, tokens : tokens + 1, :tokens].astype(jnp.float32) * span + inner
            for ref in key_refs
        ],
        axis=1,
    )
    hidden = jnp.where(key_pos <= place_ref[:, :1], 0.0, -1e30)
    hidden = jnp.concatenate([hidden] * group, axis=0)
    for j in range(heads):
        first = j * group * HD
        out_ref = part_refs[j * len(part_refs) // heads]
        columns = slice(j * HD, (j + 1) * HD)
        key_block = jnp.concatenate([ref[0, :tokens, columns] for ref in key_refs], axis=0)
        value_block = jnp.concatenate([ref[0, :, columns] for ref in value_refs], axis=0)
        queries = jnp.concatenate(
            [query_ref[0, :, first + g * HD : first + (g + 1) * HD] for g in range(group)], axis=0
        )
        scores = lax.dot_general(
            queries, key_block, (((1,), (1,)), ((), ())), preferred_element_type=jnp.float32
        )
        scores = jnp.where(hidden < 0.0, hidden, scores)
        top = jnp.max(scores, axis=1, keepdims=True)
        weights = jnp.exp2((scores - top) * (scale * math.log2(math.e)))
        total = jnp.sum(weights, axis=1, keepdims=True)
        mixed = jnp.dot(
            weights.astype(jnp.bfloat16), value_block, preferred_element_type=jnp.float32
        )
        mixed = (mixed / total).astype(jnp.bfloat16)
        for g in range(group):
            at, piece = first + g * HD, mixed[g * tokens : (g + 1) * tokens]
            whole_ref[0, :, at : at + HD] = piece
            at %= out_ref.shape[2]
            out_ref[0, :, at : at + HD] = piece


def left_sides(refs, tokens, slots):
    near, far, near_other, far_other = refs
    side = lax.axis_index("tp") & 1
    columns = [slice(s * tokens, (s + 1) * tokens) for s in slots]
    return tuple(
        (at, jnp.concatenate([ref[:, here] for ref in pair for here in columns], axis=1))
        for at, pair in ((side, (near, far)), (1 - side, (near_other, far_other)))
    )


def early_kernel(slots, *refs):
    att_refs, cot_refs, total_ref = refs[: 2 * len(slots)], refs[2 * len(slots) : -1], refs[-1]
    half = cot_refs[0].shape[0]
    tokens = att_refs[0].shape[1]
    wide = TILE if total_ref.shape[1] % TILE == 0 else total_ref.shape[1]
    for j in range(total_ref.shape[1] // wide):
        columns = slice(j * wide, (j + 1) * wide)
        rows = jnp.concatenate([ref[0, :, columns] for ref in att_refs], axis=0)
        for at, left in left_sides(cot_refs, tokens, slots):
            total_ref[pl.ds(pl.multiple_of(at * half, half), half), columns] = jnp.dot(
                left, rows, preferred_element_type=jnp.float32
            )


def finish_kernel(slots, start, *refs):
    count = 2 * len(slots)
    att_refs, cot_refs, total_ref = refs[:count], refs[count : count + 4], refs[count + 4]
    out_ref, held, sems = refs[-3:]
    tokens, width = att_refs[0].shape[1:]
    tall = held.shape[1]
    half = cot_refs[0].shape[0]
    rows = jnp.concatenate([ref[0] for ref in att_refs], axis=0)
    copies = []
    for at, left in left_sides(cot_refs, tokens, slots):
        for i in range(half // tall):
            here = pl.ds(pl.multiple_of(at * half + i * tall, tall), tall)
            slot = len(copies)
            held[slot] = (
                total_ref[here, :]
                + jnp.dot(
                    left[i * tall : (i + 1) * tall], rows, preferred_element_type=jnp.float32
                )
            ).astype(jnp.bfloat16)
            copies.append(
                pltpu.make_async_copy(
                    held.at[slot], out_ref.at[0, here, start : start + width], sems.at[slot]
                )
            )
            copies[-1].start()
    for copy in copies:
        copy.wait()


def local(queries, keys, values, span_ids, cotangent):
    n = lax.axis_size("ctx")
    far = lax.axis_size("pipe") // 2
    tokens, width = keys.shape[1:]
    spans = span_ids.shape[1]
    heads = queries.shape[2]
    parts = 2 if width % (2 * HD) == 0 else 1
    chunk = heads // parts
    features = cotangent.shape[2] // n
    half = features // 2

    packed, place, *turned = pl.pallas_call(
        functools.partial(prepare_kernel, n),
        out_shape=[
            jax.ShapeDtypeStruct((1, tokens + TAG, width), jnp.bfloat16),
            jax.ShapeDtypeStruct((tokens, 128), jnp.float32),
        ]
        + [jax.ShapeDtypeStruct((half, tokens), jnp.bfloat16)] * n,
        in_specs=[ANY] * 3,
        out_specs=[VMEM] * (n + 2),
        scratch_shapes=[
            pltpu.SMEM(span_ids.shape, jnp.int32),
            pltpu.VMEM(cotangent.shape, jnp.bfloat16),
            pltpu.SemaphoreType.DMA((3,)),
        ],
        compiler_params=params(56),
        name="prepare",
    )(span_ids, keys, cotangent)
    fetched = (place, packed, queries, values, turned[0])
    place, key_held, query_held, value_held, turned[0] = pl.pallas_call(
        fetch_kernel,
        out_shape=[jax.ShapeDtypeStruct(x.shape, x.dtype) for x in fetched],
        in_specs=[VMEM] * 5,
        out_specs=[VMEM] * 5,
        compiler_params=params(16),
        name="fetch",
    )(*fetched)
    turned = [turned[0]] + [around(turned[s], s) for s in range(1, n)]
    value_edges = [around(values, way) for way in (1, -1)]
    key_edges = [around(after(packed, *value_edges), way) for way in (1, -1)]
    mine = pl.pallas_call(
        join_kernel,
        out_shape=jax.ShapeDtypeStruct((half, n * tokens), jnp.bfloat16),
        in_specs=[VMEM] * n,
        out_specs=VMEM,
        compiler_params=params(16),
        name="join",
    )(*turned)
    mine_far = swap(mine, "pipe", far)
    key_ring = gather(packed, key_edges, 1, lambda x: after(x, query_held, mine))
    value_ring = gather(values, value_edges, -1, lambda x: after(x, value_held, mine))
    attention, *pieces = pl.pallas_call(
        functools.partial(attention_kernel, HQ // HK, 1.0 / math.sqrt(HD), n, spans),
        out_shape=[jax.ShapeDtypeStruct(queries.shape, jnp.bfloat16)]
        + [jax.ShapeDtypeStruct((1, tokens, chunk), jnp.bfloat16)] * parts,
        in_specs=[VMEM] * (2 + 2 * n),
        out_specs=[VMEM] * (1 + parts),
        compiler_params=params(40),
        name="attend",
    )(place, query_held, key_held, *key_ring[1:], value_held, *value_ring[1:])

    near, mirrored = [], []
    for c in range(parts):
        held, sent = [pieces[c]], []
        for s in range(n):
            by_ring = s == n - 1 and c < parts - 1
            sent.append(around(sent[-1], 1) if by_ring else swap(held[s], "pipe", far))
            if s < n - 1:
                arrived = around(held[s], 1)
                held.append(after(arrived, sent[s]) if s < n - 2 else arrived)
        near.append(held)
        mirrored.append(sent)
    cots = [mine, mine_far, swap(mine, "tp", 1), swap(mine_far, "tp", 1)]

    def attended(c, slots):
        return [side[c][s] for side in (near, mirrored) for s in slots]

    first_slots = list(range(n - 1))

    tall = TILE if half % TILE == 0 else half
    totals = [
        pl.pallas_call(
        functools.partial(early_kernel, first_slots),
        out_shape=jax.ShapeDtypeStruct((features, chunk), jnp.float32),
        in_specs=[VMEM] * (2 * n + 2),
        out_specs=VMEM,
        compiler_params=params(40),
        cost_estimate=pl.CostEstimate(
            flops=4 * features * chunk * (n - 1) * tokens,
            bytes_accessed=8 * 2**20,
            transcendentals=0,
        ),
        name="early",
    )(*attended(c, first_slots), *cots)
        for c in range(parts)
    ]
    grad_out = None
    for c in range(parts):
        slots = [n - 1]
        operands = attended(c, slots) + cots + [totals[c]]
        specs = [VMEM] * len(operands)
        aliases = {}
        if grad_out is not None:
            aliases = {len(operands): 0}
            operands.append(grad_out)
            specs.append(ANY)
        grad_out = pl.pallas_call(
            functools.partial(finish_kernel, slots, c * chunk),
            out_shape=jax.ShapeDtypeStruct((1, features, heads), jnp.bfloat16),
            in_specs=specs,
            out_specs=ANY,
            scratch_shapes=[
                pltpu.VMEM((features // tall, tall, chunk), jnp.bfloat16),
                pltpu.SemaphoreType.DMA((features // tall,)),
            ],
            input_output_aliases=aliases,
            compiler_params=params(40),
            cost_estimate=pl.CostEstimate(
                flops=4 * features * chunk * len(slots) * tokens,
                bytes_accessed=8 * 2**20,
                transcendentals=0,
            ),
            name="finish",
        )(*operands)
    return (attention, grad_out)


def solution(mesh):
    placed = (
        P("pipe", "ctx", "tp"),
        P("pipe", "ctx", "tp"),
        P("pipe", "ctx", "tp"),
        P("pipe", "ctx"),
        P("pipe", "ctx", None),
    )
    return jax.shard_map(
        local,
        mesh=mesh,
        in_specs=placed,
        out_specs=(P("pipe", "ctx", "tp"), P("pipe", "ctx", "tp")),
        check_vma=False,
    )
```

```python
import functools
import math

import jax
import jax.numpy as jnp
from jax import lax
from jax.experimental import pallas as pl
from jax.experimental.pallas import tpu as pltpu
from jax.sharding import PartitionSpec as P

HQ = 32
HK = 8
HD = 128
TAG = 16
TILE = 256
VMEM = pl.BlockSpec(memory_space=pltpu.VMEM)
SMEM = pl.BlockSpec(memory_space=pltpu.SMEM)
ANY = pl.BlockSpec(memory_space=pl.ANY)


def ring_order(n):
    return list(range(0, n, 2)) + list(range(1, n, 2))[::-1]


def around(x, shift):
    n = lax.axis_size("ctx")
    order = ring_order(n)
    return lax.ppermute(x, "ctx", [(order[q], order[(q + shift) % n]) for q in range(n)])


def gather(x, edges, ways, gate):
    n = lax.axis_size("ctx")
    middle = n // 2 if ways > 0 else (n - 1) // 2
    held = [x] + [None] * (n - 1)
    held[1], held[-1] = edges
    for s in range(2, middle + 1):
        held[s] = around(gate(held[s - 1]), 1)
    for s in range(2, n - middle):
        held[n - s] = around(gate(held[n - s + 1]), -1)
    return held


def swap(x, axis, mask):
    return lax.ppermute(x, axis, [(i, i ^ mask) for i in range(lax.axis_size(axis))])


def params(mib):
    return pltpu.CompilerParams(vmem_limit_bytes=mib * 2**20)


def after(x, *others):
    return lax.optimization_barrier((x, *others))[0]


def prepare_kernel(n, span_source, key_ref, cot_source, packed_ref, place_ref, *refs):
    out_refs, (span_ref, cot_ref, sems) = refs[:n], refs[n:]
    tokens, width = key_ref.shape[1:]
    copies = [
        pltpu.make_async_copy(cot_source, cot_ref, sems.at[0]),
        pltpu.make_async_copy(key_ref.at[0], packed_ref.at[0, :tokens], sems.at[1]),
        pltpu.make_async_copy(span_source, span_ref, sems.at[2]),
    ]
    for copy in copies:
        copy.start()
    copies[2].wait()
    spans = span_ref.shape[1]
    span = tokens // spans
    lane = lax.broadcasted_iota(jnp.int32, (TAG, width), 1)
    row = lax.broadcasted_iota(jnp.int32, place_ref.shape, 0)
    ids = jnp.zeros(lane.shape, jnp.float32)
    base = jnp.zeros(row.shape, jnp.int32)
    for j in range(spans):
        ids = jnp.where(lane // span == j, span_ref[0, j].astype(jnp.float32), ids)
        base = jnp.where(row // span == j, span_ref[0, j] * span, base)
    packed_ref[0, tokens:, :] = ids.astype(jnp.bfloat16)
    place_ref[...] = (base + row % span).astype(jnp.float32)
    me = lax.axis_index("ctx")
    side = lax.axis_index("tp") & 1
    half = cot_ref.shape[2] // n // 2
    copies[0].wait()
    place = jnp.where(me % 2 == 0, me // 2, n - 1 - me // 2)
    for s in range(n):
        to = (place + s) % n
        block = jnp.where(to < (n + 1) // 2, 2 * to, 2 * (n - to) - 1)
        at = pl.multiple_of((block * 2 + side) * half, 128)
        out_refs[s][...] = cot_ref[0, :, pl.ds(at, half)].T
    copies[1].wait()


def fetch_kernel(*refs):
    half = len(refs) // 2
    for ref, held_ref in zip(refs[:half], refs[half:]):
        held_ref[...] = ref[...]


def join_kernel(*refs):
    tokens = refs[0].shape[1]
    for s, ref in enumerate(refs[:-1]):
        refs[-1][:, s * tokens : (s + 1) * tokens] = ref[...]


def attention_kernel(group, scale, n, spans, first_head, place_ref, query_ref, *refs):
    key_refs, value_refs, out_ref = refs[:n], refs[n : 2 * n], refs[2 * n]
    tokens, width = value_refs[0].shape[1:]
    heads = out_ref.shape[2] // (group * HD)
    span = tokens // spans
    lane = lax.broadcasted_iota(jnp.int32, (1, tokens), 1)
    inner = (lane % span).astype(jnp.float32)
    key_pos = jnp.concatenate(
        [
            ref[0, tokens : tokens + 1, :tokens].astype(jnp.float32) * span + inner
            for ref in key_refs
        ],
        axis=1,
    )
    hidden = jnp.where(key_pos <= place_ref[:, :1], 0.0, -1e30)
    hidden = jnp.concatenate([hidden] * group, axis=0)
    for j in range(heads):
        first = (first_head + j) * group * HD
        columns = slice((first_head + j) * HD, (first_head + j + 1) * HD)
        key_block = jnp.concatenate([ref[0, :tokens, columns] for ref in key_refs], axis=0)
        value_block = jnp.concatenate([ref[0, :, columns] for ref in value_refs], axis=0)
        queries = jnp.concatenate(
            [query_ref[0, :, first + g * HD : first + (g + 1) * HD] for g in range(group)], axis=0
        )
        scores = lax.dot_general(
            queries, key_block, (((1,), (1,)), ((), ())), preferred_element_type=jnp.float32
        )
        scores = jnp.where(hidden < 0.0, hidden, scores)
        top = jnp.max(scores, axis=1, keepdims=True)
        weights = jnp.exp2((scores - top) * (scale * math.log2(math.e)))
        total = jnp.sum(weights, axis=1, keepdims=True)
        mixed = jnp.dot(
            weights.astype(jnp.bfloat16), value_block, preferred_element_type=jnp.float32
        )
        mixed = (mixed / total).astype(jnp.bfloat16)
        for g in range(group):
            at = (j * group + g) * HD
            out_ref[0, :, at : at + HD] = mixed[g * tokens : (g + 1) * tokens]


def left_sides(refs, tokens, slots):
    near, far, near_other, far_other = refs
    side = lax.axis_index("tp") & 1
    columns = [slice(s * tokens, (s + 1) * tokens) for s in slots]
    return tuple(
        (at, jnp.concatenate([ref[:, here] for ref in pair for here in columns], axis=1))
        for at, pair in ((side, (near, far)), (1 - side, (near_other, far_other)))
    )


def early_kernel(slots, *refs):
    att_refs, cot_refs, total_ref = refs[: 2 * len(slots)], refs[2 * len(slots) : -1], refs[-1]
    half = cot_refs[0].shape[0]
    tokens = att_refs[0].shape[1]
    wide = TILE if total_ref.shape[1] % TILE == 0 else total_ref.shape[1]
    for j in range(total_ref.shape[1] // wide):
        columns = slice(j * wide, (j + 1) * wide)
        rows = jnp.concatenate([ref[0, :, columns] for ref in att_refs], axis=0)
        for at, left in left_sides(cot_refs, tokens, slots):
            total_ref[pl.ds(pl.multiple_of(at * half, half), half), columns] = jnp.dot(
                left, rows, preferred_element_type=jnp.float32
            )


def finish_kernel(slots, start, *refs):
    count = 2 * len(slots)
    att_refs, cot_refs, total_ref = refs[:count], refs[count : count + 4], refs[count + 4]
    out_ref, held, sems = refs[-3:]
    tokens, width = att_refs[0].shape[1:]
    tall = held.shape[1]
    half = cot_refs[0].shape[0]
    rows = jnp.concatenate([ref[0] for ref in att_refs], axis=0)
    copies = []
    for at, left in left_sides(cot_refs, tokens, slots):
        for i in range(half // tall):
            here = pl.ds(pl.multiple_of(at * half + i * tall, tall), tall)
            slot = len(copies)
            held[slot] = (
                total_ref[here, :]
                + jnp.dot(
                    left[i * tall : (i + 1) * tall], rows, preferred_element_type=jnp.float32
                )
            ).astype(jnp.bfloat16)
            copies.append(
                pltpu.make_async_copy(
                    held.at[slot], out_ref.at[0, here, start : start + width], sems.at[slot]
                )
            )
            copies[-1].start()
    for copy in copies:
        copy.wait()


def local(queries, keys, values, span_ids, cotangent):
    n = lax.axis_size("ctx")
    far = lax.axis_size("pipe") // 2
    tokens, width = keys.shape[1:]
    spans = span_ids.shape[1]
    heads = queries.shape[2]
    parts = 2 if width % (2 * HD) == 0 else 1
    chunk = heads // parts
    features = cotangent.shape[2] // n
    half = features // 2

    packed, place, *turned = pl.pallas_call(
        functools.partial(prepare_kernel, n),
        out_shape=[
            jax.ShapeDtypeStruct((1, tokens + TAG, width), jnp.bfloat16),
            jax.ShapeDtypeStruct((tokens, 128), jnp.float32),
        ]
        + [jax.ShapeDtypeStruct((half, tokens), jnp.bfloat16)] * n,
        in_specs=[ANY] * 3,
        out_specs=[VMEM] * (n + 2),
        scratch_shapes=[
            pltpu.SMEM(span_ids.shape, jnp.int32),
            pltpu.VMEM(cotangent.shape, jnp.bfloat16),
            pltpu.SemaphoreType.DMA((3,)),
        ],
        compiler_params=params(56),
        name="prepare",
    )(span_ids, keys, cotangent)
    fetched = (place, packed, queries, values, turned[0])
    place, key_held, query_held, value_held, turned[0] = pl.pallas_call(
        fetch_kernel,
        out_shape=[jax.ShapeDtypeStruct(x.shape, x.dtype) for x in fetched],
        in_specs=[VMEM] * 5,
        out_specs=[VMEM] * 5,
        compiler_params=params(16),
        name="fetch",
    )(*fetched)
    turned = [turned[0]] + [around(turned[s], s) for s in range(1, n)]
    key_edges, value_edges = ([around(x, way) for way in (1, -1)] for x in (packed, values))
    turned[0] = after(turned[0], *value_edges)
    mine = pl.pallas_call(
        join_kernel,
        out_shape=jax.ShapeDtypeStruct((half, n * tokens), jnp.bfloat16),
        in_specs=[VMEM] * n,
        out_specs=VMEM,
        compiler_params=params(16),
        name="join",
    )(*turned)
    mine_far = swap(mine, "pipe", far)
    key_ring = gather(packed, key_edges, 1, lambda x: after(x, query_held, mine))
    value_ring = gather(values, value_edges, -1, lambda x: after(x, value_held, mine))
    pieces = []
    for c in range(parts):
        pieces.append(
            pl.pallas_call(
                functools.partial(
                    attention_kernel,
                    HQ // HK,
                    1.0 / math.sqrt(HD),
                    n,
                    spans,
                    c * (width // HD // parts),
                ),
                out_shape=jax.ShapeDtypeStruct((1, tokens, chunk), jnp.bfloat16),
                in_specs=[VMEM] * (2 + 2 * n),
                out_specs=VMEM,
                compiler_params=params(40),
                name="attend",
            )(place, query_held, key_held, *key_ring[1:], value_held, *value_ring[1:])
        )

    near, mirrored = [], []
    for c in range(parts):
        held, sent = [pieces[c]], []
        for s in range(n):
            by_ring = s == n - 1 and c < parts - 1
            sent.append(around(sent[-1], 1) if by_ring else swap(held[s], "pipe", far))
            if s < n - 1:
                arrived = around(held[s], 1)
                held.append(after(arrived, sent[s]) if s < n - 2 else arrived)
        near.append(held)
        mirrored.append(sent)
    cots = [mine, mine_far, swap(mine, "tp", 1), swap(mine_far, "tp", 1)]

    def attended(c, slots):
        return [side[c][s] for side in (near, mirrored) for s in slots]

    first_slots = list(range(n - 1))

    tall = TILE if half % TILE == 0 else half
    totals = [
        pl.pallas_call(
        functools.partial(early_kernel, first_slots),
        out_shape=jax.ShapeDtypeStruct((features, chunk), jnp.float32),
        in_specs=[VMEM] * (2 * n + 2),
        out_specs=VMEM,
        compiler_params=params(40),
        cost_estimate=pl.CostEstimate(
            flops=4 * features * chunk * (n - 1) * tokens,
            bytes_accessed=8 * 2**20,
            transcendentals=0,
        ),
        name="early",
    )(*attended(c, first_slots), *cots)
        for c in range(parts)
    ]
    grad_out = None
    for c in range(parts):
        slots = [n - 1]
        operands = attended(c, slots) + cots + [totals[c]]
        specs = [VMEM] * len(operands)
        aliases = {}
        if grad_out is not None:
            aliases = {len(operands): 0}
            operands.append(grad_out)
            specs.append(ANY)
        grad_out = pl.pallas_call(
            functools.partial(finish_kernel, slots, c * chunk),
            out_shape=jax.ShapeDtypeStruct((1, features, heads), jnp.bfloat16),
            in_specs=specs,
            out_specs=ANY,
            scratch_shapes=[
                pltpu.VMEM((features // tall, tall, chunk), jnp.bfloat16),
                pltpu.SemaphoreType.DMA((features // tall,)),
            ],
            input_output_aliases=aliases,
            compiler_params=params(40),
            cost_estimate=pl.CostEstimate(
                flops=4 * features * chunk * len(slots) * tokens,
                bytes_accessed=8 * 2**20,
                transcendentals=0,
            ),
            name="finish",
        )(*operands)
    return (jnp.concatenate(pieces, axis=2), grad_out)


def solution(mesh):
    placed = (
        P("pipe", "ctx", "tp"),
        P("pipe", "ctx", "tp"),
        P("pipe", "ctx", "tp"),
        P("pipe", "ctx"),
        P("pipe", "ctx", None),
    )
    return jax.shard_map(
        local,
        mesh=mesh,
        in_specs=placed,
        out_specs=(P("pipe", "ctx", "tp"), P("pipe", "ctx", "tp")),
        check_vma=False,
    )
```

```python
import functools
import math

import jax
import jax.numpy as jnp
from jax import lax
from jax.experimental import pallas as pl
from jax.experimental.pallas import tpu as pltpu
from jax.sharding import PartitionSpec as P

HQ = 32
HK = 8
HD = 128
TAG = 16
TILE = 256
VMEM = pl.BlockSpec(memory_space=pltpu.VMEM)
SMEM = pl.BlockSpec(memory_space=pltpu.SMEM)
ANY = pl.BlockSpec(memory_space=pl.ANY)


def ring_order(n):
    return list(range(0, n, 2)) + list(range(1, n, 2))[::-1]


def around(x, shift):
    n = lax.axis_size("ctx")
    order = ring_order(n)
    return lax.ppermute(x, "ctx", [(order[q], order[(q + shift) % n]) for q in range(n)])


def gather(x, edges, ways, gate):
    n = lax.axis_size("ctx")
    middle = n // 2 if ways > 0 else (n - 1) // 2
    held = [x] + [None] * (n - 1)
    held[1], held[-1] = edges
    for s in range(2, middle + 1):
        held[s] = around(gate(held[s - 1]), 1)
    for s in range(2, n - middle):
        held[n - s] = around(gate(held[n - s + 1]), -1)
    return held


def swap(x, axis, mask):
    return lax.ppermute(x, axis, [(i, i ^ mask) for i in range(lax.axis_size(axis))])


def params(mib):
    return pltpu.CompilerParams(vmem_limit_bytes=mib * 2**20)


def after(x, *others):
    return lax.optimization_barrier((x, *others))[0]


def prepare_kernel(n, span_source, key_ref, cot_source, packed_ref, place_ref, *refs):
    out_refs, (span_ref, cot_ref, sems) = refs[:n], refs[n:]
    tokens, width = key_ref.shape[1:]
    copies = [
        pltpu.make_async_copy(cot_source, cot_ref, sems.at[0]),
        pltpu.make_async_copy(key_ref.at[0], packed_ref.at[0, :tokens], sems.at[1]),
        pltpu.make_async_copy(span_source, span_ref, sems.at[2]),
    ]
    for copy in copies:
        copy.start()
    copies[2].wait()
    spans = span_ref.shape[1]
    span = tokens // spans
    lane = lax.broadcasted_iota(jnp.int32, (TAG, width), 1)
    row = lax.broadcasted_iota(jnp.int32, place_ref.shape, 0)
    ids = jnp.zeros(lane.shape, jnp.float32)
    base = jnp.zeros(row.shape, jnp.int32)
    for j in range(spans):
        ids = jnp.where(lane // span == j, span_ref[0, j].astype(jnp.float32), ids)
        base = jnp.where(row // span == j, span_ref[0, j] * span, base)
    packed_ref[0, tokens:, :] = ids.astype(jnp.bfloat16)
    place_ref[...] = (base + row % span).astype(jnp.float32)
    me = lax.axis_index("ctx")
    side = lax.axis_index("tp") & 1
    half = cot_ref.shape[2] // n // 2
    copies[0].wait()
    place = jnp.where(me % 2 == 0, me // 2, n - 1 - me // 2)
    for s in range(n):
        to = (place + s) % n
        block = jnp.where(to < (n + 1) // 2, 2 * to, 2 * (n - to) - 1)
        at = pl.multiple_of((block * 2 + side) * half, 128)
        out_refs[s][...] = cot_ref[0, :, pl.ds(at, half)].T
    copies[1].wait()


def fetch_kernel(*refs):
    half = len(refs) // 2
    for ref, held_ref in zip(refs[:half], refs[half:]):
        held_ref[...] = ref[...]


def join_kernel(*refs):
    tokens = refs[0].shape[1]
    for s, ref in enumerate(refs[:-1]):
        refs[-1][:, s * tokens : (s + 1) * tokens] = ref[...]


def attention_kernel(group, scale, n, spans, first_head, place_ref, query_ref, *refs):
    key_refs, value_refs, out_ref = refs[:n], refs[n : 2 * n], refs[2 * n]
    tokens, width = value_refs[0].shape[1:]
    heads = out_ref.shape[2] // (group * HD)
    span = tokens // spans
    lane = lax.broadcasted_iota(jnp.int32, (1, tokens), 1)
    inner = (lane % span).astype(jnp.float32)
    key_pos = jnp.concatenate(
        [
            ref[0, tokens : tokens + 1, :tokens].astype(jnp.float32) * span + inner
            for ref in key_refs
        ],
        axis=1,
    )
    hidden = jnp.where(key_pos <= place_ref[:, :1], 0.0, -1e30)
    hidden = jnp.concatenate([hidden] * group, axis=0)
    for j in range(heads):
        first = (first_head + j) * group * HD
        columns = slice((first_head + j) * HD, (first_head + j + 1) * HD)
        key_block = jnp.concatenate([ref[0, :tokens, columns] for ref in key_refs], axis=0)
        value_block = jnp.concatenate([ref[0, :, columns] for ref in value_refs], axis=0)
        queries = jnp.concatenate(
            [query_ref[0, :, first + g * HD : first + (g + 1) * HD] for g in range(group)], axis=0
        )
        scores = lax.dot_general(
            queries, key_block, (((1,), (1,)), ((), ())), preferred_element_type=jnp.float32
        )
        scores = jnp.where(hidden < 0.0, hidden, scores)
        top = jnp.max(scores, axis=1, keepdims=True)
        weights = jnp.exp2((scores - top) * (scale * math.log2(math.e)))
        total = jnp.sum(weights, axis=1, keepdims=True)
        mixed = jnp.dot(
            weights.astype(jnp.bfloat16), value_block, preferred_element_type=jnp.float32
        )
        mixed = (mixed / total).astype(jnp.bfloat16)
        for g in range(group):
            at = (j * group + g) * HD
            out_ref[0, :, at : at + HD] = mixed[g * tokens : (g + 1) * tokens]


def left_sides(refs, tokens, slots):
    near, far, near_other, far_other = refs
    side = lax.axis_index("tp") & 1
    columns = [slice(s * tokens, (s + 1) * tokens) for s in slots]
    return tuple(
        (at, jnp.concatenate([ref[:, here] for ref in pair for here in columns], axis=1))
        for at, pair in ((side, (near, far)), (1 - side, (near_other, far_other)))
    )


def early_kernel(slots, *refs):
    att_refs, cot_refs, total_ref = refs[: 2 * len(slots)], refs[2 * len(slots) : -1], refs[-1]
    half = cot_refs[0].shape[0]
    tokens = att_refs[0].shape[1]
    wide = TILE if total_ref.shape[1] % TILE == 0 else total_ref.shape[1]
    for j in range(total_ref.shape[1] // wide):
        columns = slice(j * wide, (j + 1) * wide)
        rows = jnp.concatenate([ref[0, :, columns] for ref in att_refs], axis=0)
        for at, left in left_sides(cot_refs, tokens, slots):
            total_ref[pl.ds(pl.multiple_of(at * half, half), half), columns] = jnp.dot(
                left, rows, preferred_element_type=jnp.float32
            )


def finish_kernel(slots, start, *refs):
    count = 2 * len(slots)
    att_refs, cot_refs, total_ref = refs[:count], refs[count : count + 4], refs[count + 4]
    out_ref, held, sems = refs[-3:]
    tokens, width = att_refs[0].shape[1:]
    tall = held.shape[1]
    half = cot_refs[0].shape[0]
    rows = jnp.concatenate([ref[0] for ref in att_refs], axis=0)
    copies = []
    for at, left in left_sides(cot_refs, tokens, slots):
        for i in range(half // tall):
            here = pl.ds(pl.multiple_of(at * half + i * tall, tall), tall)
            slot = len(copies)
            held[slot] = (
                total_ref[here, :]
                + jnp.dot(
                    left[i * tall : (i + 1) * tall], rows, preferred_element_type=jnp.float32
                )
            ).astype(jnp.bfloat16)
            copies.append(
                pltpu.make_async_copy(
                    held.at[slot], out_ref.at[0, here, start : start + width], sems.at[slot]
                )
            )
            copies[-1].start()
    for copy in copies:
        copy.wait()


def local(queries, keys, values, span_ids, cotangent):
    n = lax.axis_size("ctx")
    far = lax.axis_size("pipe") // 2
    tokens, width = keys.shape[1:]
    spans = span_ids.shape[1]
    heads = queries.shape[2]
    parts = 2 if width % (2 * HD) == 0 else 1
    chunk = heads // parts
    features = cotangent.shape[2] // n
    half = features // 2

    packed, place, *turned = pl.pallas_call(
        functools.partial(prepare_kernel, n),
        out_shape=[
            jax.ShapeDtypeStruct((1, tokens + TAG, width), jnp.bfloat16),
            jax.ShapeDtypeStruct((tokens, 128), jnp.float32),
        ]
        + [jax.ShapeDtypeStruct((half, tokens), jnp.bfloat16)] * n,
        in_specs=[ANY] * 3,
        out_specs=[VMEM] * (n + 2),
        scratch_shapes=[
            pltpu.SMEM(span_ids.shape, jnp.int32),
            pltpu.VMEM(cotangent.shape, jnp.bfloat16),
            pltpu.SemaphoreType.DMA((3,)),
        ],
        compiler_params=params(56),
        name="prepare",
    )(span_ids, keys, cotangent)
    fetched = (place, packed, queries, values, turned[0])
    place, key_held, query_held, value_held, turned[0] = pl.pallas_call(
        fetch_kernel,
        out_shape=[jax.ShapeDtypeStruct(x.shape, x.dtype) for x in fetched],
        in_specs=[VMEM] * 5,
        out_specs=[VMEM] * 5,
        compiler_params=params(16),
        name="fetch",
    )(*fetched)
    turned = [turned[0]] + [around(turned[s], s) for s in range(1, n)]
    key_edges, value_edges = ([around(x, way) for way in (1, -1)] for x in (packed, values))
    turned[0] = after(turned[0], *value_edges)
    mine = pl.pallas_call(
        join_kernel,
        out_shape=jax.ShapeDtypeStruct((half, n * tokens), jnp.bfloat16),
        in_specs=[VMEM] * n,
        out_specs=VMEM,
        compiler_params=params(16),
        name="join",
    )(*turned)
    mine_far = swap(mine, "pipe", far)
    key_ring = gather(packed, key_edges, 1, lambda x: after(x, query_held, mine))
    value_ring = gather(values, value_edges, -1, lambda x: after(x, value_held, mine))
    pieces = []
    for c in range(parts):
        pieces.append(
            pl.pallas_call(
                functools.partial(
                    attention_kernel,
                    HQ // HK,
                    1.0 / math.sqrt(HD),
                    n,
                    spans,
                    c * (width // HD // parts),
                ),
                out_shape=jax.ShapeDtypeStruct((1, tokens, chunk), jnp.bfloat16),
                in_specs=[VMEM] * (2 + 2 * n),
                out_specs=VMEM,
                compiler_params=params(40),
                name="attend",
            )(place, query_held, key_held, *key_ring[1:], value_held, *value_ring[1:])
        )

    near, mirrored = [], []
    for c in range(parts):
        held, sent = [pieces[c]], []
        for s in range(n):
            by_ring = s == n - 1 and c < parts - 1
            sent.append(around(sent[-1], 1) if by_ring else swap(held[s], "pipe", far))
            if s < n - 1:
                arrived = around(held[s], 1)
                held.append(after(arrived, sent[s]) if s < n - 2 - (c == 0) else arrived)
        near.append(held)
        mirrored.append(sent)
    cots = [mine, mine_far, swap(mine, "tp", 1), swap(mine_far, "tp", 1)]

    def attended(c, slots):
        return [side[c][s] for side in (near, mirrored) for s in slots]

    first_slots = list(range(n - 1))

    tall = TILE if half % TILE == 0 else half
    totals = [
        pl.pallas_call(
        functools.partial(early_kernel, first_slots),
        out_shape=jax.ShapeDtypeStruct((features, chunk), jnp.float32),
        in_specs=[VMEM] * (2 * n + 2),
        out_specs=VMEM,
        compiler_params=params(40),
        cost_estimate=pl.CostEstimate(
            flops=4 * features * chunk * (n - 1) * tokens,
            bytes_accessed=8 * 2**20,
            transcendentals=0,
        ),
        name="early",
    )(*attended(c, first_slots), *cots)
        for c in range(parts)
    ]
    grad_out = None
    for c in range(parts):
        slots = [n - 1]
        operands = attended(c, slots) + cots + [totals[c]]
        specs = [VMEM] * len(operands)
        aliases = {}
        if grad_out is not None:
            aliases = {len(operands): 0}
            operands.append(grad_out)
            specs.append(ANY)
        grad_out = pl.pallas_call(
            functools.partial(finish_kernel, slots, c * chunk),
            out_shape=jax.ShapeDtypeStruct((1, features, heads), jnp.bfloat16),
            in_specs=specs,
            out_specs=ANY,
            scratch_shapes=[
                pltpu.VMEM((features // tall, tall, chunk), jnp.bfloat16),
                pltpu.SemaphoreType.DMA((features // tall,)),
            ],
            input_output_aliases=aliases,
            compiler_params=params(40),
            cost_estimate=pl.CostEstimate(
                flops=4 * features * chunk * len(slots) * tokens,
                bytes_accessed=8 * 2**20,
                transcendentals=0,
            ),
            name="finish",
        )(*operands)
    return (jnp.concatenate(pieces, axis=2), grad_out)


def solution(mesh):
    placed = (
        P("pipe", "ctx", "tp"),
        P("pipe", "ctx", "tp"),
        P("pipe", "ctx", "tp"),
        P("pipe", "ctx"),
        P("pipe", "ctx", None),
    )
    return jax.shard_map(
        local,
        mesh=mesh,
        in_specs=placed,
        out_specs=(P("pipe", "ctx", "tp"), P("pipe", "ctx", "tp")),
        check_vma=False,
    )
```

```python
import functools
import math

import jax
import jax.numpy as jnp
from jax import lax
from jax.experimental import pallas as pl
from jax.experimental.pallas import tpu as pltpu
from jax.sharding import PartitionSpec as P

HQ = 32
HK = 8
HD = 128
TAG = 16
TILE = 256
VMEM = pl.BlockSpec(memory_space=pltpu.VMEM)
SMEM = pl.BlockSpec(memory_space=pltpu.SMEM)
ANY = pl.BlockSpec(memory_space=pl.ANY)


def ring_order(n):
    return list(range(0, n, 2)) + list(range(1, n, 2))[::-1]


def around(x, shift):
    n = lax.axis_size("ctx")
    order = ring_order(n)
    return lax.ppermute(x, "ctx", [(order[q], order[(q + shift) % n]) for q in range(n)])


def gather(x, edges, ways, gate):
    n = lax.axis_size("ctx")
    middle = n // 2 if ways > 0 else (n - 1) // 2
    held = [x] + [None] * (n - 1)
    held[1], held[-1] = edges
    for s in range(2, middle + 1):
        held[s] = around(gate(held[s - 1]), 1)
    for s in range(2, n - middle):
        held[n - s] = around(gate(held[n - s + 1]), -1)
    return held


def swap(x, axis, mask):
    return lax.ppermute(x, axis, [(i, i ^ mask) for i in range(lax.axis_size(axis))])


def params(mib):
    return pltpu.CompilerParams(vmem_limit_bytes=mib * 2**20)


def after(x, *others):
    return lax.optimization_barrier((x, *others))[0]


def prepare_kernel(n, span_source, key_ref, cot_source, packed_ref, place_ref, *refs):
    out_refs, (span_ref, cot_ref, sems) = refs[:n], refs[n:]
    tokens, width = key_ref.shape[1:]
    copies = [
        pltpu.make_async_copy(cot_source, cot_ref, sems.at[0]),
        pltpu.make_async_copy(key_ref.at[0], packed_ref.at[0, :tokens], sems.at[1]),
        pltpu.make_async_copy(span_source, span_ref, sems.at[2]),
    ]
    for copy in copies:
        copy.start()
    copies[2].wait()
    spans = span_ref.shape[1]
    span = tokens // spans
    lane = lax.broadcasted_iota(jnp.int32, (TAG, width), 1)
    row = lax.broadcasted_iota(jnp.int32, place_ref.shape, 0)
    ids = jnp.zeros(lane.shape, jnp.float32)
    base = jnp.zeros(row.shape, jnp.int32)
    for j in range(spans):
        ids = jnp.where(lane // span == j, span_ref[0, j].astype(jnp.float32), ids)
        base = jnp.where(row // span == j, span_ref[0, j] * span, base)
    packed_ref[0, tokens:, :] = ids.astype(jnp.bfloat16)
    place_ref[...] = (base + row % span).astype(jnp.float32)
    me = lax.axis_index("ctx")
    side = lax.axis_index("tp") & 1
    half = cot_ref.shape[2] // n // 2
    copies[0].wait()
    place = jnp.where(me % 2 == 0, me // 2, n - 1 - me // 2)
    for s in range(n):
        to = (place + s) % n
        block = jnp.where(to < (n + 1) // 2, 2 * to, 2 * (n - to) - 1)
        at = pl.multiple_of((block * 2 + side) * half, 128)
        out_refs[s][...] = cot_ref[0, :, pl.ds(at, half)].T
    copies[1].wait()


def fetch_kernel(*refs):
    half = len(refs) // 2
    for ref, held_ref in zip(refs[:half], refs[half:]):
        held_ref[...] = ref[...]


def join_kernel(*refs):
    tokens = refs[0].shape[1]
    for s, ref in enumerate(refs[:-1]):
        refs[-1][:, s * tokens : (s + 1) * tokens] = ref[...]


def attention_kernel(group, scale, n, spans, first_head, place_ref, query_ref, *refs):
    key_refs, value_refs, out_ref = refs[:n], refs[n : 2 * n], refs[2 * n]
    tokens, width = value_refs[0].shape[1:]
    heads = out_ref.shape[2] // (group * HD)
    span = tokens // spans
    lane = lax.broadcasted_iota(jnp.int32, (1, tokens), 1)
    inner = (lane % span).astype(jnp.float32)
    key_pos = jnp.concatenate(
        [
            ref[0, tokens : tokens + 1, :tokens].astype(jnp.float32) * span + inner
            for ref in key_refs
        ],
        axis=1,
    )
    hidden = jnp.where(key_pos <= place_ref[:, :1], 0.0, -1e30)
    hidden = jnp.concatenate([hidden] * group, axis=0)
    for j in range(heads):
        first = (first_head + j) * group * HD
        columns = slice((first_head + j) * HD, (first_head + j + 1) * HD)
        key_block = jnp.concatenate([ref[0, :tokens, columns] for ref in key_refs], axis=0)
        value_block = jnp.concatenate([ref[0, :, columns] for ref in value_refs], axis=0)
        queries = jnp.concatenate(
            [query_ref[0, :, first + g * HD : first + (g + 1) * HD] for g in range(group)], axis=0
        )
        scores = lax.dot_general(
            queries, key_block, (((1,), (1,)), ((), ())), preferred_element_type=jnp.float32
        )
        scores = jnp.where(hidden < 0.0, hidden, scores)
        top = jnp.max(scores, axis=1, keepdims=True)
        weights = jnp.exp2((scores - top) * (scale * math.log2(math.e)))
        total = jnp.sum(weights, axis=1, keepdims=True)
        mixed = jnp.dot(
            weights.astype(jnp.bfloat16), value_block, preferred_element_type=jnp.float32
        )
        mixed = (mixed / total).astype(jnp.bfloat16)
        for g in range(group):
            at = (j * group + g) * HD
            out_ref[0, :, at : at + HD] = mixed[g * tokens : (g + 1) * tokens]


def left_sides(refs, tokens, slots):
    near, far, near_other, far_other = refs
    side = lax.axis_index("tp") & 1
    columns = [slice(s * tokens, (s + 1) * tokens) for s in slots]
    return tuple(
        (at, jnp.concatenate([ref[:, here] for ref in pair for here in columns], axis=1))
        for at, pair in ((side, (near, far)), (1 - side, (near_other, far_other)))
    )


def early_kernel(slots, *refs):
    att_refs, cot_refs, total_ref = refs[: 2 * len(slots)], refs[2 * len(slots) : -1], refs[-1]
    half = cot_refs[0].shape[0]
    tokens = att_refs[0].shape[1]
    wide = TILE if total_ref.shape[1] % TILE == 0 else total_ref.shape[1]
    for j in range(total_ref.shape[1] // wide):
        columns = slice(j * wide, (j + 1) * wide)
        rows = jnp.concatenate([ref[0, :, columns] for ref in att_refs], axis=0)
        for at, left in left_sides(cot_refs, tokens, slots):
            total_ref[pl.ds(pl.multiple_of(at * half, half), half), columns] = jnp.dot(
                left, rows, preferred_element_type=jnp.float32
            )


def finish_kernel(slots, start, *refs):
    count = 2 * len(slots)
    att_refs, cot_refs, total_ref = refs[:count], refs[count : count + 4], refs[count + 4]
    out_ref, held, sems = refs[-3:]
    tokens, width = att_refs[0].shape[1:]
    tall = held.shape[1]
    half = cot_refs[0].shape[0]
    rows = jnp.concatenate([ref[0] for ref in att_refs], axis=0)
    copies = []
    for at, left in left_sides(cot_refs, tokens, slots):
        for i in range(half // tall):
            here = pl.ds(pl.multiple_of(at * half + i * tall, tall), tall)
            slot = len(copies)
            held[slot] = (
                total_ref[here, :]
                + jnp.dot(
                    left[i * tall : (i + 1) * tall], rows, preferred_element_type=jnp.float32
                )
            ).astype(jnp.bfloat16)
            copies.append(
                pltpu.make_async_copy(
                    held.at[slot], out_ref.at[0, here, start : start + width], sems.at[slot]
                )
            )
            copies[-1].start()
    for copy in copies:
        copy.wait()


def local(queries, keys, values, span_ids, cotangent):
    n = lax.axis_size("ctx")
    far = lax.axis_size("pipe") // 2
    tokens, width = keys.shape[1:]
    spans = span_ids.shape[1]
    heads = queries.shape[2]
    parts = 2 if width % (2 * HD) == 0 else 1
    chunk = heads // parts
    features = cotangent.shape[2] // n
    half = features // 2

    packed, place, *turned = pl.pallas_call(
        functools.partial(prepare_kernel, n),
        out_shape=[
            jax.ShapeDtypeStruct((1, tokens + TAG, width), jnp.bfloat16),
            jax.ShapeDtypeStruct((tokens, 128), jnp.float32),
        ]
        + [jax.ShapeDtypeStruct((half, tokens), jnp.bfloat16)] * n,
        in_specs=[ANY] * 3,
        out_specs=[VMEM] * (n + 2),
        scratch_shapes=[
            pltpu.SMEM(span_ids.shape, jnp.int32),
            pltpu.VMEM(cotangent.shape, jnp.bfloat16),
            pltpu.SemaphoreType.DMA((3,)),
        ],
        compiler_params=params(56),
        name="prepare",
    )(span_ids, keys, cotangent)
    fetched = (place, packed, queries, values, turned[0])
    place, key_held, query_held, value_held, turned[0] = pl.pallas_call(
        fetch_kernel,
        out_shape=[jax.ShapeDtypeStruct(x.shape, x.dtype) for x in fetched],
        in_specs=[VMEM] * 5,
        out_specs=[VMEM] * 5,
        compiler_params=params(16),
        name="fetch",
    )(*fetched)
    turned = [turned[0]] + [around(turned[s], s) for s in range(1, n)]
    key_edges, value_edges = ([around(x, way) for way in (1, -1)] for x in (packed, values))
    turned[0] = after(turned[0], *value_edges)
    mine = pl.pallas_call(
        join_kernel,
        out_shape=jax.ShapeDtypeStruct((half, n * tokens), jnp.bfloat16),
        in_specs=[VMEM] * n,
        out_specs=VMEM,
        compiler_params=params(16),
        name="join",
    )(*turned)
    mine_far = swap(mine, "pipe", far)
    key_ring = gather(packed, key_edges, 1, lambda x: after(x, query_held, mine))
    value_ring = gather(values, value_edges, -1, lambda x: after(x, value_held, mine))
    pieces = []
    for c in range(parts):
        pieces.append(
            pl.pallas_call(
                functools.partial(
                    attention_kernel,
                    HQ // HK,
                    1.0 / math.sqrt(HD),
                    n,
                    spans,
                    c * (width // HD // parts),
                ),
                out_shape=jax.ShapeDtypeStruct((1, tokens, chunk), jnp.bfloat16),
                in_specs=[VMEM] * (2 + 2 * n),
                out_specs=VMEM,
                compiler_params=params(40),
                name="attend",
            )(place, query_held, key_held, *key_ring[1:], value_held, *value_ring[1:])
        )

    near, mirrored = [], []
    for c in range(parts):
        held, sent = [pieces[c]], []
        for s in range(n):
            by_ring = s == n - 1 and c < parts - 1
            sent.append(around(sent[-1], 1) if by_ring else swap(held[s], "pipe", far))
            if s < n - 1:
                arrived = around(held[s], 1)
                held.append(after(arrived, sent[s]) if s < n - 2 else arrived)
        near.append(held)
        mirrored.append(sent)
    cots = [mine, mine_far, swap(mine, "tp", 1), swap(mine_far, "tp", 1)]

    def attended(c, slots):
        return [side[c][s] for side in (near, mirrored) for s in slots]

    first_slots = list(range(n - 1))

    tall = TILE if half % TILE == 0 else half
    totals = [
        pl.pallas_call(
        functools.partial(early_kernel, first_slots),
        out_shape=jax.ShapeDtypeStruct((features, chunk), jnp.float32),
        in_specs=[VMEM] * (2 * n + 2),
        out_specs=VMEM,
        compiler_params=params(40),
        cost_estimate=pl.CostEstimate(
            flops=4 * features * chunk * (n - 1) * tokens,
            bytes_accessed=8 * 2**20,
            transcendentals=0,
        ),
        name="early",
    )(*attended(c, first_slots), *cots)
        for c in range(parts)
    ]
    grad_out = None
    for c in reversed(range(parts)):
        slots = [n - 1]
        operands = attended(c, slots) + cots + [totals[c]]
        specs = [VMEM] * len(operands)
        aliases = {}
        if grad_out is not None:
            aliases = {len(operands): 0}
            operands.append(grad_out)
            specs.append(ANY)
        grad_out = pl.pallas_call(
            functools.partial(finish_kernel, slots, c * chunk),
            out_shape=jax.ShapeDtypeStruct((1, features, heads), jnp.bfloat16),
            in_specs=specs,
            out_specs=ANY,
            scratch_shapes=[
                pltpu.VMEM((features // tall, tall, chunk), jnp.bfloat16),
                pltpu.SemaphoreType.DMA((features // tall,)),
            ],
            input_output_aliases=aliases,
            compiler_params=params(40),
            cost_estimate=pl.CostEstimate(
                flops=4 * features * chunk * len(slots) * tokens,
                bytes_accessed=8 * 2**20,
                transcendentals=0,
            ),
            name="finish",
        )(*operands)
    return (jnp.concatenate(pieces, axis=2), grad_out)


def solution(mesh):
    placed = (
        P("pipe", "ctx", "tp"),
        P("pipe", "ctx", "tp"),
        P("pipe", "ctx", "tp"),
        P("pipe", "ctx"),
        P("pipe", "ctx", None),
    )
    return jax.shard_map(
        local,
        mesh=mesh,
        in_specs=placed,
        out_specs=(P("pipe", "ctx", "tp"), P("pipe", "ctx", "tp")),
        check_vma=False,
    )
```

```python
import functools
import math

import jax
import jax.numpy as jnp
from jax import lax
from jax.experimental import pallas as pl
from jax.experimental.pallas import tpu as pltpu
from jax.sharding import PartitionSpec as P

HQ = 32
HK = 8
HD = 128
TAG = 16
TILE = 256
VMEM = pl.BlockSpec(memory_space=pltpu.VMEM)
SMEM = pl.BlockSpec(memory_space=pltpu.SMEM)
ANY = pl.BlockSpec(memory_space=pl.ANY)


def ring_order(n):
    return list(range(0, n, 2)) + list(range(1, n, 2))[::-1]


def around(x, shift):
    n = lax.axis_size("ctx")
    order = ring_order(n)
    return lax.ppermute(x, "ctx", [(order[q], order[(q + shift) % n]) for q in range(n)])


def gather(x, edges, ways, gate):
    n = lax.axis_size("ctx")
    middle = n // 2 if ways > 0 else (n - 1) // 2
    held = [x] + [None] * (n - 1)
    held[1], held[-1] = edges
    for s in range(2, middle + 1):
        held[s] = around(gate(held[s - 1]), 1)
    for s in range(2, n - middle):
        held[n - s] = around(gate(held[n - s + 1]), -1)
    return held


def swap(x, axis, mask):
    return lax.ppermute(x, axis, [(i, i ^ mask) for i in range(lax.axis_size(axis))])


def params(mib):
    return pltpu.CompilerParams(vmem_limit_bytes=mib * 2**20)


def after(x, *others):
    return lax.optimization_barrier((x, *others))[0]


def prepare_kernel(n, span_source, key_ref, cot_source, packed_ref, place_ref, *refs):
    out_refs, (span_ref, cot_ref, sems) = refs[:n], refs[n:]
    tokens, width = key_ref.shape[1:]
    copies = [
        pltpu.make_async_copy(cot_source, cot_ref, sems.at[0]),
        pltpu.make_async_copy(key_ref.at[0], packed_ref.at[0, :tokens], sems.at[1]),
        pltpu.make_async_copy(span_source, span_ref, sems.at[2]),
    ]
    for copy in copies:
        copy.start()
    copies[2].wait()
    spans = span_ref.shape[1]
    span = tokens // spans
    lane = lax.broadcasted_iota(jnp.int32, (TAG, width), 1)
    row = lax.broadcasted_iota(jnp.int32, place_ref.shape, 0)
    ids = jnp.zeros(lane.shape, jnp.float32)
    base = jnp.zeros(row.shape, jnp.int32)
    for j in range(spans):
        ids = jnp.where(lane // span == j, span_ref[0, j].astype(jnp.float32), ids)
        base = jnp.where(row // span == j, span_ref[0, j] * span, base)
    packed_ref[0, tokens:, :] = ids.astype(jnp.bfloat16)
    place_ref[...] = (base + row % span).astype(jnp.float32)
    me = lax.axis_index("ctx")
    side = lax.axis_index("tp") & 1
    half = cot_ref.shape[2] // n // 2
    copies[0].wait()
    place = jnp.where(me % 2 == 0, me // 2, n - 1 - me // 2)
    for s in range(n):
        to = (place + s) % n
        block = jnp.where(to < (n + 1) // 2, 2 * to, 2 * (n - to) - 1)
        at = pl.multiple_of((block * 2 + side) * half, 128)
        out_refs[s][...] = cot_ref[0, :, pl.ds(at, half)].T
    copies[1].wait()


def fetch_kernel(*refs):
    half = len(refs) // 2
    for ref, held_ref in zip(refs[:half], refs[half:]):
        held_ref[...] = ref[...]


def join_kernel(*refs):
    tokens = refs[0].shape[1]
    for s, ref in enumerate(refs[:-1]):
        refs[-1][:, s * tokens : (s + 1) * tokens] = ref[...]


def attention_kernel(group, scale, n, spans, first_head, place_ref, query_ref, *refs):
    key_refs, value_refs, out_ref = refs[:n], refs[n : 2 * n], refs[2 * n]
    tokens, width = value_refs[0].shape[1:]
    heads = out_ref.shape[2] // (group * HD)
    span = tokens // spans
    lane = lax.broadcasted_iota(jnp.int32, (1, tokens), 1)
    inner = (lane % span).astype(jnp.float32)
    key_pos = jnp.concatenate(
        [
            ref[0, tokens : tokens + 1, :tokens].astype(jnp.float32) * span + inner
            for ref in key_refs
        ],
        axis=1,
    )
    hidden = jnp.where(key_pos <= place_ref[:, :1], 0.0, -1e30)
    hidden = jnp.concatenate([hidden] * group, axis=0)
    for j in range(heads):
        first = (first_head + j) * group * HD
        columns = slice((first_head + j) * HD, (first_head + j + 1) * HD)
        key_block = jnp.concatenate([ref[0, :tokens, columns] for ref in key_refs], axis=0)
        value_block = jnp.concatenate([ref[0, :, columns] for ref in value_refs], axis=0)
        queries = jnp.concatenate(
            [query_ref[0, :, first + g * HD : first + (g + 1) * HD] for g in range(group)], axis=0
        )
        scores = lax.dot_general(
            queries, key_block, (((1,), (1,)), ((), ())), preferred_element_type=jnp.float32
        )
        scores = jnp.where(hidden < 0.0, hidden, scores)
        top = jnp.max(scores, axis=1, keepdims=True)
        weights = jnp.exp2((scores - top) * (scale * math.log2(math.e)))
        total = jnp.sum(weights, axis=1, keepdims=True)
        mixed = jnp.dot(
            weights.astype(jnp.bfloat16), value_block, preferred_element_type=jnp.float32
        )
        mixed = (mixed / total).astype(jnp.bfloat16)
        for g in range(group):
            at = (j * group + g) * HD
            out_ref[0, :, at : at + HD] = mixed[g * tokens : (g + 1) * tokens]


def left_sides(refs, tokens, slots):
    near, far, near_other, far_other = refs
    side = lax.axis_index("tp") & 1
    columns = [slice(s * tokens, (s + 1) * tokens) for s in slots]
    return tuple(
        (at, jnp.concatenate([ref[:, here] for ref in pair for here in columns], axis=1))
        for at, pair in ((side, (near, far)), (1 - side, (near_other, far_other)))
    )


def early_kernel(slots, *refs):
    att_refs, cot_refs, total_ref = refs[: 2 * len(slots)], refs[2 * len(slots) : -1], refs[-1]
    half = cot_refs[0].shape[0]
    tokens = att_refs[0].shape[1]
    wide = TILE if total_ref.shape[1] % TILE == 0 else total_ref.shape[1]
    for j in range(total_ref.shape[1] // wide):
        columns = slice(j * wide, (j + 1) * wide)
        rows = jnp.concatenate([ref[0, :, columns] for ref in att_refs], axis=0)
        for at, left in left_sides(cot_refs, tokens, slots):
            total_ref[pl.ds(pl.multiple_of(at * half, half), half), columns] = jnp.dot(
                left, rows, preferred_element_type=jnp.float32
            )


def finish_kernel(slots, start, *refs):
    count = 2 * len(slots)
    att_refs, cot_refs, total_ref = refs[:count], refs[count : count + 4], refs[count + 4]
    out_ref, held, sems = refs[-3:]
    tokens, width = att_refs[0].shape[1:]
    tall = held.shape[1]
    half = cot_refs[0].shape[0]
    rows = jnp.concatenate([ref[0] for ref in att_refs], axis=0)
    copies = []
    for at, left in left_sides(cot_refs, tokens, slots):
        for i in range(half // tall):
            here = pl.ds(pl.multiple_of(at * half + i * tall, tall), tall)
            slot = len(copies)
            held[slot] = (
                total_ref[here, :]
                + jnp.dot(
                    left[i * tall : (i + 1) * tall], rows, preferred_element_type=jnp.float32
                )
            ).astype(jnp.bfloat16)
            copies.append(
                pltpu.make_async_copy(
                    held.at[slot], out_ref.at[0, here, start : start + width], sems.at[slot]
                )
            )
            copies[-1].start()
    for copy in copies:
        copy.wait()


def local(queries, keys, values, span_ids, cotangent):
    n = lax.axis_size("ctx")
    far = lax.axis_size("pipe") // 2
    tokens, width = keys.shape[1:]
    spans = span_ids.shape[1]
    heads = queries.shape[2]
    parts = 2 if width % (2 * HD) == 0 else 1
    chunk = heads // parts
    features = cotangent.shape[2] // n
    half = features // 2

    packed, place, *turned = pl.pallas_call(
        functools.partial(prepare_kernel, n),
        out_shape=[
            jax.ShapeDtypeStruct((1, tokens + TAG, width), jnp.bfloat16),
            jax.ShapeDtypeStruct((tokens, 128), jnp.float32),
        ]
        + [jax.ShapeDtypeStruct((half, tokens), jnp.bfloat16)] * n,
        in_specs=[ANY] * 3,
        out_specs=[VMEM] * (n + 2),
        scratch_shapes=[
            pltpu.SMEM(span_ids.shape, jnp.int32),
            pltpu.VMEM(cotangent.shape, jnp.bfloat16),
            pltpu.SemaphoreType.DMA((3,)),
        ],
        compiler_params=params(56),
        name="prepare",
    )(span_ids, keys, cotangent)
    fetched = (place, packed, queries, values, turned[0])
    place, key_held, query_held, value_held, turned[0] = pl.pallas_call(
        fetch_kernel,
        out_shape=[jax.ShapeDtypeStruct(x.shape, x.dtype) for x in fetched],
        in_specs=[VMEM] * 5,
        out_specs=[VMEM] * 5,
        compiler_params=params(16),
        name="fetch",
    )(*fetched)
    turned = [turned[0]] + [around(turned[s], s) for s in range(1, n)]
    key_edges, value_edges = ([around(x, way) for way in (1, -1)] for x in (packed, values))
    turned[0] = after(turned[0], *value_edges)
    mine = pl.pallas_call(
        join_kernel,
        out_shape=jax.ShapeDtypeStruct((half, n * tokens), jnp.bfloat16),
        in_specs=[VMEM] * n,
        out_specs=VMEM,
        compiler_params=params(16),
        name="join",
    )(*turned)
    mine_far = swap(mine, "pipe", far)
    key_ring = gather(packed, key_edges, 1, lambda x: after(x, query_held, mine))
    value_ring = gather(values, value_edges, -1, lambda x: after(x, value_held, mine))
    pieces = []
    for c in range(parts):
        pieces.append(
            pl.pallas_call(
                functools.partial(
                    attention_kernel,
                    HQ // HK,
                    1.0 / math.sqrt(HD),
                    n,
                    spans,
                    c * (width // HD // parts),
                ),
                out_shape=jax.ShapeDtypeStruct((1, tokens, chunk), jnp.bfloat16),
                in_specs=[VMEM] * (2 + 2 * n),
                out_specs=VMEM,
                compiler_params=params(40),
                name="attend",
            )(place, query_held, key_held, *key_ring[1:], value_held, *value_ring[1:])
        )

    near, mirrored = [], []
    for c in range(parts):
        held, sent = [pieces[c]], []
        for s in range(n):
            by_ring = s == n - 1 and c < parts - 1
            sent.append(around(sent[-1], 1) if by_ring else swap(held[s], "pipe", far))
            if s < n - 1:
                arrived = around(held[s], 1)
                held.append(after(arrived, sent[s]) if s < n - 2 - (c == 0) else arrived)
        near.append(held)
        mirrored.append(sent)
    cots = [mine, mine_far, swap(mine, "tp", 1), swap(mine_far, "tp", 1)]

    def attended(c, slots):
        return [side[c][s] for side in (near, mirrored) for s in slots]

    first_slots = list(range(n - 1))

    tall = TILE if half % TILE == 0 else half
    totals = [
        pl.pallas_call(
        functools.partial(early_kernel, first_slots),
        out_shape=jax.ShapeDtypeStruct((features, chunk), jnp.float32),
        in_specs=[VMEM] * (2 * n + 2),
        out_specs=VMEM,
        compiler_params=params(40),
        cost_estimate=pl.CostEstimate(
            flops=4 * features * chunk * (n - 1) * tokens,
            bytes_accessed=8 * 2**20,
            transcendentals=0,
        ),
        name="early",
    )(*attended(c, first_slots), *cots)
        for c in range(parts)
    ]
    grad_out = None
    for c in reversed(range(parts)):
        slots = [n - 1]
        operands = attended(c, slots) + cots + [totals[c]]
        specs = [VMEM] * len(operands)
        aliases = {}
        if grad_out is not None:
            aliases = {len(operands): 0}
            operands.append(grad_out)
            specs.append(ANY)
        grad_out = pl.pallas_call(
            functools.partial(finish_kernel, slots, c * chunk),
            out_shape=jax.ShapeDtypeStruct((1, features, heads), jnp.bfloat16),
            in_specs=specs,
            out_specs=ANY,
            scratch_shapes=[
                pltpu.VMEM((features // tall, tall, chunk), jnp.bfloat16),
                pltpu.SemaphoreType.DMA((features // tall,)),
            ],
            input_output_aliases=aliases,
            compiler_params=params(40),
            cost_estimate=pl.CostEstimate(
                flops=4 * features * chunk * len(slots) * tokens,
                bytes_accessed=8 * 2**20,
                transcendentals=0,
            ),
            name="finish",
        )(*operands)
    return (jnp.concatenate(pieces, axis=2), grad_out)


def solution(mesh):
    placed = (
        P("pipe", "ctx", "tp"),
        P("pipe", "ctx", "tp"),
        P("pipe", "ctx", "tp"),
        P("pipe", "ctx"),
        P("pipe", "ctx", None),
    )
    return jax.shard_map(
        local,
        mesh=mesh,
        in_specs=placed,
        out_specs=(P("pipe", "ctx", "tp"), P("pipe", "ctx", "tp")),
        check_vma=False,
    )
```
